32 devices in a mesh: clip: 2 (over y), height: 4 (over z), head: 4 (over x, core).
Axes of the slice: x: 2, y: 2, z: 4, core: 2. Of those that a mesh axis runs over, the one named last changes fastest.
Arguments:
- tokens: bfloat16 [8, 192, 5120], P(('clip', 'height'), None, 'head'), parts along dimension 0, may hold values from -6 to 6
- in_sign: int32 [5120], replicated, may hold values from 0 to 1
- qkv_codes: int32 [640, 3, 3072], P(None, None, 'head'), may hold values from 0 to 65535
- qkv_scale: float32 [3, 3072], P(None, 'head'), may hold values from 0.3 to 3
- qkv_sign: int32 [3, 3072], P(None, 'head'), may hold values from 0 to 1
- windows: int32 [8, 3, 27], P(('clip', 'height')), parts along dimension 0, may hold values from 0 to 11, as said below
- oin_sign: int32 [3072], P('head'), may hold values from 0 to 1
- out_codes: int32 [384, 5120], P('head'), may hold values from 0 to 65535
- out_scale: float32 [5120], replicated, may hold values from 2 to 20
- out_sign: int32 [5120], replicated, may hold values from 0 to 1
Outputs:
- attention_out: bfloat16 [8, 192, 5120], P(('clip', 'height'), 'head'), parts along dimension 0
The draws below stay inside these ranges and needn't reach their ends.
There are 2 independent parts, one for each index of `clip`. The reference program is written for one: setup_inputs(seed, part) draws one part's arguments, and reference() takes and returns one part's arrays. A program takes and returns all parts, laid end to end along the dimension named above; an argument that names none is the same for every part. Nothing has to cross between parts.
Inputs may be any that keep to these rules, and one draw needn't show every extreme that they name: `windows`: each row lists the query tile itself and 26 further entries, each one of the 27 tiles of the 3 x 3 x 3 block of tiles centred on the query tile (each of the three coordinates clipped into the grid of 1 x 4 x 3 tiles); entries may repeat and appear in any order.
All inputs are finite; a program needn't handle non-finite values.
Results may differ from the reference program's by a relative error of at most 0.015.
Values may be sent and summed in bfloat16 or wider, within the bound.
No kernel may reach another device: no remote copies, remote signals or barrier semaphores. Data moves between devices by JAX's collectives and lax.ppermute only.
A program may use at most 128 MiB of HBM per device.

```python
import math
import jax
import jax.numpy as jnp
import numpy as np
from jax import lax

D = 5120
HD = 128
HEADS = 24
HAD = 128
HROWS = 4
WTILES = 3
TTILES = 1
SLABS = 4
TILE = 64
QTILES = 3
TOK_DEV = 192
TOKENS = 768
N_HEAD = 4


def draw_windows(key, part):
    slab_index = jnp.arange(SLABS, dtype=jnp.int32)[:, None, None, None, None]
    col_index = jnp.arange(WTILES, dtype=jnp.int32)[None, :, None, None, None]
    stepping = jnp.arange(3, dtype=jnp.int32) - 1
    time_all = jnp.clip(slab_index // HROWS + stepping[None, None, :, None, None], 0, TTILES - 1)
    row_all = jnp.clip(slab_index % HROWS + stepping[None, None, None, :, None], 0, HROWS - 1)
    col_all = jnp.clip(col_index + stepping[None, None, None, None, :], 0, WTILES - 1)
    tile_ids = ((time_all * HROWS + row_all) * WTILES + col_all).reshape(SLABS * WTILES, 27)
    pick_key = jax.random.fold_in(key, 11)
    order_key = jax.random.fold_in(key, 23)
    picks = jax.random.randint(pick_key, (SLABS * WTILES, 27), 0, 27).astype(jnp.int32)
    picks = picks.at[:, 0].set(13)
    chosen = jnp.take_along_axis(tile_ids, picks, axis=1)
    row_keys = jax.random.split(order_key, SLABS * WTILES)
    orders = jax.vmap(lambda one_key: jax.random.permutation(one_key, 27))(row_keys)
    shuffled = jnp.take_along_axis(chosen, orders.astype(jnp.int32), axis=1)
    return shuffled.reshape(SLABS, WTILES, 27).astype(jnp.int32)


def with_ends(entries, own_key, low, high):
    spot = [jax.random.randint(jax.random.fold_in(own_key, axis), (), 0, length) for axis, length in enumerate(entries.shape)]
    widest = entries.shape.index(max(entries.shape))
    next_to = spot[:widest] + [(spot[widest] + 1) % entries.shape[widest]] + spot[widest + 1:]
    return entries.at[tuple(spot)].set(low).at[tuple(next_to)].set(high)


def block_scale(stream_key, shape, shards, smallest, top_value):
    def one(position, blocks):
        heights = jax.random.uniform(jax.random.fold_in(jax.random.fold_in(stream_key, 6), position), (blocks,), jnp.float32, smallest / len(shards), top_value / len(shards))
        return jnp.repeat(jnp.exp(heights), shape[position] // blocks).reshape((-1,) + (1,) * (len(shape) - position - 1))

    level = one(*shards[0])
    for cut in shards[1:]:
        level = level * one(*cut)
    return level


def centred(stream_key, shape, deviation, limit, cuts=(), held_as=jnp.bfloat16):
    values = jax.random.normal(stream_key, shape, jnp.float32) * deviation
    if len(cuts) > 0:
        values = block_scale(stream_key, shape, cuts, -0.22, 0.18) * values
    return jnp.clip(values, min=-limit, max=limit).astype(held_as)


def setup_inputs(seed: int = 0, part: int = 0) -> dict:
    splits = jax.random.split(jax.random.key(seed), 11)
    own_keys = jax.random.split(jax.random.fold_in(splits[10], part), 11)
    return {
        "tokens": centred(own_keys[0], (SLABS, TOK_DEV, D), 1.0, 6.0, ((0, 4), (2, 4))),
        "in_sign": with_ends(jax.random.randint(splits[1], (D,), 0, 2), jax.random.fold_in(splits[1], 1), 0, 1).astype(jnp.int32),
        "qkv_codes": with_ends(jax.random.randint(splits[2], (D // 8, 3, HEADS * HD), 0, 65536), jax.random.fold_in(splits[2], 1), 0, 65535).astype(jnp.int32),
        "qkv_scale": jnp.clip(jnp.exp(math.log(3.0) - 2.3025851 * jax.random.uniform(splits[3], (3, HEADS * HD), jnp.float32) ** block_scale(splits[3], (3, HEADS * HD), ((1, 4),), -0.2, 0.2)), 0.3, 3.0),
        "qkv_sign": with_ends(jax.random.randint(splits[4], (3, HEADS * HD), 0, 2), jax.random.fold_in(splits[4], 1), 0, 1).astype(jnp.int32),
        "windows": draw_windows(jax.random.fold_in(jax.random.fold_in(splits[10], part), 71), part),
        "oin_sign": with_ends(jax.random.randint(splits[6], (HEADS * HD,), 0, 2), jax.random.fold_in(splits[6], 1), 0, 1).astype(jnp.int32),
        "out_codes": with_ends(jax.random.randint(splits[7], (HEADS * HD // 8, D), 0, 65536), jax.random.fold_in(splits[7], 1), 0, 65535).astype(jnp.int32),
        "out_scale": jnp.clip(jnp.exp(jax.random.uniform(splits[8], (D,), jnp.float32, math.log(2.0), math.log(20.0))), 2.0, 20.0),
        "out_sign": with_ends(jax.random.randint(splits[9], (D,), 0, 2), jax.random.fold_in(splits[9], 1), 0, 1).astype(jnp.int32),
    }


epsilon = 1e-06

def sylvester(order_size):
    matrix_now = np.ones((1, 1), np.float32)
    seed_pair = np.array([[1.0, 1.0], [1.0, -1.0]], np.float32)
    while matrix_now.shape[0] < order_size:
        matrix_now = np.kron(matrix_now, seed_pair)
    return matrix_now

def signed(sign_bits):
    return (2 * sign_bits - 1).astype(jnp.float32)

def unpack(packed):
    powers = np.array([4 ** k for k in range(8)], np.int32)
    powers = jnp.asarray(powers.reshape((1, 8) + (1,) * (packed.ndim - 1)), jnp.int32)
    digits = packed[:, None] // powers % 4
    return digits.reshape((packed.shape[0] * 8,) + packed.shape[1:])

def levels(packed, column_scale, fan_in):
    return ((unpack(packed).astype(jnp.float32) - 1.5) * (column_scale * fan_in ** (-0.5))).astype(jnp.bfloat16)

def rotate_exact(matrix_in):
    row_count, columns = matrix_in.shape
    hadamard = jnp.asarray(sylvester(HAD), jnp.float32)
    grouped = matrix_in.astype(jnp.float32).reshape(row_count, columns // HAD, HAD)
    turned = jnp.einsum('rbi,ij->rbj', grouped, hadamard, precision=lax.Precision.HIGHEST)
    return turned.reshape(row_count, columns) * HAD ** (-0.5)

def normalize(vectors):
    return vectors / jnp.sqrt(lax.optimization_barrier(jnp.mean(vectors * vectors, axis=-1, keepdims=True)) + epsilon)

def reference(tokens, in_sign, qkv_codes, qkv_scale, qkv_sign, windows, oin_sign, out_codes, out_scale, out_sign):
    flat_tokens = tokens.reshape(TOKENS, D)
    turned = rotate_exact(flat_tokens.astype(jnp.float32) * signed(in_sign)).astype(jnp.bfloat16)
    qkv_weight = levels(qkv_codes, qkv_scale, D).reshape(D, 3 * HEADS * HD)
    projected = jnp.dot(turned, qkv_weight, preferred_element_type=jnp.float32)
    mixed = rotate_exact(projected) * signed(qkv_sign).reshape(-1)
    mixed = mixed.reshape(TOKENS, 3, HEADS, HD)
    queries = normalize(mixed[:, 0]).astype(jnp.bfloat16).reshape(SLABS, TOK_DEV, HEADS, HD)
    key_rows = normalize(mixed[:, 1]).astype(jnp.bfloat16).reshape(SLABS, TOK_DEV, HEADS, HD)
    value_rows = mixed[:, 2].astype(jnp.bfloat16).reshape(SLABS, TOK_DEV, HEADS, HD)
    padding = jnp.zeros((5, TOK_DEV, HEADS, HD), jnp.bfloat16)
    keys_padded = jnp.concatenate([padding, key_rows, padding], 0)
    values_padded = jnp.concatenate([padding, value_rows, padding], 0)
    local_tiles = jnp.arange(11 * QTILES, dtype=jnp.int32)

    def attend(tile_row):
        near_keys = lax.dynamic_slice_in_dim(keys_padded, tile_row, 11, 0).reshape(11 * TOK_DEV, HEADS, HD)
        near_values = lax.dynamic_slice_in_dim(values_padded, tile_row, 11, 0).reshape(11 * TOK_DEV, HEADS, HD)
        key_ids = (tile_row - 5) * QTILES + local_tiles
        listed = lax.dynamic_index_in_dim(windows, tile_row, 0, keepdims=False)
        allowed = jnp.any(listed[:, :, None] == key_ids[None, None, :], axis=1)
        allowed = jnp.broadcast_to(allowed[:, None, :, None], (QTILES, TILE, 11 * QTILES, TILE))
        allowed = allowed.reshape(TOK_DEV, 11 * TOK_DEV)
        own_queries = lax.dynamic_index_in_dim(queries, tile_row, 0, keepdims=False)
        score = jnp.einsum('qhd,khd->hqk', own_queries.astype(jnp.float32), near_keys.astype(jnp.float32)) * HD ** (-0.5)
        weight = jnp.where(allowed[None], jnp.exp(score), 0.0)
        totals = lax.optimization_barrier(jnp.sum(weight, axis=-1))
        rounded = lax.optimization_barrier(weight.astype(jnp.bfloat16)).astype(jnp.float32)
        gathered_sum = jnp.einsum('hqk,khd->qhd', rounded, near_values.astype(jnp.float32))
        return (gathered_sum / totals.T[:, :, None]).astype(jnp.bfloat16)
    attended = lax.map(attend, jnp.arange(SLABS, dtype=jnp.int32))
    attended = attended.reshape(TOKENS, HEADS * HD)
    rotated_heads = rotate_exact(attended.astype(jnp.float32) * signed(oin_sign)).astype(jnp.bfloat16)
    out_weight = levels(out_codes, out_scale, HEADS * HD)
    group_cols = HEADS * HD // N_HEAD
    summed = jnp.zeros((TOKENS, D), jnp.float32)
    for group in range(N_HEAD):
        group_term = jnp.dot(rotated_heads[:, group * group_cols:(group + 1) * group_cols], out_weight[group * group_cols:(group + 1) * group_cols], preferred_element_type=jnp.float32)
        summed = summed + lax.optimization_barrier(group_term.astype(jnp.bfloat16)).astype(jnp.float32)
    result_rows = (rotate_exact(summed) * signed(out_sign)).astype(jnp.bfloat16)
    return result_rows.reshape(SLABS, TOK_DEV, D)
```

```python
import functools

import jax
import jax.numpy as jnp
import numpy as np
from jax import lax
from jax.experimental import pallas as pl
from jax.experimental.pallas import tpu as pltpu
from jax.sharding import PartitionSpec as P

D = 5120
HD = 128
HEADS = 24
HAD = 128
TILE = 64
HROWS = 4
PLANES = 8
WORDS = HAD // PLANES
OUT_BLOCK = 1024

epsilon = 1e-06
f32 = jnp.float32
bf16 = jnp.bfloat16


def sylvester(order_size):
    matrix_now = np.ones((1, 1), np.float32)
    seed_pair = np.array([[1.0, 1.0], [1.0, -1.0]], np.float32)
    while matrix_now.shape[0] < order_size:
        matrix_now = np.kron(matrix_now, seed_pair)
    return matrix_now


PLANE_ORDER = np.array([PLANES * i + k for k in range(PLANES) for i in range(WORDS)])
PLANE_POWER = np.repeat(4.0 ** np.arange(PLANES), WORDS).astype(np.float32)


def plane_hadamard():
    return jnp.asarray(sylvester(HAD)[:, PLANE_ORDER], bf16)


def plane_rows():
    rows = np.zeros((8, HAD), np.float32)
    rows[0] = np.float32(HAD ** (-0.5)) / PLANE_POWER
    rows[1] = 1.5 * PLANE_POWER
    return jnp.asarray(rows)


def spec_of(array):
    return pl.BlockSpec(array.shape, lambda *_: (0,) * array.ndim)


def params(megabytes=40):
    return pltpu.CompilerParams(vmem_limit_bytes=megabytes * 2**20)


def cost(flops, moved):
    return pl.CostEstimate(flops=int(flops), bytes_accessed=int(moved), transcendentals=0)


def tile_width(columns):
    for width in (256, 128):
        if columns % width == 0:
            return width


def decode(words):
    blocks = []
    for first in range(0, words.shape[0], WORDS):
        part = words[first : first + WORDS]
        for k in range(PLANES):
            blocks.append((part & (3 << (2 * k))).astype(f32).astype(bf16))
    return jnp.concatenate(blocks, 0)


def row_correction(rows, factor_row):
    total = None
    for first in range(0, rows.shape[1], HAD):
        term = rows[:, first : first + HAD].astype(f32) * factor_row
        total = term if total is None else total + term
    return jnp.sum(total, axis=1, keepdims=True)


def rotate_halves(values, hadamard):
    high = values.astype(bf16)
    low = (values - high.astype(f32)).astype(bf16)
    both = jnp.concatenate([high, low], 1)
    return jnp.dot(both, hadamard, preferred_element_type=f32)


def double_hadamard():
    plain = sylvester(HAD)
    return jnp.asarray(np.concatenate([plain, plain], 0), bf16)


def signed(sign_bits):
    return (2 * sign_bits - 1).astype(f32)


def turn_kernel(place_ref, x_ref, sign_ref, hadamard_ref, rows_ref, out_ref):
    blocks = x_ref.shape[1] // HAD
    first = place_ref[0] * blocks
    for b in range(blocks):
        cols = slice(b * HAD, (b + 1) * HAD)
        sign_row = signed(sign_ref[pl.ds(first + b, 1), :])
        flipped = (x_ref[:, cols].astype(f32) * sign_row).astype(bf16)
        turned = jnp.dot(flipped, hadamard_ref[...], preferred_element_type=f32)
        out_ref[:, cols] = (turned * rows_ref[0:1, :]).astype(bf16)


def turn(place, own_tokens, in_sign):
    args = (own_tokens, in_sign.reshape(-1, HAD), plane_hadamard(), plane_rows())
    return pl.pallas_call(
        turn_kernel,
        out_shape=jax.ShapeDtypeStruct(own_tokens.shape, bf16),
        grid_spec=pltpu.PrefetchScalarGridSpec(
            num_scalar_prefetch=1,
            grid=(1,),
            in_specs=[spec_of(a) for a in args],
            out_specs=spec_of(own_tokens),
        ),
        compiler_params=params(),
        cost_estimate=cost(2 * own_tokens.size * HAD, 4 * own_tokens.size),
        name="turn",
    )(place, *args)


def project_kernel(has_sum, last, place_ref, x_ref, rows_ref, codes_ref, *rest):
    rest = list(rest)
    sum_ref = rest.pop(0) if has_sum else None
    if last:
        scale_ref, sign_ref, hadamard_ref, q_ref, kv_ref = rest
    else:
        (out_ref,) = rest
    step = pl.program_id(0)
    rows = x_ref[...]
    fix = row_correction(rows, rows_ref[1:2, :])
    columns = codes_ref.shape[2]
    width = tile_width(columns)
    for first in range(0, columns, width):
        cols = slice(first, first + width)
        weights = decode(codes_ref[0, :, cols])
        part = jnp.dot(rows, weights, preferred_element_type=f32) - fix
        if has_sum:
            part = part + sum_ref[:, cols]
        if not last:
            out_ref[:, cols] = part
            continue
        for head in range(first, first + width, HD):
            at = slice(head, head + HD)
            scale_row = scale_ref[0, 0:1, at] * np.float32(D ** (-0.5))
            projected = part[:, head - first : head - first + HD] * scale_row
            sign_row = signed(sign_ref[0, 0:1, at]) * np.float32(HAD ** (-0.5))
            mixed = rotate_halves(projected, hadamard_ref[...]) * sign_row
            mean = jnp.mean(mixed * mixed, axis=1, keepdims=True)
            factor = jnp.where(step == 1, 1.0, lax.rsqrt(mean + epsilon))
            done = (mixed * factor).astype(bf16)

            @pl.when(step < 2)
            def _():
                kv_ref[0, :, at] = done

            @pl.when(step == 2)
            def _():
                q_ref[:, at] = done


def kind(step):
    return lax.rem(step + 1, 3)


def project(place, flip, shard, codes, running, ending):
    row_count, inner = shard.shape
    columns = codes.shape[2]
    words = inner // PLANES
    sums = jax.ShapeDtypeStruct((row_count, 3 * columns), f32)
    sum_spec = pl.BlockSpec((row_count, columns), lambda i, p: (0, i))
    rows = plane_rows()
    args = [shard, rows, codes]
    in_specs = [
        spec_of(shard),
        spec_of(rows),
        pl.BlockSpec((1, words, columns), lambda i, p: (kind(i), p[0] ^ flip, 0)),
    ]
    if running is not None:
        args.append(running)
        in_specs.append(sum_spec)
    if ending is None:
        out_shape, out_specs = sums, sum_spec
    else:
        scale, sign = ending
        hadamard = double_hadamard()
        args += [scale, sign, hadamard]
        per_kind = pl.BlockSpec((1, 1, columns), lambda i, p: (kind(i), 0, 0))
        in_specs += [per_kind, per_kind, spec_of(hadamard)]
        out_shape = (
            jax.ShapeDtypeStruct((row_count, columns), bf16),
            jax.ShapeDtypeStruct((2, row_count, columns), bf16),
        )
        out_specs = (
            pl.BlockSpec((row_count, columns), lambda i, p: (0, 0)),
            pl.BlockSpec((1, row_count, columns), lambda i, p: (jnp.minimum(i, 1), 0, 0)),
        )
    return pl.pallas_call(
        functools.partial(project_kernel, running is not None, ending is not None),
        out_shape=out_shape,
        grid_spec=pltpu.PrefetchScalarGridSpec(
            num_scalar_prefetch=1, grid=(3,), in_specs=in_specs, out_specs=out_specs
        ),
        compiler_params=params(),
        cost_estimate=cost(2 * 4 * row_count * inner * 3 * columns, 12 * words * columns),
        name="project",
    )(place, *args)


def attend_kernel(near, share_order, place_ref, q_ref, allowed_ref, *rest):
    kv_refs = rest[:near]
    sign_ref, hadamard_ref, rows_ref, out_ref, rotated_ref = rest[near:]
    row_count, columns = q_ref.shape
    for head in range(columns // HD):
        at = slice(head * HD, (head + 1) * HD)
        keys = jnp.concatenate([ref[0, :, at] for ref in kv_refs], 0)
        values = jnp.concatenate([ref[1, :, at] for ref in kv_refs], 0)
        sign_row = signed(sign_ref[head : head + 1, :])
        score = lax.dot_general(
            q_ref[:, at], keys, (((1,), (1,)), ((), ())), preferred_element_type=f32
        )
        weight = jnp.exp(score * np.float32(HD ** (-0.5)))
        weight = jnp.concatenate(
            [
                weight[t * TILE : (t + 1) * TILE] * allowed_ref[t : t + 1, :]
                for t in range(row_count // TILE)
            ],
            0,
        )
        totals = jnp.sum(weight, axis=1, keepdims=True)
        gathered = jnp.dot(weight.astype(bf16), values, preferred_element_type=f32)
        attended = (gathered / totals).astype(bf16)
        flipped = (attended.astype(f32) * sign_row).astype(bf16)
        rotated = jnp.dot(flipped, hadamard_ref[...], preferred_element_type=f32)
        rotated_ref[:, at] = rotated * rows_ref[0:1, :]
    share = row_count // len(share_order)
    pieces = []
    for flip in share_order:
        owner = place_ref[0] ^ flip
        pieces.append(rotated_ref[pl.ds(pl.multiple_of(owner * share, 8), share), :])
    out_ref[...] = jnp.concatenate(pieces, 0).astype(bf16)


def attend(place, queries, blocks, allowed, oin_sign, share_order):
    args = [queries, allowed, *blocks, oin_sign.reshape(-1, HAD), plane_hadamard(), plane_rows()]
    row_count, columns = queries.shape
    return pl.pallas_call(
        functools.partial(attend_kernel, len(blocks), share_order),
        out_shape=jax.ShapeDtypeStruct(queries.shape, bf16),
        grid_spec=pltpu.PrefetchScalarGridSpec(
            num_scalar_prefetch=1,
            grid=(1,),
            in_specs=[spec_of(a) for a in args],
            out_specs=spec_of(queries),
            scratch_shapes=[pltpu.VMEM(queries.shape, f32)],
        ),
        compiler_params=params(),
        cost_estimate=cost(
            8 * row_count * columns * row_count * len(blocks), 4 * queries.size * len(blocks)
        ),
        name="attend",
    )(place, *args)


def out_kernel(first, rotated_ref, rows_ref, codes_ref, scale_ref, send_ref, keep_ref):
    step = pl.program_id(0) + first
    rows = rotated_ref[...]
    fix = row_correction(rows, rows_ref[1:2, :])
    half = send_ref.shape[0]
    columns = codes_ref.shape[1]
    width = 256
    for at in range(0, columns, width):
        cols = slice(at, at + width)
        part = jnp.dot(rows, decode(codes_ref[:, cols]), preferred_element_type=f32) - fix
        for lane in range(0, width, HAD):
            place = step * (columns // HAD) + (at + lane) // HAD
            scale_row = scale_ref[pl.ds(place, 1), :] * np.float32((HEADS * HD) ** (-0.5))
            done = (part[:, lane : lane + HAD] * scale_row).astype(bf16)
            send_ref[:, at + lane : at + lane + HAD] = done[:half]
            keep_ref[:, at + lane : at + lane + HAD] = done[half:]


def out_project(rotated, codes, scale, first, count):
    row_count, inner = rotated.shape
    half = row_count // 2
    rows = plane_rows()
    scale_rows = scale.reshape(-1, HAD)
    result = jax.ShapeDtypeStruct((half, count * OUT_BLOCK), bf16)
    result_spec = pl.BlockSpec((half, OUT_BLOCK), lambda i: (0, i))
    return pl.pallas_call(
        functools.partial(out_kernel, first),
        out_shape=(result, result),
        grid=(count,),
        in_specs=[
            spec_of(rotated),
            spec_of(rows),
            pl.BlockSpec((codes.shape[0], OUT_BLOCK), lambda i: (0, i + first)),
            spec_of(scale_rows),
        ],
        out_specs=(result_spec, result_spec),
        compiler_params=params(),
        cost_estimate=cost(
            8 * row_count * inner * count * OUT_BLOCK, 4 * codes.shape[0] * count * OUT_BLOCK
        ),
        name="out_project",
    )(rotated, rows, codes, scale_rows)


def finish_kernel(chunks, sign_ref, hadamard_ref, *rest):
    out_ref = rest[-1]
    column = 0
    for chunk in range(chunks):
        keep_ref, more_ref = rest[2 * chunk : 2 * chunk + 2]
        for at in range(0, keep_ref.shape[1], HAD):
            cols = slice(at, at + HAD)
            total = keep_ref[:, cols].astype(f32) + more_ref[:, cols].astype(f32)
            sign_row = signed(sign_ref[column : column + 1, :]) * np.float32(HAD ** (-0.5))
            done = rotate_halves(total, hadamard_ref[...]) * sign_row
            out_ref[:, column * HAD : (column + 1) * HAD] = done.astype(bf16)
            column += 1


def finish(pairs, out_sign):
    args = [out_sign.reshape(-1, HAD), double_hadamard()]
    for pair in pairs:
        args += pair
    return pl.pallas_call(
        functools.partial(finish_kernel, len(pairs)),
        out_shape=jax.ShapeDtypeStruct((pairs[0][0].shape[0], D), bf16),
        grid=(1,),
        in_specs=[spec_of(a) for a in args],
        out_specs=pl.BlockSpec((pairs[0][0].shape[0], D), lambda i: (0, 0)),
        compiler_params=params(),
        name="finish",
    )(*args)


def swap(shard, bit):
    peers = lax.axis_size("head")
    return lax.ppermute(shard, "head", [(i, i ^ bit) for i in range(peers)])


def from_behind(shard, axis, by):
    peers = lax.axis_size(axis)
    pairs = [(i, i + by) for i in range(peers) if 0 <= i + by < peers]
    return lax.ppermute(shard, axis, pairs)


def halving_order(head_count):
    flips = [0]
    bit = head_count // 2
    while bit >= 1:
        flips = [f | bit for f in flips] + flips
        bit //= 2
    return tuple(flips)


CHUNKS = (2, 3)


def on_device(
    tokens,
    in_sign,
    qkv_codes,
    qkv_scale,
    qkv_sign,
    windows,
    oin_sign,
    out_codes,
    out_scale,
    out_sign,
):
    head_count = lax.axis_size("head")
    row_tiles = lax.axis_size("height")
    row_place = lax.axis_index("height")
    place = jnp.reshape(lax.axis_index("head"), (1,)).astype(jnp.int32)
    own = turn(place, tokens[0], in_sign)
    bits = [1 << b for b in range(head_count.bit_length() - 1)]

    shards = {0: own}
    for bit in reversed(bits):
        for flip in list(shards):
            shards[flip ^ bit] = swap(shards[flip], bit)
    codes = jnp.transpose(qkv_codes, (1, 0, 2))
    arrival = sorted(shards)
    running = None
    for flip in arrival[:-1]:
        running = project(place, flip, shards[flip], codes, running, None)
    flip = arrival[-1]
    ending = (qkv_scale[:, None, :], qkv_sign[:, None, :])
    queries, key_value = project(place, flip, shards[flip], codes, running, ending)

    distances = (5, 4, 3, 1, -1, -3, -4, -5) if row_tiles > HROWS else (1, -1)
    blocks = [key_value] + [from_behind(key_value, "height", offset) for offset in distances]
    listed = windows[0]
    qtile_count = listed.shape[0]
    tile_steps = jnp.arange(qtile_count, dtype=jnp.int32)
    all_ids = jnp.concatenate(
        [(row_place - offset) * qtile_count + tile_steps for offset in (0,) + distances]
    )
    allowed = jnp.any(listed[:, :, None] == all_ids[None, None, :], axis=1)
    allowed = jnp.repeat(allowed.astype(f32), TILE, axis=1)
    rotated = attend(place, queries, blocks, allowed, oin_sign, halving_order(head_count))

    pairs = []
    first = 0
    for count in CHUNKS:
        send, keep = out_project(rotated, out_codes, out_scale, first, count)
        for bit in bits:
            more = swap(send, bit)
            if bit == bits[-1]:
                pairs.append((keep, more))
                break
            total = keep.astype(f32) + more.astype(f32)
            half = total.shape[0] // 2
            send, keep = total[:half].astype(bf16), total[half:]
        first += count
    return finish(pairs, out_sign)[None]


def solution(mesh):
    return jax.shard_map(
        on_device,
        mesh=mesh,
        in_specs=(
            P(("clip", "height"), None, "head"),
            P(),
            P(None, None, "head"),
            P(None, "head"),
            P(None, "head"),
            P(("clip", "height"), None, None),
            P("head"),
            P("head", None),
            P(),
            P(),
        ),
        out_specs=P(("clip", "height"), "head", None),
        check_vma=False,
    )
```

```python
import functools

import jax
import jax.numpy as jnp
import numpy as np
from jax import lax
from jax.experimental import pallas as pl
from jax.experimental.pallas import tpu as pltpu
from jax.sharding import PartitionSpec as P

D = 5120
HD = 128
HEADS = 24
HAD = 128
TILE = 64
HROWS = 4
WTILES = 3
PLANES = 8
WORDS = HAD // PLANES
EARLY = 2 * TILE

epsilon = 1e-06
f32 = jnp.float32
bf16 = jnp.bfloat16
VMEM = pl.BlockSpec(memory_space=pltpu.VMEM)
SMEM = pl.BlockSpec(memory_space=pltpu.SMEM)
ANY = pl.BlockSpec(memory_space=pl.ANY)


def shape_of(shape, dtype):
    return jax.ShapeDtypeStruct(tuple(shape), dtype)


def call(body, out_shape, in_specs, args, name, flops=0, out_specs=None, megabytes=16, **more):
    if out_specs is None:
        out_specs = jax.tree.map(lambda _: VMEM, out_shape)
    moved = sum(a.size * a.dtype.itemsize for a in args)
    return pl.pallas_call(
        body,
        out_shape=out_shape,
        in_specs=in_specs,
        out_specs=out_specs,
        compiler_params=pltpu.CompilerParams(vmem_limit_bytes=megabytes * 2**20),
        cost_estimate=pl.CostEstimate(
            flops=int(flops), bytes_accessed=int(moved), transcendentals=0
        ),
        name=name,
        **more,
    )(*args)


def lanes(shape=(HAD, HAD)):
    return lax.broadcasted_iota(jnp.int32, shape, len(shape) - 1)


def hadamard(plane_order):
    row = lax.broadcasted_iota(jnp.int32, (HAD, HAD), 0)
    column = lanes()
    if plane_order:
        column = PLANES * (column & (WORDS - 1)) + column // WORDS
    shared = row & column
    shared = shared ^ (shared >> 4)
    shared = shared ^ (shared >> 2)
    shared = shared ^ (shared >> 1)
    return (1 - 2 * (shared & 1)).astype(f32).astype(bf16)


def double_hadamard():
    plain = hadamard(False)
    return jnp.concatenate([plain, plain], 0)


def plane_power(base):
    plane = lanes((1, HAD)) // WORDS
    power = jnp.where(plane & 1 == 1, base, 1.0)
    power = power * jnp.where(plane & 2 == 2, base**2, 1.0)
    return power * jnp.where(plane & 4 == 4, base**4, 1.0)


def turn_factor():
    return plane_power(0.25) * np.float32(HAD ** (-0.5))


def signed(sign_bits):
    return (2 * sign_bits - 1).astype(f32)


def plane_piece(words, k):
    return (words & (3 << (2 * k))).astype(f32).astype(bf16)


def decode(words):
    blocks = []
    for first in range(0, words.shape[0], WORDS):
        part = words[first : first + WORDS]
        blocks += [plane_piece(part, k) for k in range(PLANES)]
    return jnp.concatenate(blocks, 0)


def row_correction(row_list):
    factor_row = plane_power(4.0) * 1.5
    total = None
    for rows in row_list:
        for first in range(0, rows.shape[1], HAD):
            term = rows[:, first : first + HAD].astype(f32)
            total = term if total is None else total + term
    return jnp.sum(total * factor_row, axis=1, keepdims=True)


def rotate_halves(values, doubled):
    high = values.astype(bf16)
    low = (values - high.astype(f32)).astype(bf16)
    return jnp.dot(jnp.concatenate([high, low], 1), doubled, preferred_element_type=f32)


def tile_width(columns):
    for width in (256, 128):
        if columns % width == 0:
            return width


def turn_kernel(place_ref, x_hbm, sign_hbm, own_ref, send_ref, x_ref, sign_ref, sems):
    copies = [
        pltpu.make_async_copy(x_hbm, x_ref, sems.at[0]),
        pltpu.make_async_copy(sign_hbm, sign_ref, sems.at[1]),
    ]
    for copy in copies:
        copy.start()
    matrix = hadamard(True)
    factor = turn_factor()
    for copy in copies:
        copy.wait()
    blocks = x_ref.shape[1] // HAD
    first = place_ref[0] * blocks
    end = place_ref[1]
    tiles = (end, 1, 2 - end)
    for b in range(blocks):
        cols = slice(b * HAD, (b + 1) * HAD)
        sign_row = signed(sign_ref[pl.ds(first + b, 1), :])
        own = [x_ref[pl.ds(pl.multiple_of(t * TILE, TILE), TILE), cols] for t in tiles]
        flipped = (jnp.concatenate(own, 0).astype(f32) * sign_row).astype(bf16)
        turned = jnp.dot(flipped, matrix, preferred_element_type=f32)
        turned = (turned * factor).astype(bf16)
        own_ref[:, cols] = turned
        send_ref[:TILE, cols] = turned[2 * TILE :]
        send_ref[TILE:, cols] = turned[TILE : 2 * TILE]


def turn(place, own_tokens, in_sign):
    sign_rows = in_sign.reshape(-1, HAD)
    rows, inner = own_tokens.shape
    return call(
        turn_kernel,
        (shape_of((rows, inner), bf16), shape_of((EARLY, inner), bf16)),
        [SMEM, ANY, ANY],
        (place, own_tokens, sign_rows),
        "turn",
        flops=2 * own_tokens.size * HAD,
        scratch_shapes=[
            pltpu.VMEM(own_tokens.shape, bf16),
            pltpu.VMEM(sign_rows.shape, jnp.int32),
            pltpu.SemaphoreType.DMA((2,)),
        ],
    )


def prepare_kernel(near, far, place_ref, *rest):
    shard_refs = rest[: len(near)]
    codes_hbm, sums_ref, weights_ref, late_ref, words_ref, sems = rest[len(near) :]
    words, columns = words_ref.shape[1:]
    flips = list(near) + list(far)

    def fetch(piece, kind, flip):
        first = pl.multiple_of((place_ref[0] ^ flip) * words, WORDS)
        return pltpu.make_async_copy(
            codes_hbm.at[kind, pl.ds(first, words), :], words_ref.at[piece], sems.at[piece]
        )

    def piece_of(position, kind):
        return position * 3 + kind

    for position, flip in enumerate(flips):
        for kind in range(3):
            fetch(piece_of(position, kind), kind, flip).start()
    fix = row_correction([ref[...] for ref in shard_refs])
    width = tile_width(columns)
    late_ref[...] = shard_refs[0][:TILE, :]

    def product(kind, carry):
        for position, flip in enumerate(near):
            fetch(piece_of(position, kind), kind, flip).wait()
        for first in range(0, columns, width):
            cols = slice(first, first + width)
            total = -fix
            for position, ref in enumerate(shard_refs):
                weights = decode(words_ref[piece_of(position, kind), :, cols])
                total = total + jnp.dot(ref[...], weights, preferred_element_type=f32)
            sums_ref[kind, :, cols] = total
        return carry

    lax.fori_loop(0, 3, product, 0)
    for position, flip in enumerate(far):

        def unpack(kind, carry):
            piece = piece_of(position + len(near), kind)
            fetch(piece, kind, flip).wait()
            for first in range(0, words, WORDS):
                part = words_ref[piece, first : first + WORDS, :]
                for k in range(PLANES):
                    at = first * PLANES + k * WORDS
                    weights_ref[position, kind, at : at + WORDS, :] = plane_piece(part, k)
            return carry

        lax.fori_loop(0, 3, unpack, 0)


def prepare(place, near, far, shards, codes):
    rows, inner = shards[0].shape
    columns = codes.shape[2]
    pieces = 3 * (len(near) + len(far))
    return call(
        functools.partial(prepare_kernel, near, far),
        (
            shape_of((3, rows, columns), f32),
            shape_of((len(far), 3, inner, columns), bf16),
            shape_of((TILE, inner), bf16),
        ),
        [SMEM] + [VMEM] * len(near) + [ANY],
        (place, *shards, codes),
        "prepare",
        flops=16 * rows * inner * 3 * columns,
        scratch_shapes=[
            pltpu.VMEM((pieces, inner // PLANES, columns), jnp.int32),
            pltpu.SemaphoreType.DMA((pieces,)),
        ],
    )


def project_kernel(kinds, first_row, groups, far, *rest):
    shard_refs = rest[: groups * far]
    sums_ref, weights_ref, scale_ref, sign_ref, out_ref = rest[groups * far :]
    columns = sums_ref.shape[2]
    width = tile_width(columns)
    doubled = double_hadamard()
    ones = jnp.ones((HD, HD), bf16)
    shards = []
    for position in range(far):
        parts = [shard_refs[g * far + position][...] for g in range(groups)]
        shards.append(parts[0] if groups == 1 else jnp.concatenate(parts, 0))
    fix = row_correction(shards)
    row_count = shards[0].shape[0]
    rows = slice(first_row, first_row + row_count)
    for place, kind in enumerate(kinds):
        for first in range(0, columns, width):
            cols = slice(first, first + width)
            part = sums_ref[kind, rows, cols] - fix
            for position in range(far):
                part = part + jnp.dot(
                    shards[position], weights_ref[position, kind, :, cols], preferred_element_type=f32
                )
            for lane in range(0, width, HD):
                at = slice(first + lane, first + lane + HD)
                scale_row = scale_ref[kind : kind + 1, at] * np.float32(D ** (-0.5))
                sign_row = signed(sign_ref[kind : kind + 1, at]) * np.float32(HAD ** (-0.5))
                mixed = rotate_halves(part[:, lane : lane + HD] * scale_row, doubled) * sign_row
                if kind != 2:
                    square = (mixed * mixed).astype(bf16)
                    mean = jnp.dot(square, ones, preferred_element_type=f32) * (1.0 / HD)
                    mixed = mixed * lax.rsqrt(mean + epsilon)
                out_ref[place, :, at] = mixed.astype(bf16)


def project(kinds, first_row, groups, sums, weights, scale, sign):
    far = len(groups[0])
    inner = groups[0][0].shape[1]
    columns = sums.shape[2]
    row_count = sum(group[0].shape[0] for group in groups)
    args = [shard for group in groups for shard in group] + [sums, weights, scale, sign]
    return call(
        functools.partial(project_kernel, kinds, first_row, len(groups), far),
        shape_of((len(kinds), row_count, columns), bf16),
        [VMEM] * len(args),
        args,
        "project",
        flops=2 * row_count * inner * far * len(kinds) * columns,
    )


def attend_kernel(blocks, has_sum, last, share_order, place_ref, q_ref, *rest):
    rest = list(rest)
    kv_refs = [rest.pop(0) for _ in range(blocks)]
    mask_ref = rest.pop(0)
    sum_ref = rest.pop(0) if has_sum else None
    if last:
        oin_ref, out_ref, rotated_ref = rest
    else:
        (out_ref,) = rest
    row_count, columns = q_ref.shape[1:]
    heads = [slice(head, head + HD) for head in range(0, columns, HD)]
    mask = jnp.concatenate(
        [
            jnp.broadcast_to(mask_ref[t : t + 1, :], (TILE, mask_ref.shape[1]))
            for t in range(row_count // TILE)
        ],
        0,
    )
    scores = []
    for at in heads:
        keys = jnp.concatenate([ref[0, :, at] for ref in kv_refs], 0)
        scores.append(
            lax.dot_general(
                q_ref[0, :, at], keys, (((1,), (1,)), ((), ())), preferred_element_type=f32
            )
        )
    weights = [
        (jnp.exp(score * np.float32(HD ** (-0.5))) * mask).astype(bf16) for score in scores
    ]
    totals = []
    for head, at in enumerate(heads):
        values = jnp.concatenate([ref[1, :, at] for ref in kv_refs], 0)
        values = jnp.concatenate([values, jnp.ones_like(values)], 1)
        total = jnp.dot(weights[head], values, preferred_element_type=f32)
        if has_sum:
            total = total + sum_ref[head]
        totals.append(total)
    if not last:
        for head, total in enumerate(totals):
            out_ref[head] = total
        return
    matrix = hadamard(True)
    factor = turn_factor()
    end = place_ref[1]
    for head, at in enumerate(heads):
        attended = (totals[head][:, :HD] / totals[head][:, HD:]).astype(bf16)
        sign_row = signed(oin_ref[head : head + 1, :])
        flipped = (attended.astype(f32) * sign_row).astype(bf16)
        rotated = jnp.dot(flipped, matrix, preferred_element_type=f32) * factor
        for position, tile in enumerate((end, 1, 2 - end)):
            rotated_ref[pl.ds(pl.multiple_of(tile * TILE, TILE), TILE), at] = rotated[
                position * TILE : (position + 1) * TILE
            ]
    share = row_count // len(share_order)
    pieces = []
    for flip in share_order:
        owner = place_ref[0] ^ flip
        pieces.append(rotated_ref[pl.ds(pl.multiple_of(owner * share, 8), share), :])
    out_ref[...] = jnp.concatenate(pieces, 0).astype(bf16)


def attend(place, queries, blocks, mask, running, ending):
    row_count, columns = queries.shape[1:]
    args = [place, queries, *blocks, mask]
    if running is not None:
        args.append(running)
    scratch, share_order = [], None
    if ending is None:
        out_shape = shape_of((columns // HD, row_count, 2 * HD), f32)
    else:
        oin_sign, share_order = ending
        args.append(oin_sign.reshape(-1, HAD))
        out_shape = shape_of((row_count, columns), bf16)
        scratch = [pltpu.VMEM((row_count, columns), f32)]
    return call(
        functools.partial(
            attend_kernel, len(blocks), running is not None, ending is not None, share_order
        ),
        out_shape,
        [SMEM] + [VMEM] * (len(args) - 1),
        args,
        "attend",
        flops=8 * row_count * columns * mask.shape[1],
        scratch_shapes=scratch,
    )


def unpack_out_kernel(codes_ref, after_ref, weights_ref):
    for first in range(0, codes_ref.shape[0], WORDS):

        def some(step, carry):
            cols = pl.ds(pl.multiple_of(step * 512, 512), 512)
            part = codes_ref[first : first + WORDS, cols]
            for k in range(PLANES):
                at = first * PLANES + k * WORDS
                weights_ref[at : at + WORDS, cols] = plane_piece(part, k)
            return carry

        lax.fori_loop(0, codes_ref.shape[1] // 512, some, 0)


def unpack_out(codes, after):
    words, columns = codes.shape
    return call(
        unpack_out_kernel,
        shape_of((words * PLANES, columns), bf16),
        [VMEM, ANY],
        (codes, after),
        "unpack_out",
        flops=2000 * words * columns,
    )


def out_kernel(first, rotated_ref, weights_ref, scale_ref, send_ref, keep_ref):
    rows = rotated_ref[...]
    fix = row_correction([rows])
    half, columns = send_ref.shape
    width = 256
    for at in range(0, columns, width):
        cols = slice(first + at, first + at + width)
        part = jnp.dot(rows, weights_ref[:, cols], preferred_element_type=f32) - fix
        for lane in range(0, width, HAD):
            place = (first + at + lane) // HAD
            scale_row = scale_ref[place : place + 1, :] * np.float32((HEADS * HD) ** (-0.5))
            done = (part[:, lane : lane + HAD] * scale_row).astype(bf16)
            send_ref[:, at + lane : at + lane + HAD] = done[:half]
            keep_ref[:, at + lane : at + lane + HAD] = done[half:]


def out_project(rotated, weights, scale_rows, first, columns):
    row_count, inner = rotated.shape
    result = shape_of((row_count // 2, columns), bf16)
    return call(
        functools.partial(out_kernel, first),
        (result, result),
        [VMEM] * 3,
        (rotated, weights, scale_rows),
        "out_project",
        flops=2 * row_count * inner * columns,
    )


def finish_kernel(first, has_base, sign_ref, keep_ref, more_ref, *rest):
    out_hbm, done_ref, sem = rest[1:] if has_base else rest
    columns = keep_ref.shape[1]
    doubled = double_hadamard()
    for at in range(0, columns, HAD):
        cols = slice(at, at + HAD)
        total = keep_ref[:, cols].astype(f32) + more_ref[:, cols].astype(f32)
        place = (first + at) // HAD
        sign_row = signed(sign_ref[place : place + 1, :]) * np.float32(HAD ** (-0.5))
        done_ref[:, cols] = (rotate_halves(total, doubled) * sign_row).astype(bf16)
    copy = pltpu.make_async_copy(done_ref, out_hbm.at[:, pl.ds(first, columns)], sem)
    copy.start()
    copy.wait()


def finish(base, sign_rows, keep, more, first):
    share, columns = keep.shape
    args = [sign_rows, keep, more]
    in_specs = [VMEM] * 3
    aliases = {}
    if base is not None:
        args.append(base)
        in_specs.append(ANY)
        aliases = {3: 0}
    return call(
        functools.partial(finish_kernel, first, base is not None),
        shape_of((share, D), bf16),
        in_specs,
        args,
        "finish",
        flops=4 * share * columns * HAD,
        out_specs=ANY,
        scratch_shapes=[pltpu.VMEM((share, columns), bf16), pltpu.SemaphoreType.DMA],
        input_output_aliases=aliases,
    )


def swap(shard, bit):
    peers = lax.axis_size("head")
    return lax.ppermute(shard, "head", [(i, i ^ bit) for i in range(peers)])


def row_swaps(row_tiles):
    swaps = []
    for by in (1, 3, 4, 5) if row_tiles > HROWS else (1,):
        for odd in (0, 1):
            low = [i for i in range(row_tiles - by) if (i // by) % 2 == odd]
            swaps.append((by, odd, [(i, i + by) for i in low] + [(i + by, i) for i in low]))
    return swaps


def halving_order(head_count):
    flips = [0]
    bit = head_count // 2
    while bit >= 1:
        flips = [f | bit for f in flips] + flips
        bit //= 2
    return tuple(flips)


CHUNKS = (2048, 3072)


def on_device(
    tokens,
    in_sign,
    qkv_codes,
    qkv_scale,
    qkv_sign,
    windows,
    oin_sign,
    out_codes,
    out_scale,
    out_sign,
):
    head_count = lax.axis_size("head")
    row_tiles = lax.axis_size("height")
    row_place = lax.axis_index("height")
    head_place = lax.axis_index("head").astype(jnp.int32)
    top = head_count // 2
    end = jnp.where(head_place >= top, 0, 2).astype(jnp.int32)
    place = jnp.stack([head_place, end])
    low_bits = [1 << b for b in range(top.bit_length() - 1)]

    own, early = turn(place, tokens[0], in_sign)
    early = {top: swap(early, top)}
    near = {0: own}
    for bit in low_bits:
        for flip in list(near):
            near[flip ^ bit] = swap(near[flip], bit)
    codes = jnp.transpose(qkv_codes, (1, 0, 2))
    near_flips = tuple(sorted(near))
    far_flips = tuple(flip ^ top for flip in near_flips)
    sums, weights, late = prepare(
        place, near_flips, far_flips, [near[flip] for flip in near_flips], codes
    )
    late = {top: swap(late, top)}
    for bit in low_bits:
        for flip in list(early):
            early[flip ^ bit] = swap(early[flip], bit)
    early = [early[flip] for flip in far_flips]
    swaps = row_swaps(row_tiles)
    key_values = [project((1, 2), 0, [early], sums, weights, qkv_scale, qkv_sign)]
    early_blocks = [lax.ppermute(key_values[0], "height", pairs) for _, _, pairs in swaps]
    for bit in low_bits:
        for flip in list(late):
            late[flip ^ bit] = swap(late[flip], bit)
    late = [late[flip] for flip in far_flips]
    key_values.append(project((1, 2), EARLY, [late], sums, weights, qkv_scale, qkv_sign))
    late_blocks = [lax.ppermute(key_values[1], "height", pairs) for _, _, pairs in swaps]
    queries = project((0,), 0, [early, late], sums, weights, qkv_scale, qkv_sign)
    out_weights = unpack_out(out_codes, key_values[1])

    listed = windows[0]
    qtile_count = listed.shape[0]
    listed = jnp.where(end == 0, listed, listed[::-1])
    near_rows = []
    for by, odd, _ in swaps:
        near_rows.append(jnp.where((row_place // by) % 2 == odd, row_place + by, row_place - by))
    near_rows = jnp.stack(near_rows)[:, None] * qtile_count
    tiles = jnp.stack([end, jnp.int32(1), 2 - end])

    def mask_of(ids):
        allowed = jnp.any(listed[:, :, None] == ids.reshape(1, 1, -1), axis=1)
        return jnp.repeat(allowed.astype(f32), TILE, axis=1)

    own_mask = mask_of(row_place * qtile_count + tiles)
    early_mask = mask_of(near_rows + tiles[None, :2])
    late_mask = mask_of(near_rows + tiles[None, 2:])
    running = attend(place, queries, key_values, own_mask, None, None)
    running = attend(place, queries, early_blocks, early_mask, running, None)
    rotated = attend(
        place, queries, late_blocks, late_mask, running, (oin_sign, halving_order(head_count))
    )

    bits = low_bits + [top]
    scale_rows = out_scale.reshape(-1, HAD)
    sign_rows = out_sign.reshape(-1, HAD)
    result = None
    first = 0
    for columns in CHUNKS:
        send, keep = out_project(rotated, out_weights, scale_rows, first, columns)
        for bit in bits:
            more = swap(send, bit)
            if bit == top:
                break
            total = keep.astype(f32) + more.astype(f32)
            half = total.shape[0] // 2
            send, keep = total[:half].astype(bf16), total[half:]
        result = finish(result, sign_rows, keep, more, first)
        first += columns
    return result[None]


def solution(mesh):
    return jax.shard_map(
        on_device,
        mesh=mesh,
        in_specs=(
            P(("clip", "height"), None, "head"),
            P(),
            P(None, None, "head"),
            P(None, "head"),
            P(None, "head"),
            P(("clip", "height"), None, None),
            P("head"),
            P("head", None),
            P(),
            P(),
        ),
        out_specs=P(("clip", "height"), "head", None),
        check_vma=False,
    )
```

```python
import functools

import jax
import jax.numpy as jnp
import numpy as np
from jax import lax
from jax.experimental import pallas as pl
from jax.experimental.pallas import tpu as pltpu
from jax.sharding import PartitionSpec as P

D = 5120
HD = 128
HEADS = 24
HAD = 128
TILE = 64
HROWS = 4
WTILES = 3
PLANES = 8
WORDS = HAD // PLANES
EARLY = 2 * TILE
QKV_ORDER = "half"
OUT_ORDER = "byte"

epsilon = 1e-06
f32 = jnp.float32
bf16 = jnp.bfloat16
VMEM = pl.BlockSpec(memory_space=pltpu.VMEM)
SMEM = pl.BlockSpec(memory_space=pltpu.SMEM)
ANY = pl.BlockSpec(memory_space=pl.ANY)
HBM = pl.BlockSpec(memory_space=pltpu.HBM)


def shape_of(shape, dtype):
    return jax.ShapeDtypeStruct(tuple(shape), dtype)


def in_hbm(array):
    return pltpu.with_memory_space_constraint(array, pltpu.HBM)


def call(body, out_shape, in_specs, args, name, flops=0, out_specs=None, megabytes=16, **more):
    if out_specs is None:
        out_specs = jax.tree.map(lambda _: VMEM, out_shape)
    moved = sum(a.size * a.dtype.itemsize for a in args)
    return pl.pallas_call(
        body,
        out_shape=out_shape,
        in_specs=in_specs,
        out_specs=out_specs,
        compiler_params=pltpu.CompilerParams(vmem_limit_bytes=megabytes * 2**20),
        cost_estimate=pl.CostEstimate(
            flops=1, bytes_accessed=1, transcendentals=0
        ),
        name=name,
        **more,
    )(*args)


def lanes():
    return lax.broadcasted_iota(jnp.int32, (HAD, HAD), 1)


def hadamard(order):
    row = lax.broadcasted_iota(jnp.int32, (HAD, HAD), 0)
    column = lanes()
    word = PLANES * (column & (WORDS - 1))
    if order == "half":
        column = word + column // WORDS
    if order == "byte":
        column = word + column // (2 * WORDS) + (PLANES // 2) * ((column // WORDS) & 1)
    shared = row & column
    shared = shared ^ (shared >> 4)
    shared = shared ^ (shared >> 2)
    shared = shared ^ (shared >> 1)
    return (1 - 2 * (shared & 1)).astype(f32).astype(bf16)


def double_hadamard():
    plain = hadamard("plain")
    return jnp.concatenate([plain, plain], 0)


def plane_power(base, order):
    lane = lax.broadcasted_iota(jnp.int32, (1, HAD), 1)
    if order == "half":
        power = jnp.minimum(lane // WORDS, PLANES - 2)
    else:
        power = jnp.minimum(lane // (2 * WORDS), PLANES // 2 - 2)
    value = jnp.where(power & 1 == 1, base, 1.0)
    value = value * jnp.where(power & 2 == 2, base**2, 1.0)
    return value * jnp.where(power & 4 == 4, base**4, 1.0)


def turn_factor(order):
    return plane_power(0.25, order) * np.float32(HAD ** (-0.5))


def signed(sign_bits):
    return (2 * sign_bits - 1).astype(f32)


def pieces_of(words, order):
    if order == "half":
        packed = words.astype(jnp.int16)
        masked = [packed & jnp.int16(3 << (2 * k)) for k in range(PLANES - 1)]
        masked.append((words >> 2).astype(jnp.int16) & jnp.int16(3 << (2 * PLANES - 4)))
    else:
        pair = jnp.concatenate([words & 255, words >> 8], 0)
        packed = pair.astype(jnp.int8)
        masked = [packed & jnp.int8(3 << (2 * k)) for k in range(PLANES // 2 - 1)]
        masked.append((pair >> 2).astype(jnp.int8) & jnp.int8(3 << (PLANES - 4)))
    return [piece.astype(bf16) for piece in masked]


def decode(words, order):
    blocks = []
    for first in range(0, words.shape[0], WORDS):
        blocks += pieces_of(words[first : first + WORDS], order)
    return jnp.concatenate(blocks, 0)


def row_correction(row_list, order):
    factor_row = plane_power(4.0, order) * 1.5
    total = None
    for rows in row_list:
        for first in range(0, rows.shape[1], HAD):
            term = rows[:, first : first + HAD].astype(f32)
            total = term if total is None else total + term
    return jnp.sum(total * factor_row, axis=1, keepdims=True)


def rotate_halves(values, doubled):
    high = values.astype(bf16)
    low = (values - high.astype(f32)).astype(bf16)
    return jnp.dot(jnp.concatenate([high, low], 1), doubled, preferred_element_type=f32)


def tile_width(columns):
    for width in (256, 128):
        if columns % width == 0:
            return width


def turn_kernel(place_ref, x_hbm, sign_hbm, own_ref, send_ref, x_ref, sign_ref, sems):
    copies = [
        pltpu.make_async_copy(x_hbm, x_ref, sems.at[0]),
        pltpu.make_async_copy(sign_hbm, sign_ref, sems.at[1]),
    ]
    for copy in copies:
        copy.start()
    matrix = hadamard(QKV_ORDER)
    factor = turn_factor(QKV_ORDER)
    for copy in copies:
        copy.wait()
    blocks = x_ref.shape[1] // HAD
    first = place_ref[0] * blocks
    end = place_ref[1]
    tiles = (end, 1, 2 - end)
    for b in range(blocks):
        cols = slice(b * HAD, (b + 1) * HAD)
        sign_row = signed(sign_ref[pl.ds(first + b, 1), :])
        own = [x_ref[pl.ds(pl.multiple_of(t * TILE, TILE), TILE), cols] for t in tiles]
        flipped = (jnp.concatenate(own, 0).astype(f32) * sign_row).astype(bf16)
        turned = jnp.dot(flipped, matrix, preferred_element_type=f32)
        turned = (turned * factor).astype(bf16)
        own_ref[:, cols] = turned
        send_ref[:TILE, cols] = turned[2 * TILE :]
        send_ref[TILE:, cols] = turned[TILE : 2 * TILE]


def turn(place, own_tokens, in_sign):
    sign_rows = in_sign.reshape(-1, HAD)
    rows, inner = own_tokens.shape
    return call(
        turn_kernel,
        (shape_of((rows, inner), bf16), shape_of((EARLY, inner), bf16)),
        [SMEM, HBM, HBM],
        (place, in_hbm(own_tokens), in_hbm(sign_rows)),
        "turn",
        flops=2 * own_tokens.size * HAD,
        scratch_shapes=[
            pltpu.VMEM(own_tokens.shape, bf16),
            pltpu.VMEM(sign_rows.shape, jnp.int32),
            pltpu.SemaphoreType.DMA((2,)),
        ],
    )


def tie(array, *after):
    return call(
        lambda *refs: None,
        shape_of(array.shape, array.dtype),
        [ANY] * (1 + len(after)),
        (array, *after),
        "tie",
        out_specs=ANY,
        input_output_aliases={0: 0},
    )


def prepare_kernel(near, far, place_ref, *rest):
    shard_refs = rest[: len(near)]
    codes_hbm, sums_ref, far_ref, late_ref, near_ref, sems = rest[len(near) :]
    words, columns = near_ref.shape[2:]

    def fetch(position, kind):
        flip = (near + far)[position]
        first = pl.multiple_of((place_ref[0] ^ flip) * words, WORDS)
        there = position - len(near)
        target = near_ref.at[position, kind] if there < 0 else far_ref.at[there, kind]
        return pltpu.make_async_copy(
            codes_hbm.at[kind, pl.ds(first, words), :], target, sems.at[position, kind]
        )

    for kind in range(3):
        for position in range(len(near)):
            fetch(position, kind).start()
    for position in range(len(near), len(near + far)):
        for kind in range(3):
            fetch(position, kind).start()
    fix = row_correction([ref[...] for ref in shard_refs], QKV_ORDER)
    width = tile_width(columns)
    late_ref[...] = shard_refs[0][:TILE, :]

    def product(kind, carry):
        for position in range(len(near)):
            fetch(position, kind).wait()
        for first in range(0, columns, width):
            cols = slice(first, first + width)
            total = -fix
            for position, ref in enumerate(shard_refs):
                weights = decode(near_ref[position, kind, :, cols], QKV_ORDER)
                total = total + jnp.dot(ref[...], weights, preferred_element_type=f32)
            sums_ref[kind, :, cols] = total
        return carry

    lax.fori_loop(0, 3, product, 0)
    for position in range(len(near), len(near + far)):
        for kind in range(3):
            fetch(position, kind).wait()


def prepare(place, near, far, shards, codes):
    rows, inner = shards[0].shape
    columns = codes.shape[2]
    words = inner // PLANES
    return call(
        functools.partial(prepare_kernel, near, far),
        (
            shape_of((3, rows, columns), f32),
            shape_of((len(far), 3, words, columns), jnp.int32),
            shape_of((TILE, inner), bf16),
        ),
        [SMEM] + [VMEM] * len(near) + [HBM],
        (place, *shards, in_hbm(codes)),
        "prepare",
        flops=16 * rows * inner * 3 * columns,
        scratch_shapes=[
            pltpu.VMEM((len(near), 3, words, columns), jnp.int32),
            pltpu.SemaphoreType.DMA((len(near + far), 3)),
        ],
    )


def project_kernel(kinds, first_row, groups, positions, whole, ending, *rest):
    count = len(positions)
    shard_refs = rest[: groups * count]
    sums_ref, words_ref = rest[groups * count : groups * count + 2]
    if ending:
        scale_ref, sign_ref = rest[-3:-1]
    out_ref = rest[-1]
    columns = sums_ref.shape[2]
    width = tile_width(columns)
    shards = []
    for place in range(count):
        parts = [shard_refs[g * count + place][...] for g in range(groups)]
        shards.append(parts[0] if groups == 1 else jnp.concatenate(parts, 0))
    fix = row_correction(shards, QKV_ORDER)
    row_count = shards[0].shape[0]
    rows = slice(first_row, first_row + row_count)
    doubled = double_hadamard()
    ones = jnp.ones((HD, HD), bf16)
    for place, kind in enumerate(kinds):
        heads = []
        for first in range(0, columns, width):
            cols = slice(first, first + width)
            part = (sums_ref[kind, rows, cols] if whole else sums_ref[place, :, cols]) - fix
            for shard, position in zip(shards, positions):
                weights = decode(words_ref[position, kind, :, cols], QKV_ORDER)
                part = part + jnp.dot(shard, weights, preferred_element_type=f32)
            if not ending:
                out_ref[place, :, cols] = part
                continue
            for lane in range(0, width, HD):
                at = slice(first + lane, first + lane + HD)
                scale_row = scale_ref[kind : kind + 1, at] * np.float32(D ** (-0.5))
                heads.append(part[:, lane : lane + HD] * scale_row)
        if not ending:
            continue
        mixed = rotate_halves(jnp.concatenate(heads, 0), doubled)
        signs = []
        for head in range(len(heads)):
            sign_row = sign_ref[kind : kind + 1, head * HD : (head + 1) * HD]
            sign_row = signed(sign_row) * np.float32(HAD ** (-0.5))
            signs.append(mixed[head * row_count : (head + 1) * row_count] * sign_row)
        if kind != 2:
            square = jnp.concatenate([(part * part).astype(bf16) for part in signs], 0)
            mean = jnp.dot(square, ones, preferred_element_type=f32) * (1.0 / HD)
            factor = lax.rsqrt(mean + epsilon)
            signs = [
                part * factor[head * row_count : (head + 1) * row_count]
                for head, part in enumerate(signs)
            ]
        for head, part in enumerate(signs):
            out_ref[place, :, head * HD : (head + 1) * HD] = part.astype(bf16)


def project(kinds, first_row, groups, positions, sums, words, ending):
    inner = groups[0][0].shape[1]
    columns = sums.shape[2]
    row_count = sum(group[0].shape[0] for group in groups)
    whole = sums.shape[0] == 3
    args = [shard for group in groups for shard in group] + [sums, words]
    if ending is not None:
        args += ending
    return call(
        functools.partial(
            project_kernel, kinds, first_row, len(groups), positions, whole, ending is not None
        ),
        shape_of((len(kinds), row_count, columns), f32 if ending is None else bf16),
        [VMEM] * len(args),
        args,
        "project",
        flops=4 * row_count * inner * len(positions) * len(kinds) * columns,
    )


def near_row(row, swap_pair):
    if swap_pair is None:
        return row
    by, odd = swap_pair
    return jnp.where(lax.rem(row // by, 2) == odd, row + by, row - by)


def window_mask(place_ref, windows_ref, key_tiles, row_count):
    end = place_ref[1]
    order = (end, 1, 2 - end)
    lane = lax.broadcasted_iota(jnp.int32, (1, len(key_tiles) * TILE), 1) // TILE
    ids = None
    for index, (swap_pair, position) in enumerate(key_tiles):
        one = near_row(place_ref[2], swap_pair) * WTILES + order[position]
        ids = jnp.full(lane.shape, one, jnp.int32) if ids is None else jnp.where(lane == index, one, ids)
    masks = []
    for tile in order:
        hit = jnp.zeros(lane.shape, f32)
        for entry in range(windows_ref.shape[1]):
            hit = jnp.where(ids == windows_ref[tile, entry], 1.0, hit)
        masks.append(jnp.broadcast_to(hit, (TILE, lane.shape[1])))
    return jnp.concatenate(masks, 0)


def attend_kernel(key_tiles, blocks, has_sum, last, share_order, place_ref, windows_ref, q_ref, *rest):
    rest = list(rest)
    kv_refs = [rest.pop(0) for _ in range(blocks)]
    sum_ref = rest.pop(0) if has_sum else None
    if last:
        oin_ref, out_ref, rotated_ref = rest
    else:
        (out_ref,) = rest
    row_count, columns = q_ref.shape[1:]
    heads = [slice(head, head + HD) for head in range(0, columns, HD)]
    mask = window_mask(place_ref, windows_ref, key_tiles, row_count)
    scores = []
    for at in heads:
        keys = jnp.concatenate([ref[0, :, at] for ref in kv_refs], 0)
        scores.append(
            lax.dot_general(
                q_ref[0, :, at], keys, (((1,), (1,)), ((), ())), preferred_element_type=f32
            )
        )
    weights = [
        (jnp.exp(score * np.float32(HD ** (-0.5))) * mask).astype(bf16) for score in scores
    ]
    totals = []
    for head, at in enumerate(heads):
        values = jnp.concatenate([ref[1, :, at] for ref in kv_refs], 0)
        values = jnp.concatenate([values, jnp.ones_like(values)], 1)
        total = jnp.dot(weights[head], values, preferred_element_type=f32)
        if has_sum:
            total = total + sum_ref[head]
        totals.append(total)
    if not last:
        for head, total in enumerate(totals):
            out_ref[head] = total
        return
    matrix = hadamard(OUT_ORDER)
    factor = turn_factor(OUT_ORDER)
    end = place_ref[1]
    for head, at in enumerate(heads):
        attended = (totals[head][:, :HD] / totals[head][:, HD:]).astype(bf16)
        sign_row = signed(oin_ref[head : head + 1, :])
        flipped = (attended.astype(f32) * sign_row).astype(bf16)
        rotated = jnp.dot(flipped, matrix, preferred_element_type=f32) * factor
        for position, tile in enumerate((end, 1, 2 - end)):
            rotated_ref[pl.ds(pl.multiple_of(tile * TILE, TILE), TILE), at] = rotated[
                position * TILE : (position + 1) * TILE
            ]
    share = row_count // len(share_order)
    pieces = []
    for flip in share_order:
        owner = place_ref[0] ^ flip
        pieces.append(rotated_ref[pl.ds(pl.multiple_of(owner * share, 8), share), :])
    out_ref[...] = jnp.concatenate(pieces, 0).astype(bf16)


def attend(place, windows, queries, blocks, key_tiles, running, ending):
    row_count, columns = queries.shape[1:]
    args = [place, windows, queries, *blocks]
    if running is not None:
        args.append(running)
    scratch, share_order = [], None
    if ending is None:
        out_shape = shape_of((columns // HD, row_count, 2 * HD), f32)
    else:
        oin_sign, share_order = ending
        args.append(oin_sign.reshape(-1, HAD))
        out_shape = shape_of((row_count, columns), bf16)
        scratch = [pltpu.VMEM((row_count, columns), f32)]
    return call(
        functools.partial(
            attend_kernel,
            key_tiles,
            len(blocks),
            running is not None,
            ending is not None,
            share_order,
        ),
        out_shape,
        [SMEM] * 2 + [VMEM] * (len(args) - 2),
        args,
        "attend",
        flops=8 * row_count * columns * len(key_tiles) * TILE,
        scratch_shapes=scratch,
    )


def unpack_out_kernel(codes_ref, after_ref, weights_ref):
    for first in range(0, codes_ref.shape[0], WORDS):

        def some(step, carry):
            cols = pl.ds(pl.multiple_of(step * 512, 512), 512)
            at = first * PLANES
            for piece in pieces_of(codes_ref[first : first + WORDS, cols], OUT_ORDER):
                weights_ref[at : at + piece.shape[0], cols] = piece
                at += piece.shape[0]
            return carry

        lax.fori_loop(0, codes_ref.shape[1] // 512, some, 0)


def unpack_out(codes, after):
    words, columns = codes.shape
    return call(
        unpack_out_kernel,
        shape_of((words * PLANES, columns), bf16),
        [VMEM, ANY],
        (codes, after),
        "unpack_out",
        flops=2000 * words * columns,
    )


def out_kernel(first, rotated_ref, weights_ref, scale_ref, after_ref, send_ref, keep_ref):
    rows = rotated_ref[...]
    fix = row_correction([rows], OUT_ORDER)
    half, columns = send_ref.shape
    width = 256
    for at in range(0, columns, width):
        cols = slice(first + at, first + at + width)
        part = jnp.dot(rows, weights_ref[:, cols], preferred_element_type=f32) - fix
        for lane in range(0, width, HAD):
            place = (first + at + lane) // HAD
            scale_row = scale_ref[place : place + 1, :] * np.float32((HEADS * HD) ** (-0.5))
            done = (part[:, lane : lane + HAD] * scale_row).astype(bf16)
            send_ref[:, at + lane : at + lane + HAD] = done[:half]
            keep_ref[:, at + lane : at + lane + HAD] = done[half:]


def out_project(rotated, weights, scale_rows, after, first, columns):
    row_count, inner = rotated.shape
    result = shape_of((row_count // 2, columns), bf16)
    return call(
        functools.partial(out_kernel, first),
        (result, result),
        [VMEM] * 3 + [ANY],
        (rotated, weights, scale_rows, after),
        "out_project",
        flops=2 * row_count * inner * columns,
    )


def finish_kernel(first, has_base, sign_ref, keep_ref, more_ref, *rest):
    out_hbm, done_ref, sem = rest[1:] if has_base else rest
    columns = keep_ref.shape[1]
    doubled = double_hadamard()
    for at in range(0, columns, HAD):
        cols = slice(at, at + HAD)
        total = keep_ref[:, cols].astype(f32) + more_ref[:, cols].astype(f32)
        place = (first + at) // HAD
        sign_row = signed(sign_ref[place : place + 1, :]) * np.float32(HAD ** (-0.5))
        done_ref[:, cols] = (rotate_halves(total, doubled) * sign_row).astype(bf16)
    copy = pltpu.make_async_copy(done_ref, out_hbm.at[:, pl.ds(first, columns)], sem)
    copy.start()
    copy.wait()


def finish(base, sign_rows, keep, more, first):
    share, columns = keep.shape
    args = [sign_rows, keep, more]
    in_specs = [VMEM] * 3
    aliases = {}
    if base is not None:
        args.append(base)
        in_specs.append(ANY)
        aliases = {3: 0}
    return call(
        functools.partial(finish_kernel, first, base is not None),
        shape_of((share, D), bf16),
        in_specs,
        args,
        "finish",
        flops=4 * share * columns * HAD,
        out_specs=ANY,
        scratch_shapes=[pltpu.VMEM((share, columns), bf16), pltpu.SemaphoreType.DMA],
        input_output_aliases=aliases,
    )


def swap(shard, bit):
    peers = lax.axis_size("head")
    return lax.ppermute(shard, "head", [(i, i ^ bit) for i in range(peers)])


def row_swaps(row_tiles):
    swaps = []
    for by in (1, 3, 4, 5) if row_tiles > HROWS else (1,):
        for odd in (0, 1):
            low = [i for i in range(row_tiles - by) if (i // by) % 2 == odd]
            swaps.append((by, odd, [(i, i + by) for i in low] + [(i + by, i) for i in low]))
    return swaps


def halving_order(head_count):
    flips = [0]
    bit = head_count // 2
    while bit >= 1:
        flips = [f | bit for f in flips] + flips
        bit //= 2
    return tuple(flips)


CHUNKS = (2048, 3072)


def on_device(
    tokens,
    in_sign,
    qkv_codes,
    qkv_scale,
    qkv_sign,
    windows,
    oin_sign,
    out_codes,
    out_scale,
    out_sign,
):
    head_count = lax.axis_size("head")
    row_tiles = lax.axis_size("height")
    row_place = lax.axis_index("height")
    head_place = lax.axis_index("head").astype(jnp.int32)
    top = head_count // 2
    end = jnp.where(head_place >= top, 0, 2).astype(jnp.int32)
    place = jnp.stack([head_place, end, row_place.astype(jnp.int32)])
    low_bits = [1 << b for b in range(top.bit_length() - 1)]

    own, early = turn(place, tokens[0], in_sign)
    early = swap(early, top)
    near = {0: own}
    for bit in low_bits:
        for flip in list(near):
            near[flip ^ bit] = swap(near[flip], bit)
    codes = jnp.transpose(qkv_codes, (1, 0, 2))
    near_flips = tuple(sorted(near))
    far_flips = tuple(flip ^ top for flip in near_flips)
    sums, words, late = prepare(
        place, near_flips, far_flips, [near[flip] for flip in near_flips], codes
    )
    out_weights = unpack_out(out_codes, sums)
    late = {top: swap(late, top)}
    early = {top: tie(early, sums, out_weights)}
    for bit in low_bits:
        for flip in list(early):
            early[flip ^ bit] = swap(early[flip], bit)
    early = [early[flip] for flip in far_flips]
    swaps = row_swaps(row_tiles)
    ending = [qkv_scale, qkv_sign]
    every = tuple(range(len(far_flips)))
    partial = project((1, 2), 0, [early[:-1]], every[:-1], sums, words, None)
    key_values = [project((1, 2), 0, [early[-1:]], every[-1:], partial, words, ending)]
    early_blocks = [lax.ppermute(key_values[0], "height", pairs) for _, _, pairs in swaps]
    for bit in low_bits:
        for flip in list(late):
            late[flip ^ bit] = swap(late[flip], bit)
    late = [late[flip] for flip in far_flips]
    key_values.append(project((1, 2), EARLY, [late], every, sums, words, ending))
    late_blocks = [lax.ppermute(key_values[1], "height", pairs) for _, _, pairs in swaps]
    queries = project((0,), 0, [early, late], every, sums, words, ending)

    listed = windows[0]
    own_tiles = tuple((None, position) for position in range(WTILES))
    early_tiles = tuple(((by, odd), position) for by, odd, _ in swaps for position in (0, 1))
    late_tiles = tuple(((by, odd), 2) for by, odd, _ in swaps)
    running = attend(place, listed, queries, key_values, own_tiles, None, None)
    running = attend(place, listed, queries, early_blocks, early_tiles, running, None)
    rotated = attend(
        place,
        listed,
        queries,
        late_blocks,
        late_tiles,
        running,
        (oin_sign, halving_order(head_count)),
    )

    bits = low_bits + [top]
    scale_rows = out_scale.reshape(-1, HAD)
    sign_rows = out_sign.reshape(-1, HAD)
    result = None
    first = 0
    send = rotated
    for columns in CHUNKS:
        send, keep = out_project(rotated, out_weights, scale_rows, send, first, columns)
        part = send
        for bit in bits:
            more = swap(part, bit)
            if bit == top:
                break
            total = keep.astype(f32) + more.astype(f32)
            half = total.shape[0] // 2
            part, keep = total[:half].astype(bf16), total[half:]
        send = part
        result = finish(result, sign_rows, keep, more, first)
        first += columns
    return result[None]


def solution(mesh):
    return jax.shard_map(
        on_device,
        mesh=mesh,
        in_specs=(
            P(("clip", "height"), None, "head"),
            P(),
            P(None, None, "head"),
            P(None, "head"),
            P(None, "head"),
            P(("clip", "height"), None, None),
            P("head"),
            P("head", None),
            P(),
            P(),
        ),
        out_specs=P(("clip", "height"), "head", None),
        check_vma=False,
    )
```

```python
import functools

import jax
import jax.numpy as jnp
import numpy as np
from jax import lax
from jax.experimental import pallas as pl
from jax.experimental.pallas import tpu as pltpu
from jax.sharding import PartitionSpec as P

D = 5120
HD = 128
HEADS = 24
HAD = 128
TILE = 64
HROWS = 4
WTILES = 3
PLANES = 8
WORDS = HAD // PLANES
QKV_ORDER = "half"
OUT_ORDER = "byte"

epsilon = 1e-06
f32 = jnp.float32
bf16 = jnp.bfloat16
VMEM = pl.BlockSpec(memory_space=pltpu.VMEM)
SMEM = pl.BlockSpec(memory_space=pltpu.SMEM)
ANY = pl.BlockSpec(memory_space=pl.ANY)
HBM = pl.BlockSpec(memory_space=pltpu.HBM)


def shape_of(shape, dtype):
    return jax.ShapeDtypeStruct(tuple(shape), dtype)


def in_hbm(array):
    return pltpu.with_memory_space_constraint(array, pltpu.HBM)


def call(body, out_shape, in_specs, args, name, out_specs=None, megabytes=16, **more):
    if out_specs is None:
        out_specs = jax.tree.map(lambda _: VMEM, out_shape)
    return pl.pallas_call(
        body,
        out_shape=out_shape,
        in_specs=in_specs,
        out_specs=out_specs,
        compiler_params=pltpu.CompilerParams(vmem_limit_bytes=megabytes * 2**20),
        cost_estimate=pl.CostEstimate(flops=1, bytes_accessed=1, transcendentals=0),
        name=name,
        **more,
    )(*args)


def lanes():
    return lax.broadcasted_iota(jnp.int32, (HAD, HAD), 1)


def hadamard(order):
    row = lax.broadcasted_iota(jnp.int32, (HAD, HAD), 0)
    column = lanes()
    word = PLANES * (column & (WORDS - 1))
    if order == "half":
        column = word + column // WORDS
    if order == "byte":
        column = word + column // (2 * WORDS) + (PLANES // 2) * ((column // WORDS) & 1)
    shared = row & column
    shared = shared ^ (shared >> 4)
    shared = shared ^ (shared >> 2)
    shared = shared ^ (shared >> 1)
    return (1 - 2 * (shared & 1)).astype(f32).astype(bf16)


def double_hadamard():
    plain = hadamard("plain")
    return jnp.concatenate([plain, plain], 0)


def plane_power(base, order):
    lane = lax.broadcasted_iota(jnp.int32, (1, HAD), 1)
    if order == "half":
        power = jnp.minimum(lane // WORDS, PLANES - 2)
    else:
        power = jnp.minimum(lane // (2 * WORDS), PLANES // 2 - 2)
    value = jnp.where(power & 1 == 1, base, 1.0)
    value = value * jnp.where(power & 2 == 2, base**2, 1.0)
    return value * jnp.where(power & 4 == 4, base**4, 1.0)


def turn_factor(order):
    return plane_power(0.25, order) * np.float32(HAD ** (-0.5))


def signed(sign_bits):
    return (2 * sign_bits - 1).astype(f32)


def pieces_of(words, order):
    if order == "half":
        packed = words.astype(jnp.int16)
        masked = [packed & jnp.int16(3 << (2 * k)) for k in range(PLANES - 1)]
        masked.append((words >> 2).astype(jnp.int16) & jnp.int16(3 << (2 * PLANES - 4)))
    else:
        pair = jnp.concatenate([words & 255, words >> 8], 0)
        packed = pair.astype(jnp.int8)
        masked = [packed & jnp.int8(3 << (2 * k)) for k in range(PLANES // 2 - 1)]
        masked.append((pair >> 2).astype(jnp.int8) & jnp.int8(3 << (PLANES - 4)))
    return [piece.astype(bf16) for piece in masked]


def decode(words, order):
    blocks = []
    for first in range(0, words.shape[0], WORDS):
        blocks += pieces_of(words[first : first + WORDS], order)
    return jnp.concatenate(blocks, 0)


def row_correction(row_list, order):
    factor_row = plane_power(4.0, order) * 1.5
    total = None
    for rows in row_list:
        for first in range(0, rows.shape[1], HAD):
            term = rows[:, first : first + HAD].astype(f32)
            total = term if total is None else total + term
    return jnp.sum(total * factor_row, axis=1, keepdims=True)


def rotate_halves(values, doubled):
    high = values.astype(bf16)
    low = (values - high.astype(f32)).astype(bf16)
    return jnp.dot(jnp.concatenate([high, low], 1), doubled, preferred_element_type=f32)


def tile_width(columns):
    for width in (256, 128):
        if columns % width == 0:
            return width


def turn_kernel(place_ref, x_hbm, sign_hbm, own_ref, send_ref, x_ref, sign_ref, sems):
    copies = [
        pltpu.make_async_copy(x_hbm, x_ref, sems.at[0]),
        pltpu.make_async_copy(sign_hbm, sign_ref, sems.at[1]),
    ]
    for copy in copies:
        copy.start()
    matrix = hadamard(QKV_ORDER)
    factor = turn_factor(QKV_ORDER)
    for copy in copies:
        copy.wait()
    blocks = x_ref.shape[1] // HAD
    first = place_ref[0] * blocks
    for b in range(blocks):
        cols = slice(b * HAD, (b + 1) * HAD)
        sign_row = signed(sign_ref[pl.ds(first + b, 1), :])
        flipped = (x_ref[:, cols].astype(f32) * sign_row).astype(bf16)
        turned = jnp.dot(flipped, matrix, preferred_element_type=f32)
        turned = (turned * factor).astype(bf16)
        own_ref[:, cols] = turned
        send_ref[:, cols] = turned[: send_ref.shape[0]]


def turn(place, own_tokens, in_sign):
    sign_rows = in_sign.reshape(-1, HAD)
    rows, inner = own_tokens.shape
    return call(
        turn_kernel,
        (shape_of((rows, inner), bf16), shape_of((rows // 2, inner), bf16)),
        [SMEM, HBM, HBM],
        (place, in_hbm(own_tokens), in_hbm(sign_rows)),
        "turn",
        scratch_shapes=[
            pltpu.VMEM(own_tokens.shape, bf16),
            pltpu.VMEM(sign_rows.shape, jnp.int32),
            pltpu.SemaphoreType.DMA((2,)),
        ],
    )


def tie(array, *after):
    return call(
        lambda *refs: None,
        shape_of(array.shape, array.dtype),
        [ANY] * (1 + len(after)),
        (array, *after),
        "tie",
        out_specs=ANY,
        input_output_aliases={0: 0},
    )


def prepare_kernel(near, far, place_ref, *rest):
    shard_refs = rest[: len(near)]
    codes_hbm, sums_ref, far_ref, late_ref, near_ref, sems = rest[len(near) :]
    words, columns = near_ref.shape[2:]

    def fetch(position, kind):
        flip = (near + far)[position]
        first = pl.multiple_of((place_ref[0] ^ flip) * words, WORDS)
        there = position - len(near)
        target = near_ref.at[position, kind] if there < 0 else far_ref.at[there, kind]
        return pltpu.make_async_copy(
            codes_hbm.at[kind, pl.ds(first, words), :], target, sems.at[position, kind]
        )

    for kind in range(3):
        for position in range(len(near)):
            fetch(position, kind).start()
    for position in range(len(near), len(near + far)):
        for kind in range(3):
            fetch(position, kind).start()
    fix = row_correction([ref[...] for ref in shard_refs], QKV_ORDER)
    width = tile_width(columns)
    late_ref[...] = shard_refs[0][late_ref.shape[0] :, :]

    def product(kind, carry):
        for position in range(len(near)):
            fetch(position, kind).wait()
        for first in range(0, columns, width):
            cols = slice(first, first + width)
            total = -fix
            for position, ref in enumerate(shard_refs):
                weights = decode(near_ref[position, kind, :, cols], QKV_ORDER)
                total = total + jnp.dot(ref[...], weights, preferred_element_type=f32)
            sums_ref[kind, :, cols] = total
        return carry

    lax.fori_loop(0, 3, product, 0)
    for position in range(len(near), len(near + far)):
        for kind in range(3):
            fetch(position, kind).wait()


def prepare(place, near, far, shards, codes):
    rows, inner = shards[0].shape
    columns = codes.shape[2]
    words = inner // PLANES
    return call(
        functools.partial(prepare_kernel, near, far),
        (
            shape_of((3, rows, columns), f32),
            shape_of((len(far), 3, words, columns), jnp.int32),
            shape_of((rows // 2, inner), bf16),
        ),
        [SMEM] + [VMEM] * len(near) + [HBM],
        (place, *shards, in_hbm(codes)),
        "prepare",
        scratch_shapes=[
            pltpu.VMEM((len(near), 3, words, columns), jnp.int32),
            pltpu.SemaphoreType.DMA((len(near + far), 3)),
        ],
    )


def project_kernel(kinds, first_row, groups, positions, whole, ending, *rest):
    count = len(positions)
    shard_refs = rest[: groups * count]
    sums_ref, words_ref = rest[groups * count : groups * count + 2]
    if ending:
        scale_ref, sign_ref = rest[-3:-1]
    out_ref = rest[-1]
    columns = sums_ref.shape[2]
    width = tile_width(columns)
    shards = []
    for place in range(count):
        parts = [shard_refs[g * count + place][...] for g in range(groups)]
        shards.append(parts[0] if groups == 1 else jnp.concatenate(parts, 0))
    fix = row_correction(shards, QKV_ORDER)
    row_count = shards[0].shape[0]
    rows = slice(first_row, first_row + row_count)
    doubled = double_hadamard()
    ones = jnp.ones((HD, HD), bf16)
    for place, kind in enumerate(kinds):
        heads = []
        for first in range(0, columns, width):
            cols = slice(first, first + width)
            part = (sums_ref[kind, rows, cols] if whole else sums_ref[place, :, cols]) - fix
            for shard, position in zip(shards, positions):
                weights = decode(words_ref[position, kind, :, cols], QKV_ORDER)
                part = part + jnp.dot(shard, weights, preferred_element_type=f32)
            if not ending:
                out_ref[place, :, cols] = part
                continue
            for lane in range(0, width, HD):
                at = slice(first + lane, first + lane + HD)
                scale_row = scale_ref[kind : kind + 1, at] * np.float32(D ** (-0.5))
                heads.append(part[:, lane : lane + HD] * scale_row)
        if not ending:
            continue
        mixed = rotate_halves(jnp.concatenate(heads, 0), doubled)
        signs = []
        for head in range(len(heads)):
            sign_row = sign_ref[kind : kind + 1, head * HD : (head + 1) * HD]
            sign_row = signed(sign_row) * np.float32(HAD ** (-0.5))
            signs.append(mixed[head * row_count : (head + 1) * row_count] * sign_row)
        if kind != 2:
            square = jnp.concatenate([(part * part).astype(bf16) for part in signs], 0)
            mean = jnp.dot(square, ones, preferred_element_type=f32) * (1.0 / HD)
            factor = lax.rsqrt(mean + epsilon)
            signs = [
                part * factor[head * row_count : (head + 1) * row_count]
                for head, part in enumerate(signs)
            ]
        for head, part in enumerate(signs):
            out_ref[place, :, head * HD : (head + 1) * HD] = part.astype(bf16)


def project(kinds, first_row, groups, positions, sums, words, ending):
    inner = groups[0][0].shape[1]
    columns = sums.shape[2]
    row_count = sum(group[0].shape[0] for group in groups)
    whole = sums.shape[0] == 3
    args = [shard for group in groups for shard in group] + [sums, words]
    if ending is not None:
        args += ending
    return call(
        functools.partial(
            project_kernel, kinds, first_row, len(groups), positions, whole, ending is not None
        ),
        shape_of((len(kinds), row_count, columns), f32 if ending is None else bf16),
        [VMEM] * len(args),
        args,
        "project",
    )


def near_row(row, swap_pair):
    if swap_pair is None:
        return row
    by, odd = swap_pair
    return jnp.where(lax.rem(row // by, 2) == odd, row + by, row - by)


def window_mask(place_ref, windows_ref, segments, row_count):
    lane = lax.broadcasted_iota(jnp.int32, (1, sum(rows for _, _, rows in segments)), 1)
    ids, base = None, 0
    for swap_pair, first, rows in segments:
        tile = (lane + (first - base)) // TILE
        ids_here = near_row(place_ref[1], swap_pair) * WTILES + tile
        ids = ids_here if ids is None else jnp.where(lane >= base, ids_here, ids)
        base += rows
    masks = []
    for tile in range(row_count // TILE):
        hit = jnp.zeros(lane.shape, f32)
        for entry in range(windows_ref.shape[1]):
            hit = jnp.where(ids == windows_ref[tile, entry], 1.0, hit)
        masks.append(jnp.broadcast_to(hit, (TILE, lane.shape[1])))
    return jnp.concatenate(masks, 0)


def attend_kernel(segments, blocks, has_sum, last, share_order, place_ref, windows_ref, q_ref, *rest):
    rest = list(rest)
    kv_refs = [rest.pop(0) for _ in range(blocks)]
    sum_ref = rest.pop(0) if has_sum else None
    if last:
        oin_ref, out_ref, rotated_ref = rest
    else:
        (out_ref,) = rest
    row_count, columns = q_ref.shape[1:]
    heads = [slice(head, head + HD) for head in range(0, columns, HD)]
    mask = window_mask(place_ref, windows_ref, segments, row_count)
    scores = []
    for at in heads:
        keys = jnp.concatenate([ref[0, :, at] for ref in kv_refs], 0)
        scores.append(
            lax.dot_general(
                q_ref[0, :, at], keys, (((1,), (1,)), ((), ())), preferred_element_type=f32
            )
        )
    weights = [
        (jnp.exp(score * np.float32(HD ** (-0.5))) * mask).astype(bf16) for score in scores
    ]
    totals = []
    for head, at in enumerate(heads):
        values = jnp.concatenate([ref[1, :, at] for ref in kv_refs], 0)
        values = jnp.concatenate([values, jnp.ones_like(values)], 1)
        total = jnp.dot(weights[head], values, preferred_element_type=f32)
        if has_sum:
            total = total + sum_ref[head]
        totals.append(total)
    if not last:
        for head, total in enumerate(totals):
            out_ref[head] = total
        return
    matrix = hadamard(OUT_ORDER)
    factor = turn_factor(OUT_ORDER)
    for head, at in enumerate(heads):
        attended = (totals[head][:, :HD] / totals[head][:, HD:]).astype(bf16)
        sign_row = signed(oin_ref[head : head + 1, :])
        flipped = (attended.astype(f32) * sign_row).astype(bf16)
        rotated_ref[:, at] = jnp.dot(flipped, matrix, preferred_element_type=f32) * factor
    share = row_count // len(share_order)
    pieces = []
    for flip in share_order:
        owner = place_ref[0] ^ flip
        pieces.append(rotated_ref[pl.ds(pl.multiple_of(owner * share, 8), share), :])
    out_ref[...] = jnp.concatenate(pieces, 0).astype(bf16)


def attend(place, windows, queries, blocks, segments, running, ending):
    row_count, columns = queries.shape[1:]
    args = [place, windows, queries, *blocks]
    if running is not None:
        args.append(running)
    scratch, share_order = [], None
    if ending is None:
        out_shape = shape_of((columns // HD, row_count, 2 * HD), f32)
    else:
        oin_sign, share_order = ending
        args.append(oin_sign.reshape(-1, HAD))
        out_shape = shape_of((row_count, columns), bf16)
        scratch = [pltpu.VMEM((row_count, columns), f32)]
    return call(
        functools.partial(
            attend_kernel,
            segments,
            len(blocks),
            running is not None,
            ending is not None,
            share_order,
        ),
        out_shape,
        [SMEM] * 2 + [VMEM] * (len(args) - 2),
        args,
        "attend",
        scratch_shapes=scratch,
    )


def unpack_out_kernel(codes_ref, after_ref, weights_ref):
    for first in range(0, codes_ref.shape[0], WORDS):

        def some(step, carry):
            cols = pl.ds(pl.multiple_of(step * 512, 512), 512)
            at = first * PLANES
            for piece in pieces_of(codes_ref[first : first + WORDS, cols], OUT_ORDER):
                weights_ref[at : at + piece.shape[0], cols] = piece
                at += piece.shape[0]
            return carry

        lax.fori_loop(0, codes_ref.shape[1] // 512, some, 0)


def unpack_out(codes, after):
    words, columns = codes.shape
    return call(
        unpack_out_kernel,
        shape_of((words * PLANES, columns), bf16),
        [VMEM, ANY],
        (codes, after),
        "unpack_out",
    )


def out_kernel(first, rotated_ref, weights_ref, scale_ref, send_ref, keep_ref):
    rows = rotated_ref[...]
    fix = row_correction([rows], OUT_ORDER)
    half, columns = send_ref.shape
    width = 256
    for at in range(0, columns, width):
        cols = slice(first + at, first + at + width)
        part = jnp.dot(rows, weights_ref[:, cols], preferred_element_type=f32) - fix
        for lane in range(0, width, HAD):
            place = (first + at + lane) // HAD
            scale_row = scale_ref[place : place + 1, :] * np.float32((HEADS * HD) ** (-0.5))
            done = (part[:, lane : lane + HAD] * scale_row).astype(bf16)
            send_ref[:, at + lane : at + lane + HAD] = done[:half]
            keep_ref[:, at + lane : at + lane + HAD] = done[half:]


def out_project(rotated, weights, scale_rows, first, columns):
    row_count, inner = rotated.shape
    result = shape_of((row_count // 2, columns), bf16)
    return call(
        functools.partial(out_kernel, first),
        (result, result),
        [VMEM] * 3,
        (rotated, weights, scale_rows),
        "out_project",
    )


def finish_kernel(first, has_base, sign_ref, keep_ref, more_ref, *rest):
    out_hbm, done_ref, sem = rest[1:] if has_base else rest
    columns = keep_ref.shape[1]
    doubled = double_hadamard()
    for at in range(0, columns, HAD):
        cols = slice(at, at + HAD)
        total = keep_ref[:, cols].astype(f32) + more_ref[:, cols].astype(f32)
        place = (first + at) // HAD
        sign_row = signed(sign_ref[place : place + 1, :]) * np.float32(HAD ** (-0.5))
        done_ref[:, cols] = (rotate_halves(total, doubled) * sign_row).astype(bf16)
    copy = pltpu.make_async_copy(done_ref, out_hbm.at[:, pl.ds(first, columns)], sem)
    copy.start()
    copy.wait()


def finish(base, sign_rows, keep, more, first):
    share, columns = keep.shape
    args = [sign_rows, keep, more]
    in_specs = [VMEM] * 3
    aliases = {}
    if base is not None:
        args.append(base)
        in_specs.append(ANY)
        aliases = {3: 0}
    return call(
        functools.partial(finish_kernel, first, base is not None),
        shape_of((share, D), bf16),
        in_specs,
        args,
        "finish",
        out_specs=ANY,
        scratch_shapes=[pltpu.VMEM((share, columns), bf16), pltpu.SemaphoreType.DMA],
        input_output_aliases=aliases,
    )


def swap(shard, bit):
    peers = lax.axis_size("head")
    return lax.ppermute(shard, "head", [(i, i ^ bit) for i in range(peers)])


def row_swaps(row_tiles):
    swaps = []
    for by in (1, 3, 4, 5) if row_tiles > HROWS else (1,):
        for odd in (0, 1):
            low = [i for i in range(row_tiles - by) if (i // by) % 2 == odd]
            swaps.append((by, odd, [(i, i + by) for i in low] + [(i + by, i) for i in low]))
    return swaps


def halving_order(head_count):
    flips = [0]
    bit = head_count // 2
    while bit >= 1:
        flips = [f | bit for f in flips] + flips
        bit //= 2
    return tuple(flips)


CHUNKS = (3072, 2048)


def on_device(
    tokens,
    in_sign,
    qkv_codes,
    qkv_scale,
    qkv_sign,
    windows,
    oin_sign,
    out_codes,
    out_scale,
    out_sign,
):
    head_count = lax.axis_size("head")
    row_tiles = lax.axis_size("height")
    row_place = lax.axis_index("height")
    head_place = lax.axis_index("head").astype(jnp.int32)
    top = head_count // 2
    place = jnp.stack([head_place, row_place.astype(jnp.int32)])
    low_bits = [1 << b for b in range(top.bit_length() - 1)]

    own, early = turn(place, tokens[0], in_sign)
    half_rows = early.shape[0]
    early = swap(early, top)
    near = {0: own}
    for bit in low_bits:
        for flip in list(near):
            near[flip ^ bit] = swap(near[flip], bit)
    codes = jnp.transpose(qkv_codes, (1, 0, 2))
    near_flips = tuple(sorted(near))
    far_flips = tuple(flip ^ top for flip in near_flips)
    sums, words, late = prepare(
        place, near_flips, far_flips, [near[flip] for flip in near_flips], codes
    )
    late = swap(late, top)
    swaps = row_swaps(row_tiles)
    ending = [qkv_scale, qkv_sign]
    every = tuple(range(len(far_flips)))
    halves, key_values, moved = [], [], []
    for half, first_row in ((early, 0), (late, half_rows)):
        shards = {top: tie(half, *key_values, sums)}
        for bit in low_bits:
            for flip in list(shards):
                shards[flip ^ bit] = swap(shards[flip], bit)
        shards = [shards[flip] for flip in far_flips]
        halves.append(shards)
        partial = project((1, 2), first_row, [shards[:-1]], every[:-1], sums, words, None)
        key_values.append(project((1, 2), 0, [shards[-1:]], every[-1:], partial, words, ending))
        moved.append([lax.ppermute(key_values[-1], "height", pairs) for _, _, pairs in swaps])
    queries = project((0,), 0, halves, every, sums, words, ending)
    out_weights = unpack_out(out_codes, key_values[1])

    listed = windows[0]
    own_rows = ((None, 0, half_rows), (None, half_rows, half_rows))
    early_rows = tuple(((by, odd), 0, half_rows) for by, odd, _ in swaps)
    late_rows = tuple(((by, odd), half_rows, half_rows) for by, odd, _ in swaps)
    running = attend(place, listed, queries, key_values, own_rows, None, None)
    running = attend(place, listed, queries, moved[0], early_rows, running, None)
    rotated = attend(
        place,
        listed,
        queries,
        moved[1],
        late_rows,
        running,
        (oin_sign, halving_order(head_count)),
    )

    bits = low_bits + [top]
    scale_rows = out_scale.reshape(-1, HAD)
    sign_rows = out_sign.reshape(-1, HAD)
    result = None
    first = 0
    for columns in CHUNKS:
        part, keep = out_project(rotated, out_weights, scale_rows, first, columns)
        for bit in bits:
            more = swap(part, bit)
            if bit == top:
                break
            total = keep.astype(f32) + more.astype(f32)
            half = total.shape[0] // 2
            part, keep = total[:half].astype(bf16), total[half:]
        result = finish(result, sign_rows, keep, more, first)
        first += columns
    return result[None]


def solution(mesh):
    return jax.shard_map(
        on_device,
        mesh=mesh,
        in_specs=(
            P(("clip", "height"), None, "head"),
            P(),
            P(None, None, "head"),
            P(None, "head"),
            P(None, "head"),
            P(("clip", "height"), None, None),
            P("head"),
            P("head", None),
            P(),
            P(),
        ),
        out_specs=P(("clip", "height"), "head", None),
        check_vma=False,
    )
```

```python
import functools

import jax
import jax.numpy as jnp
import numpy as np
from jax import lax
from jax.experimental import pallas as pl
from jax.experimental.pallas import tpu as pltpu
from jax.sharding import PartitionSpec as P

D = 5120
HD = 128
HEADS = 24
HAD = 128
TILE = 64
HROWS = 4
WTILES = 3
PLANES = 8
WORDS = HAD // PLANES
QKV_ORDER = "half"
OUT_ORDER = "byte"

epsilon = 1e-06
f32 = jnp.float32
bf16 = jnp.bfloat16
VMEM = pl.BlockSpec(memory_space=pltpu.VMEM)
SMEM = pl.BlockSpec(memory_space=pltpu.SMEM)
ANY = pl.BlockSpec(memory_space=pl.ANY)
HBM = pl.BlockSpec(memory_space=pltpu.HBM)


def shape_of(shape, dtype):
    return jax.ShapeDtypeStruct(tuple(shape), dtype)


def in_hbm(array):
    return pltpu.with_memory_space_constraint(array, pltpu.HBM)


def call(body, out_shape, in_specs, args, name, out_specs=None, megabytes=16, flops=1, **more):
    if out_specs is None:
        out_specs = jax.tree.map(lambda _: VMEM, out_shape)
    return pl.pallas_call(
        body,
        out_shape=out_shape,
        in_specs=in_specs,
        out_specs=out_specs,
        compiler_params=pltpu.CompilerParams(vmem_limit_bytes=megabytes * 2**20),
        cost_estimate=pl.CostEstimate(flops=flops, bytes_accessed=1, transcendentals=0),
        name=name,
        **more,
    )(*args)


def lanes():
    return lax.broadcasted_iota(jnp.int32, (HAD, HAD), 1)


def hadamard(order):
    row = lax.broadcasted_iota(jnp.int32, (HAD, HAD), 0)
    column = lanes()
    word = PLANES * (column & (WORDS - 1))
    if order == "half":
        column = word + column // WORDS
    if order == "byte":
        column = word + column // (2 * WORDS) + (PLANES // 2) * ((column // WORDS) & 1)
    shared = row & column
    shared = shared ^ (shared >> 4)
    shared = shared ^ (shared >> 2)
    shared = shared ^ (shared >> 1)
    return (1 - 2 * (shared & 1)).astype(f32).astype(bf16)


def double_hadamard():
    plain = hadamard("plain")
    return jnp.concatenate([plain, plain], 0)


def plane_power(base, order):
    lane = lax.broadcasted_iota(jnp.int32, (1, HAD), 1)
    if order == "half":
        power = jnp.minimum(lane // WORDS, PLANES - 2)
    else:
        power = jnp.minimum(lane // (2 * WORDS), PLANES // 2 - 2)
    value = jnp.where(power & 1 == 1, base, 1.0)
    value = value * jnp.where(power & 2 == 2, base**2, 1.0)
    return value * jnp.where(power & 4 == 4, base**4, 1.0)


def turn_factor(order):
    return plane_power(0.25, order) * np.float32(HAD ** (-0.5))


def signed(sign_bits):
    return (2 * sign_bits - 1).astype(f32)


def pieces_of(words, order):
    if order == "half":
        packed = words.astype(jnp.int16)
        masked = [packed & jnp.int16(3 << (2 * k)) for k in range(PLANES - 1)]
        masked.append((words >> 2).astype(jnp.int16) & jnp.int16(3 << (2 * PLANES - 4)))
    else:
        pair = jnp.concatenate([words & 255, words >> 8], 0)
        packed = pair.astype(jnp.int8)
        masked = [packed & jnp.int8(3 << (2 * k)) for k in range(PLANES // 2 - 1)]
        masked.append((pair >> 2).astype(jnp.int8) & jnp.int8(3 << (PLANES - 4)))
    return [piece.astype(bf16) for piece in masked]


def decode(words, order):
    blocks = []
    for first in range(0, words.shape[0], WORDS):
        blocks += pieces_of(words[first : first + WORDS], order)
    return jnp.concatenate(blocks, 0)


def row_correction(row_list, order):
    factor_row = plane_power(4.0, order) * 1.5
    total = None
    for rows in row_list:
        for first in range(0, rows.shape[1], HAD):
            term = rows[:, first : first + HAD].astype(f32)
            total = term if total is None else total + term
    return jnp.sum(total * factor_row, axis=1, keepdims=True)


def rotate_halves(values, doubled):
    high = values.astype(bf16)
    low = (values - high.astype(f32)).astype(bf16)
    return jnp.dot(jnp.concatenate([high, low], 1), doubled, preferred_element_type=f32)


def tile_width(columns):
    for width in (256, 128):
        if columns % width == 0:
            return width


def turn_kernel(place_ref, x_hbm, sign_hbm, own_ref, send_ref, x_ref, sign_ref, sems):
    copies = [
        pltpu.make_async_copy(x_hbm, x_ref, sems.at[0]),
        pltpu.make_async_copy(sign_hbm, sign_ref, sems.at[1]),
    ]
    for copy in copies:
        copy.start()
    matrix = hadamard(QKV_ORDER)
    factor = turn_factor(QKV_ORDER)
    for copy in copies:
        copy.wait()
    blocks = x_ref.shape[1] // HAD
    first = place_ref[0] * blocks
    for b in range(blocks):
        cols = slice(b * HAD, (b + 1) * HAD)
        sign_row = signed(sign_ref[pl.ds(first + b, 1), :])
        flipped = (x_ref[:, cols].astype(f32) * sign_row).astype(bf16)
        turned = jnp.dot(flipped, matrix, preferred_element_type=f32)
        turned = (turned * factor).astype(bf16)
        own_ref[:, cols] = turned
        send_ref[:, cols] = turned[: send_ref.shape[0]]


def turn(place, own_tokens, in_sign):
    sign_rows = in_sign.reshape(-1, HAD)
    rows, inner = own_tokens.shape
    return call(
        turn_kernel,
        (shape_of((rows, inner), bf16), shape_of((rows // 2, inner), bf16)),
        [SMEM, HBM, HBM],
        (place, in_hbm(own_tokens), in_hbm(sign_rows)),
        "turn",
        scratch_shapes=[
            pltpu.VMEM(own_tokens.shape, bf16),
            pltpu.VMEM(sign_rows.shape, jnp.int32),
            pltpu.SemaphoreType.DMA((2,)),
        ],
    )


def tie(array, *after):
    return call(
        lambda *refs: None,
        shape_of(array.shape, array.dtype),
        [ANY] * (1 + len(after)),
        (array, *after),
        "tie",
        out_specs=ANY,
        input_output_aliases={0: 0},
    )


def prepare_kernel(near, far, place_ref, *rest):
    shard_refs = rest[: len(near)]
    codes_hbm, sums_ref, far_ref, late_ref, near_ref, sems = rest[len(near) :]
    words, columns = near_ref.shape[2:]

    def fetch(position, kind):
        flip = (near + far)[position]
        first = pl.multiple_of((place_ref[0] ^ flip) * words, WORDS)
        there = position - len(near)
        target = near_ref.at[position, kind] if there < 0 else far_ref.at[there, kind]
        return pltpu.make_async_copy(
            codes_hbm.at[kind, pl.ds(first, words), :], target, sems.at[position, kind]
        )

    for kind in range(3):
        for position in range(len(near)):
            fetch(position, kind).start()
    for position in range(len(near), len(near + far)):
        for kind in range(3):
            fetch(position, kind).start()
    fix = row_correction([ref[...] for ref in shard_refs], QKV_ORDER)
    width = tile_width(columns)
    late_ref[...] = shard_refs[0][late_ref.shape[0] :, :]

    def product(kind, carry):
        for position in range(len(near)):
            fetch(position, kind).wait()
        for first in range(0, columns, width):
            cols = slice(first, first + width)
            total = -fix
            for position, ref in enumerate(shard_refs):
                weights = decode(near_ref[position, kind, :, cols], QKV_ORDER)
                total = total + jnp.dot(ref[...], weights, preferred_element_type=f32)
            sums_ref[kind, :, cols] = total
        return carry

    lax.fori_loop(0, 3, product, 0)
    for position in range(len(near), len(near + far)):
        for kind in range(3):
            fetch(position, kind).wait()


def prepare(place, near, far, shards, codes):
    rows, inner = shards[0].shape
    columns = codes.shape[2]
    words = inner // PLANES
    return call(
        functools.partial(prepare_kernel, near, far),
        (
            shape_of((3, rows, columns), f32),
            shape_of((len(far), 3, words, columns), jnp.int32),
            shape_of((rows // 2, inner), bf16),
        ),
        [SMEM] + [VMEM] * len(near) + [HBM],
        (place, *shards, in_hbm(codes)),
        "prepare",
        scratch_shapes=[
            pltpu.VMEM((len(near), 3, words, columns), jnp.int32),
            pltpu.SemaphoreType.DMA((len(near + far), 3)),
        ],
    )


def project_kernel(kinds, first_row, groups, positions, whole, ending, *rest):
    count = len(positions)
    shard_refs = rest[: groups * count]
    sums_ref, words_ref = rest[groups * count : groups * count + 2]
    if ending:
        scale_ref, sign_ref = rest[groups * count + 2 : groups * count + 4]
    out_ref = rest[-1]
    columns = sums_ref.shape[2]
    width = tile_width(columns)
    shards = []
    for place in range(count):
        parts = [shard_refs[g * count + place][...] for g in range(groups)]
        shards.append(parts[0] if groups == 1 else jnp.concatenate(parts, 0))
    fix = row_correction(shards, QKV_ORDER)
    row_count = shards[0].shape[0]
    rows = slice(first_row, first_row + row_count)
    doubled = double_hadamard()
    ones = jnp.ones((HD, HD), bf16)
    for place, kind in enumerate(kinds):
        heads = []
        for first in range(0, columns, width):
            cols = slice(first, first + width)
            part = (sums_ref[kind, rows, cols] if whole else sums_ref[place, :, cols]) - fix
            for shard, position in zip(shards, positions):
                weights = decode(words_ref[position, kind, :, cols], QKV_ORDER)
                part = part + jnp.dot(shard, weights, preferred_element_type=f32)
            if not ending:
                out_ref[place, :, cols] = part
                continue
            for lane in range(0, width, HD):
                at = slice(first + lane, first + lane + HD)
                scale_row = scale_ref[kind : kind + 1, at] * np.float32(D ** (-0.5))
                heads.append(part[:, lane : lane + HD] * scale_row)
        if not ending:
            continue
        mixed = rotate_halves(jnp.concatenate(heads, 0), doubled)
        signs = []
        for head in range(len(heads)):
            sign_row = sign_ref[kind : kind + 1, head * HD : (head + 1) * HD]
            sign_row = signed(sign_row) * np.float32(HAD ** (-0.5))
            signs.append(mixed[head * row_count : (head + 1) * row_count] * sign_row)
        if kind != 2:
            square = jnp.concatenate([(part * part).astype(bf16) for part in signs], 0)
            mean = jnp.dot(square, ones, preferred_element_type=f32) * (1.0 / HD)
            factor = lax.rsqrt(mean + epsilon)
            signs = [
                part * factor[head * row_count : (head + 1) * row_count]
                for head, part in enumerate(signs)
            ]
        for head, part in enumerate(signs):
            out_ref[place, :, head * HD : (head + 1) * HD] = part.astype(bf16)


def project(kinds, first_row, groups, positions, sums, words, ending, flops=1):
    inner = groups[0][0].shape[1]
    columns = sums.shape[2]
    row_count = sum(group[0].shape[0] for group in groups)
    whole = sums.shape[0] == 3
    args = [shard for group in groups for shard in group] + [sums, words]
    own_args = len(args) + 2
    if ending is not None:
        args += ending
    return call(
        functools.partial(
            project_kernel, kinds, first_row, len(groups), positions, whole, ending is not None
        ),
        shape_of((len(kinds), row_count, columns), f32 if ending is None else bf16),
        [VMEM] * min(len(args), own_args) + [ANY] * max(len(args) - own_args, 0),
        args,
        "project",
        flops=flops,
    )


def near_row(row, swap_pair):
    if swap_pair is None:
        return row
    by, odd = swap_pair
    return jnp.where(lax.rem(row // by, 2) == odd, row + by, row - by)


def window_mask(place_ref, windows_ref, segments, row_count):
    lane = lax.broadcasted_iota(jnp.int32, (1, sum(rows for _, _, rows in segments)), 1)
    ids, base = None, 0
    for swap_pair, first, rows in segments:
        tile = (lane + (first - base)) // TILE
        ids_here = near_row(place_ref[1], swap_pair) * WTILES + tile
        ids = ids_here if ids is None else jnp.where(lane >= base, ids_here, ids)
        base += rows
    masks = []
    for tile in range(row_count // TILE):
        hit = jnp.zeros(lane.shape, f32)
        for entry in range(windows_ref.shape[1]):
            hit = jnp.where(ids == windows_ref[tile, entry], 1.0, hit)
        masks.append(jnp.broadcast_to(hit, (TILE, lane.shape[1])))
    return jnp.concatenate(masks, 0)


def attend_kernel(
    segments, halves, blocks, has_sum, last, share_order, place_ref, windows_ref, *rest
):
    rest = list(rest)
    q_refs = [rest.pop(0) for _ in range(halves)]
    kv_refs = [rest.pop(0) for _ in range(blocks)]
    sum_ref = rest.pop(0) if has_sum else None
    if last:
        oin_ref, out_ref, rotated_ref = rest
    else:
        (out_ref,) = rest
    columns = q_refs[0].shape[2]
    row_count = sum(ref.shape[1] for ref in q_refs)
    heads = [slice(head, head + HD) for head in range(0, columns, HD)]
    mask = window_mask(place_ref, windows_ref, segments, row_count)
    scores = []
    for at in heads:
        keys = jnp.concatenate([ref[0, :, at] for ref in kv_refs], 0)
        scores.append(
            lax.dot_general(
                jnp.concatenate([ref[0, :, at] for ref in q_refs], 0),
                keys,
                (((1,), (1,)), ((), ())),
                preferred_element_type=f32,
            )
        )
    weights = [
        (jnp.exp(score * np.float32(HD ** (-0.5))) * mask).astype(bf16) for score in scores
    ]
    totals = []
    for head, at in enumerate(heads):
        values = jnp.concatenate([ref[1, :, at] for ref in kv_refs], 0)
        values = jnp.concatenate([values, jnp.ones_like(values)], 1)
        total = jnp.dot(weights[head], values, preferred_element_type=f32)
        if has_sum:
            total = total + sum_ref[head]
        totals.append(total)
    if not last:
        for head, total in enumerate(totals):
            out_ref[head] = total
        return
    matrix = hadamard(OUT_ORDER)
    factor = turn_factor(OUT_ORDER)
    for head, at in enumerate(heads):
        attended = (totals[head][:, :HD] / totals[head][:, HD:]).astype(bf16)
        sign_row = signed(oin_ref[head : head + 1, :])
        flipped = (attended.astype(f32) * sign_row).astype(bf16)
        rotated_ref[:, at] = jnp.dot(flipped, matrix, preferred_element_type=f32) * factor
    share = row_count // len(share_order)
    pieces = []
    for flip in share_order:
        owner = place_ref[0] ^ flip
        pieces.append(rotated_ref[pl.ds(pl.multiple_of(owner * share, 8), share), :])
    out_ref[...] = jnp.concatenate(pieces, 0).astype(bf16)


def attend(place, windows, queries, blocks, segments, running, ending):
    columns = queries[0].shape[2]
    row_count = sum(part.shape[1] for part in queries)
    args = [place, windows, *queries, *blocks]
    if running is not None:
        args.append(running)
    scratch, share_order = [], None
    if ending is None:
        out_shape = shape_of((columns // HD, row_count, 2 * HD), f32)
    else:
        oin_sign, share_order = ending
        args.append(oin_sign.reshape(-1, HAD))
        out_shape = shape_of((row_count, columns), bf16)
        scratch = [pltpu.VMEM((row_count, columns), f32)]
    return call(
        functools.partial(
            attend_kernel,
            segments,
            len(queries),
            len(blocks),
            running is not None,
            ending is not None,
            share_order,
        ),
        out_shape,
        [SMEM] * 2 + [VMEM] * (len(args) - 2),
        args,
        "attend",
        scratch_shapes=scratch,
    )


def unpack_out_kernel(codes_ref, after_ref, weights_ref):
    for first in range(0, codes_ref.shape[0], WORDS):

        def some(step, carry):
            cols = pl.ds(pl.multiple_of(step * 512, 512), 512)
            at = first * PLANES
            for piece in pieces_of(codes_ref[first : first + WORDS, cols], OUT_ORDER):
                weights_ref[at : at + piece.shape[0], cols] = piece
                at += piece.shape[0]
            return carry

        lax.fori_loop(0, codes_ref.shape[1] // 512, some, 0)


def unpack_out(codes, after):
    words, columns = codes.shape
    return call(
        unpack_out_kernel,
        shape_of((words * PLANES, columns), bf16),
        [VMEM, ANY],
        (codes, after),
        "unpack_out",
    )


def out_kernel(first, rotated_ref, weights_ref, scale_ref, send_ref, keep_ref):
    rows = rotated_ref[...]
    fix = row_correction([rows], OUT_ORDER)
    half, columns = send_ref.shape
    width = 256
    for at in range(0, columns, width):
        cols = slice(first + at, first + at + width)
        part = jnp.dot(rows, weights_ref[:, cols], preferred_element_type=f32) - fix
        for lane in range(0, width, HAD):
            place = (first + at + lane) // HAD
            scale_row = scale_ref[place : place + 1, :] * np.float32((HEADS * HD) ** (-0.5))
            done = (part[:, lane : lane + HAD] * scale_row).astype(bf16)
            send_ref[:, at + lane : at + lane + HAD] = done[:half]
            keep_ref[:, at + lane : at + lane + HAD] = done[half:]


def out_project(rotated, weights, scale_rows, first, columns):
    row_count, inner = rotated.shape
    result = shape_of((row_count // 2, columns), bf16)
    return call(
        functools.partial(out_kernel, first),
        (result, result),
        [VMEM] * 3,
        (rotated, weights, scale_rows),
        "out_project",
    )


def finish_kernel(first, has_base, sign_ref, keep_ref, more_ref, *rest):
    out_hbm, done_ref, sem = rest[1:] if has_base else rest
    columns = keep_ref.shape[1]
    doubled = double_hadamard()
    for at in range(0, columns, HAD):
        cols = slice(at, at + HAD)
        total = keep_ref[:, cols].astype(f32) + more_ref[:, cols].astype(f32)
        place = (first + at) // HAD
        sign_row = signed(sign_ref[place : place + 1, :]) * np.float32(HAD ** (-0.5))
        done_ref[:, cols] = (rotate_halves(total, doubled) * sign_row).astype(bf16)
    copy = pltpu.make_async_copy(done_ref, out_hbm.at[:, pl.ds(first, columns)], sem)
    copy.start()
    copy.wait()


def finish(base, sign_rows, keep, more, first):
    share, columns = keep.shape
    args = [sign_rows, keep, more]
    in_specs = [VMEM] * 3
    aliases = {}
    if base is not None:
        args.append(base)
        in_specs.append(ANY)
        aliases = {3: 0}
    return call(
        functools.partial(finish_kernel, first, base is not None),
        shape_of((share, D), bf16),
        in_specs,
        args,
        "finish",
        out_specs=ANY,
        scratch_shapes=[pltpu.VMEM((share, columns), bf16), pltpu.SemaphoreType.DMA],
        input_output_aliases=aliases,
    )


def swap(shard, bit):
    peers = lax.axis_size("head")
    return lax.ppermute(shard, "head", [(i, i ^ bit) for i in range(peers)])


def row_swaps(row_tiles):
    swaps = []
    for by in (1, 3, 4, 5) if row_tiles > HROWS else (1,):
        for odd in (0, 1):
            low = [i for i in range(row_tiles - by) if (i // by) % 2 == odd]
            swaps.append((by, odd, [(i, i + by) for i in low] + [(i + by, i) for i in low]))
    return swaps


def halving_order(head_count):
    flips = [0]
    bit = head_count // 2
    while bit >= 1:
        flips = [f | bit for f in flips] + flips
        bit //= 2
    return tuple(flips)


CHUNKS = (2048, 1792, 1280)


def on_device(
    tokens,
    in_sign,
    qkv_codes,
    qkv_scale,
    qkv_sign,
    windows,
    oin_sign,
    out_codes,
    out_scale,
    out_sign,
):
    head_count = lax.axis_size("head")
    row_tiles = lax.axis_size("height")
    row_place = lax.axis_index("height")
    head_place = lax.axis_index("head").astype(jnp.int32)
    top = head_count // 2
    place = jnp.stack([head_place, row_place.astype(jnp.int32)])
    low_bits = [1 << b for b in range(top.bit_length() - 1)]

    own, early = turn(place, tokens[0], in_sign)
    half_rows = early.shape[0]
    early = swap(early, top)
    near = {0: own}
    for bit in low_bits:
        for flip in list(near):
            near[flip ^ bit] = swap(near[flip], bit)
    codes = jnp.transpose(qkv_codes, (1, 0, 2))
    near_flips = tuple(sorted(near))
    far_flips = tuple(flip ^ top for flip in near_flips)
    sums, words, late = prepare(
        place, near_flips, far_flips, [near[flip] for flip in near_flips], codes
    )
    late = swap(late, top)
    swaps = row_swaps(row_tiles)
    ending = [qkv_scale, qkv_sign]
    every = tuple(range(len(far_flips)))
    key_values, moved, queries = [], [], []
    for half, first_row in ((early, 0), (late, half_rows)):
        shards = {top: tie(half, *queries, sums)}
        for bit in low_bits:
            for flip in list(shards):
                shards[flip ^ bit] = swap(shards[flip], bit)
        shards = [shards[flip] for flip in far_flips]
        partial = project((1, 2), first_row, [shards[:-1]], every[:-1], sums, words, None, 4 * 10**9)
        key_value = project((1, 2), 0, [shards[-1:]], every[-1:], partial, words, ending)
        moved.append([lax.ppermute(key_value, "height", pairs) for _, _, pairs in swaps])
        key_values.append(key_value)
        queries.append(
            project((0,), first_row, [shards], every, sums, words, ending + [key_value], 4 * 10**9)
        )
    out_weights = unpack_out(out_codes, key_values[1])

    listed = windows[0]
    own_rows = ((None, 0, half_rows), (None, half_rows, half_rows))
    early_rows = tuple(((by, odd), 0, half_rows) for by, odd, _ in swaps)
    late_rows = tuple(((by, odd), half_rows, half_rows) for by, odd, _ in swaps)
    running = attend(place, listed, queries, key_values, own_rows, None, None)
    running = attend(place, listed, queries, moved[0], early_rows, running, None)
    rotated = attend(
        place,
        listed,
        queries,
        moved[1],
        late_rows,
        running,
        (oin_sign, halving_order(head_count)),
    )

    bits = low_bits + [top]
    scale_rows = out_scale.reshape(-1, HAD)
    sign_rows = out_sign.reshape(-1, HAD)
    result = None
    first = 0
    for columns in CHUNKS:
        part, keep = out_project(rotated, out_weights, scale_rows, first, columns)
        for bit in bits:
            more = swap(part, bit)
            if bit == top:
                break
            total = keep.astype(f32) + more.astype(f32)
            half = total.shape[0] // 2
            part, keep = total[:half].astype(bf16), total[half:]
        result = finish(result, sign_rows, keep, more, first)
        first += columns
    return result[None]


def solution(mesh):
    return jax.shard_map(
        on_device,
        mesh=mesh,
        in_specs=(
            P(("clip", "height"), None, "head"),
            P(),
            P(None, None, "head"),
            P(None, "head"),
            P(None, "head"),
            P(("clip", "height"), None, None),
            P("head"),
            P("head", None),
            P(),
            P(),
        ),
        out_specs=P(("clip", "height"), "head", None),
        check_vma=False,
    )
```

```python
import functools

import jax
import jax.numpy as jnp
import numpy as np
from jax import lax
from jax.experimental import pallas as pl
from jax.experimental.pallas import tpu as pltpu
from jax.sharding import PartitionSpec as P

D = 5120
HD = 128
HEADS = 24
HAD = 128
TILE = 64
HROWS = 4
WTILES = 3
PLANES = 8
WORDS = HAD // PLANES
QKV_ORDER = "half"
OUT_ORDER = "byte"

epsilon = 1e-06
f32 = jnp.float32
bf16 = jnp.bfloat16
VMEM = pl.BlockSpec(memory_space=pltpu.VMEM)
SMEM = pl.BlockSpec(memory_space=pltpu.SMEM)
ANY = pl.BlockSpec(memory_space=pl.ANY)
HBM = pl.BlockSpec(memory_space=pltpu.HBM)


def shape_of(shape, dtype):
    return jax.ShapeDtypeStruct(tuple(shape), dtype)


def in_hbm(array):
    return pltpu.with_memory_space_constraint(array, pltpu.HBM)


def call(body, out_shape, in_specs, args, name, out_specs=None, megabytes=16, flops=1, **more):
    if out_specs is None:
        out_specs = jax.tree.map(lambda _: VMEM, out_shape)
    return pl.pallas_call(
        body,
        out_shape=out_shape,
        in_specs=in_specs,
        out_specs=out_specs,
        compiler_params=pltpu.CompilerParams(vmem_limit_bytes=megabytes * 2**20),
        cost_estimate=pl.CostEstimate(flops=flops, bytes_accessed=1, transcendentals=0),
        name=name,
        **more,
    )(*args)


def lanes():
    return lax.broadcasted_iota(jnp.int32, (HAD, HAD), 1)


def hadamard(order):
    row = lax.broadcasted_iota(jnp.int32, (HAD, HAD), 0)
    column = lanes()
    word = PLANES * (column & (WORDS - 1))
    if order == "half":
        column = word + column // WORDS
    if order == "byte":
        column = word + column // (2 * WORDS) + (PLANES // 2) * ((column // WORDS) & 1)
    shared = row & column
    shared = shared ^ (shared >> 4)
    shared = shared ^ (shared >> 2)
    shared = shared ^ (shared >> 1)
    return (1 - 2 * (shared & 1)).astype(f32).astype(bf16)


def double_hadamard():
    plain = hadamard("plain")
    return jnp.concatenate([plain, plain], 0)


def plane_power(base, order):
    lane = lax.broadcasted_iota(jnp.int32, (1, HAD), 1)
    if order == "half":
        power = jnp.minimum(lane // WORDS, PLANES - 2)
    else:
        power = jnp.minimum(lane // (2 * WORDS), PLANES // 2 - 2)
    value = jnp.where(power & 1 == 1, base, 1.0)
    value = value * jnp.where(power & 2 == 2, base**2, 1.0)
    return value * jnp.where(power & 4 == 4, base**4, 1.0)


def turn_factor(order):
    return plane_power(0.25, order) * np.float32(HAD ** (-0.5))


def signed(sign_bits):
    return (2 * sign_bits - 1).astype(f32)


def pieces_of(words, order):
    if order == "half":
        packed = words.astype(jnp.int16)
        masked = [packed & jnp.int16(3 << (2 * k)) for k in range(PLANES - 1)]
        masked.append((words >> 2).astype(jnp.int16) & jnp.int16(3 << (2 * PLANES - 4)))
    else:
        pair = jnp.concatenate([words & 255, words >> 8], 0)
        packed = pair.astype(jnp.int8)
        masked = [packed & jnp.int8(3 << (2 * k)) for k in range(PLANES // 2 - 1)]
        masked.append((pair >> 2).astype(jnp.int8) & jnp.int8(3 << (PLANES - 4)))
    return [piece.astype(bf16) for piece in masked]


def decode(words, order):
    blocks = []
    for first in range(0, words.shape[0], WORDS):
        blocks += pieces_of(words[first : first + WORDS], order)
    return jnp.concatenate(blocks, 0)


def row_correction(row_list, order):
    factor_row = plane_power(4.0, order) * 1.5
    total = None
    for rows in row_list:
        for first in range(0, rows.shape[1], HAD):
            term = rows[:, first : first + HAD].astype(f32)
            total = term if total is None else total + term
    return jnp.sum(total * factor_row, axis=1, keepdims=True)


def rotate_halves(values, doubled):
    high = values.astype(bf16)
    low = (values - high.astype(f32)).astype(bf16)
    return jnp.dot(jnp.concatenate([high, low], 1), doubled, preferred_element_type=f32)


def tile_width(columns):
    for width in (256, 128):
        if columns % width == 0:
            return width


def turn_kernel(place_ref, x_hbm, sign_hbm, own_ref, send_ref, x_ref, sign_ref, sems):
    copies = [
        pltpu.make_async_copy(x_hbm, x_ref, sems.at[0]),
        pltpu.make_async_copy(sign_hbm, sign_ref, sems.at[1]),
    ]
    for copy in copies:
        copy.start()
    matrix = hadamard(QKV_ORDER)
    factor = turn_factor(QKV_ORDER)
    for copy in copies:
        copy.wait()
    blocks = x_ref.shape[1] // HAD
    first = place_ref[0] * blocks
    for b in range(blocks):
        cols = slice(b * HAD, (b + 1) * HAD)
        sign_row = signed(sign_ref[pl.ds(first + b, 1), :])
        flipped = (x_ref[:, cols].astype(f32) * sign_row).astype(bf16)
        turned = jnp.dot(flipped, matrix, preferred_element_type=f32)
        turned = (turned * factor).astype(bf16)
        own_ref[:, cols] = turned
        send_ref[:, cols] = turned[: send_ref.shape[0]]


def turn(place, own_tokens, in_sign):
    sign_rows = in_sign.reshape(-1, HAD)
    rows, inner = own_tokens.shape
    return call(
        turn_kernel,
        (shape_of((rows, inner), bf16), shape_of((rows // 2, inner), bf16)),
        [SMEM, HBM, HBM],
        (place, in_hbm(own_tokens), in_hbm(sign_rows)),
        "turn",
        scratch_shapes=[
            pltpu.VMEM(own_tokens.shape, bf16),
            pltpu.VMEM(sign_rows.shape, jnp.int32),
            pltpu.SemaphoreType.DMA((2,)),
        ],
    )


def tie(array, *after):
    return call(
        lambda *refs: None,
        shape_of(array.shape, array.dtype),
        [ANY] * (1 + len(after)),
        (array, *after),
        "tie",
        out_specs=ANY,
        input_output_aliases={0: 0},
    )


def gate(array):
    def body(array_ref, out_ref):
        out_ref[...] = jnp.zeros_like(out_ref)

    return call(body, shape_of((8, HAD), f32), [ANY], (array,), "gate", flops=4 * 10**9)


def prepare_kernel(near, far, place_ref, *rest):
    shard_refs = rest[: len(near)]
    codes_hbm, sums_ref, far_ref, late_ref, near_ref, sems = rest[len(near) :]
    words, columns = near_ref.shape[2:]

    def fetch(position, kind):
        flip = (near + far)[position]
        first = pl.multiple_of((place_ref[0] ^ flip) * words, WORDS)
        there = position - len(near)
        target = near_ref.at[position, kind] if there < 0 else far_ref.at[there, kind]
        return pltpu.make_async_copy(
            codes_hbm.at[kind, pl.ds(first, words), :], target, sems.at[position, kind]
        )

    for kind in range(3):
        for position in range(len(near)):
            fetch(position, kind).start()
    for position in range(len(near), len(near + far)):
        for kind in range(3):
            fetch(position, kind).start()
    fix = row_correction([ref[...] for ref in shard_refs], QKV_ORDER)
    width = tile_width(columns)
    late_ref[...] = shard_refs[0][late_ref.shape[0] :, :]

    def product(kind, carry):
        for position in range(len(near)):
            fetch(position, kind).wait()
        for first in range(0, columns, width):
            cols = slice(first, first + width)
            total = -fix
            for position, ref in enumerate(shard_refs):
                weights = decode(near_ref[position, kind, :, cols], QKV_ORDER)
                total = total + jnp.dot(ref[...], weights, preferred_element_type=f32)
            sums_ref[kind, :, cols] = total
        return carry

    lax.fori_loop(0, 3, product, 0)
    for position in range(len(near), len(near + far)):
        for kind in range(3):
            fetch(position, kind).wait()


def prepare(place, near, far, shards, codes):
    rows, inner = shards[0].shape
    columns = codes.shape[2]
    words = inner // PLANES
    return call(
        functools.partial(prepare_kernel, near, far),
        (
            shape_of((3, rows, columns), f32),
            shape_of((len(far), 3, words, columns), jnp.int32),
            shape_of((rows // 2, inner), bf16),
        ),
        [SMEM] + [VMEM] * len(near) + [HBM],
        (place, *shards, in_hbm(codes)),
        "prepare",
        scratch_shapes=[
            pltpu.VMEM((len(near), 3, words, columns), jnp.int32),
            pltpu.SemaphoreType.DMA((len(near + far), 3)),
        ],
    )


def project_kernel(kinds, first_row, groups, positions, whole, ending, *rest):
    count = len(positions)
    shard_refs = rest[: groups * count]
    sums_ref, words_ref = rest[groups * count : groups * count + 2]
    if ending:
        scale_ref, sign_ref = rest[groups * count + 2 : groups * count + 4]
    out_ref = rest[-1]
    columns = sums_ref.shape[2]
    width = tile_width(columns)
    shards = []
    for place in range(count):
        parts = [shard_refs[g * count + place][...] for g in range(groups)]
        shards.append(parts[0] if groups == 1 else jnp.concatenate(parts, 0))
    fix = row_correction(shards, QKV_ORDER)
    row_count = shards[0].shape[0]
    rows = slice(first_row, first_row + row_count)
    doubled = double_hadamard()
    ones = jnp.ones((HD, HD), bf16)
    for place, kind in enumerate(kinds):
        heads = []
        for first in range(0, columns, width):
            cols = slice(first, first + width)
            part = (sums_ref[kind, rows, cols] if whole else sums_ref[place, :, cols]) - fix
            for shard, position in zip(shards, positions):
                weights = decode(words_ref[position, kind, :, cols], QKV_ORDER)
                part = part + jnp.dot(shard, weights, preferred_element_type=f32)
            if not ending:
                out_ref[place, :, cols] = part
                continue
            for lane in range(0, width, HD):
                at = slice(first + lane, first + lane + HD)
                scale_row = scale_ref[kind : kind + 1, at] * np.float32(D ** (-0.5))
                heads.append(part[:, lane : lane + HD] * scale_row)
        if not ending:
            continue
        mixed = rotate_halves(jnp.concatenate(heads, 0), doubled)
        signs = []
        for head in range(len(heads)):
            sign_row = sign_ref[kind : kind + 1, head * HD : (head + 1) * HD]
            sign_row = signed(sign_row) * np.float32(HAD ** (-0.5))
            signs.append(mixed[head * row_count : (head + 1) * row_count] * sign_row)
        if kind != 2:
            square = jnp.concatenate([(part * part).astype(bf16) for part in signs], 0)
            mean = jnp.dot(square, ones, preferred_element_type=f32) * (1.0 / HD)
            factor = lax.rsqrt(mean + epsilon)
            signs = [
                part * factor[head * row_count : (head + 1) * row_count]
                for head, part in enumerate(signs)
            ]
        for head, part in enumerate(signs):
            out_ref[place, :, head * HD : (head + 1) * HD] = part.astype(bf16)


def project(kinds, first_row, groups, positions, sums, words, ending, flops=1):
    inner = groups[0][0].shape[1]
    columns = sums.shape[2]
    row_count = sum(group[0].shape[0] for group in groups)
    whole = sums.shape[0] == 3
    args = [shard for group in groups for shard in group] + [sums, words]
    own_args = len(args) + 2
    if ending is not None:
        args += ending
    return call(
        functools.partial(
            project_kernel, kinds, first_row, len(groups), positions, whole, ending is not None
        ),
        shape_of((len(kinds), row_count, columns), f32 if ending is None else bf16),
        [VMEM] * min(len(args), own_args) + [ANY] * max(len(args) - own_args, 0),
        args,
        "project",
        flops=flops,
    )


def near_row(row, swap_pair):
    if swap_pair is None:
        return row
    by, odd = swap_pair
    return jnp.where(lax.rem(row // by, 2) == odd, row + by, row - by)


def window_mask(place_ref, windows_ref, segments, row_count):
    lane = lax.broadcasted_iota(jnp.int32, (1, sum(rows for _, _, rows in segments)), 1)
    ids, base = None, 0
    for swap_pair, first, rows in segments:
        tile = (lane + (first - base)) // TILE
        ids_here = near_row(place_ref[1], swap_pair) * WTILES + tile
        ids = ids_here if ids is None else jnp.where(lane >= base, ids_here, ids)
        base += rows
    masks = []
    for tile in range(row_count // TILE):
        hit = jnp.zeros(lane.shape, f32)
        for entry in range(windows_ref.shape[2]):
            hit = jnp.where(ids == windows_ref[tile, 0, entry], 1.0, hit)
        masks.append(jnp.broadcast_to(hit, (TILE, lane.shape[1])))
    return jnp.concatenate(masks, 0)


def attend_kernel(
    segments, halves, blocks, has_sum, last, share_order, place_ref, windows_ref, *rest
):
    rest = list(rest)
    q_refs = [rest.pop(0) for _ in range(halves)]
    kv_refs = [rest.pop(0) for _ in range(blocks)]
    sum_ref = rest.pop(0) if has_sum else None
    if last:
        oin_ref, out_ref, rotated_ref = rest
    else:
        (out_ref,) = rest
    columns = q_refs[0].shape[2]
    row_count = sum(ref.shape[1] for ref in q_refs)
    heads = [slice(head, head + HD) for head in range(0, columns, HD)]
    mask = window_mask(place_ref, windows_ref, segments, row_count)
    scores = []
    for at in heads:
        keys = jnp.concatenate([ref[0, :, at] for ref in kv_refs], 0)
        scores.append(
            lax.dot_general(
                jnp.concatenate([ref[0, :, at] for ref in q_refs], 0),
                keys,
                (((1,), (1,)), ((), ())),
                preferred_element_type=f32,
            )
        )
    weights = [
        (jnp.exp(score * np.float32(HD ** (-0.5))) * mask).astype(bf16) for score in scores
    ]
    totals = []
    for head, at in enumerate(heads):
        values = jnp.concatenate([ref[1, :, at] for ref in kv_refs], 0)
        values = jnp.concatenate([values, jnp.ones_like(values)], 1)
        total = jnp.dot(weights[head], values, preferred_element_type=f32)
        if has_sum:
            total = total + sum_ref[head]
        totals.append(total)
    if not last:
        for head, total in enumerate(totals):
            out_ref[head] = total
        return
    matrix = hadamard(OUT_ORDER)
    factor = turn_factor(OUT_ORDER)
    for head, at in enumerate(heads):
        attended = (totals[head][:, :HD] / totals[head][:, HD:]).astype(bf16)
        sign_row = signed(oin_ref[head : head + 1, :])
        flipped = (attended.astype(f32) * sign_row).astype(bf16)
        rotated_ref[:, at] = jnp.dot(flipped, matrix, preferred_element_type=f32) * factor
    share = row_count // len(share_order)
    pieces = []
    for flip in share_order:
        owner = place_ref[0] ^ flip
        pieces.append(rotated_ref[pl.ds(pl.multiple_of(owner * share, 8), share), :])
    out_ref[...] = jnp.concatenate(pieces, 0).astype(bf16)


def attend(place, windows, queries, blocks, segments, running, ending):
    columns = queries[0].shape[2]
    row_count = sum(part.shape[1] for part in queries)
    args = [place, windows, *queries, *blocks]
    if running is not None:
        args.append(running)
    scratch, share_order = [], None
    if ending is None:
        out_shape = shape_of((columns // HD, row_count, 2 * HD), f32)
    else:
        oin_sign, share_order = ending
        args.append(oin_sign.reshape(-1, HAD))
        out_shape = shape_of((row_count, columns), bf16)
        scratch = [pltpu.VMEM((row_count, columns), f32)]
    return call(
        functools.partial(
            attend_kernel,
            segments,
            len(queries),
            len(blocks),
            running is not None,
            ending is not None,
            share_order,
        ),
        out_shape,
        [SMEM] * 2 + [VMEM] * (len(args) - 2),
        args,
        "attend",
        scratch_shapes=scratch,
    )


def unpack_out_kernel(codes_ref, after_ref, weights_ref):
    for first in range(0, codes_ref.shape[0], WORDS):

        def some(step, carry):
            cols = pl.ds(pl.multiple_of(step * 512, 512), 512)
            at = first * PLANES
            for piece in pieces_of(codes_ref[first : first + WORDS, cols], OUT_ORDER):
                weights_ref[at : at + piece.shape[0], cols] = piece
                at += piece.shape[0]
            return carry

        lax.fori_loop(0, codes_ref.shape[1] // 512, some, 0)


def unpack_out(codes, after):
    words, columns = codes.shape
    return call(
        unpack_out_kernel,
        shape_of((words * PLANES, columns), bf16),
        [VMEM, ANY],
        (codes, after),
        "unpack_out",
    )


def out_kernel(first, rotated_ref, weights_ref, scale_ref, send_ref, keep_ref):
    rows = rotated_ref[...]
    fix = row_correction([rows], OUT_ORDER)
    half, columns = send_ref.shape
    width = 256
    for at in range(0, columns, width):
        cols = slice(first + at, first + at + width)
        part = jnp.dot(rows, weights_ref[:, cols], preferred_element_type=f32) - fix
        for lane in range(0, width, HAD):
            place = (first + at + lane) // HAD
            scale_row = scale_ref[place : place + 1, :] * np.float32((HEADS * HD) ** (-0.5))
            done = (part[:, lane : lane + HAD] * scale_row).astype(bf16)
            send_ref[:, at + lane : at + lane + HAD] = done[:half]
            keep_ref[:, at + lane : at + lane + HAD] = done[half:]


def out_project(rotated, weights, scale_rows, first, columns):
    row_count, inner = rotated.shape
    result = shape_of((row_count // 2, columns), bf16)
    return call(
        functools.partial(out_kernel, first),
        (result, result),
        [VMEM] * 3,
        (rotated, weights, scale_rows),
        "out_project",
    )


def finish_kernel(chunks, sign_ref, *rest):
    out_hbm, done_ref, sems = rest[2 * chunks :]
    doubled = double_hadamard()
    first, copies = 0, []
    for chunk in range(chunks):
        keep_ref, more_ref = rest[2 * chunk : 2 * chunk + 2]
        share, columns = keep_ref.shape
        totals = keep_ref[...].astype(f32) + more_ref[...].astype(f32)
        blocks = [totals[:, at : at + HAD] for at in range(0, columns, HAD)]
        turned = rotate_halves(jnp.concatenate(blocks, 0), doubled)
        for block in range(len(blocks)):
            place = first // HAD + block
            sign_row = signed(sign_ref[place : place + 1, :]) * np.float32(HAD ** (-0.5))
            done = turned[block * share : (block + 1) * share] * sign_row
            done_ref[:, place * HAD : (place + 1) * HAD] = done.astype(bf16)
        cols = pl.ds(first, columns)
        copies.append(
            pltpu.make_async_copy(done_ref.at[:, cols], out_hbm.at[:, cols], sems.at[chunk])
        )
        copies[-1].start()
        first += columns
    for copy in copies:
        copy.wait()


def finish(pairs, sign_rows):
    share = pairs[0][0].shape[0]
    args = [sign_rows] + [array for pair in pairs for array in pair]
    return call(
        functools.partial(finish_kernel, len(pairs)),
        shape_of((share, D), bf16),
        [VMEM] * len(args),
        args,
        "finish",
        out_specs=HBM,
        scratch_shapes=[pltpu.VMEM((share, D), bf16), pltpu.SemaphoreType.DMA((len(pairs),))],
    )


def swap(shard, bit):
    peers = lax.axis_size("head")
    return lax.ppermute(shard, "head", [(i, i ^ bit) for i in range(peers)])


def row_swaps(row_tiles):
    swaps = []
    for by in (1, 3, 4, 5) if row_tiles > HROWS else (1,):
        for odd in (0, 1):
            low = [i for i in range(row_tiles - by) if (i // by) % 2 == odd]
            swaps.append((by, odd, [(i, i + by) for i in low] + [(i + by, i) for i in low]))
    return swaps


def halving_order(head_count):
    flips = [0]
    bit = head_count // 2
    while bit >= 1:
        flips = [f | bit for f in flips] + flips
        bit //= 2
    return tuple(flips)


CHUNKS = (2560, 2560)


def on_device(
    tokens,
    in_sign,
    qkv_codes,
    qkv_scale,
    qkv_sign,
    windows,
    oin_sign,
    out_codes,
    out_scale,
    out_sign,
):
    head_count = lax.axis_size("head")
    row_tiles = lax.axis_size("height")
    row_place = lax.axis_index("height")
    head_place = lax.axis_index("head").astype(jnp.int32)
    top = head_count // 2
    place = jnp.stack([head_place, row_place.astype(jnp.int32)])
    low_bits = [1 << b for b in range(top.bit_length() - 1)]

    own, early = turn(place, tokens[0], in_sign)
    half_rows = early.shape[0]
    early = swap(early, top)
    near = {0: own}
    for bit in low_bits:
        for flip in list(near):
            near[flip ^ bit] = swap(near[flip], bit)
    codes = jnp.transpose(qkv_codes, (1, 0, 2))
    near_flips = tuple(sorted(near))
    far_flips = tuple(flip ^ top for flip in near_flips)
    sums, words, late = prepare(
        place, near_flips, far_flips, [near[flip] for flip in near_flips], codes
    )
    late = swap(late, top)
    swaps = row_swaps(row_tiles)
    ending = [qkv_scale, qkv_sign]
    every = tuple(range(len(far_flips)))
    halves, key_values, moved, gates = [], [], [], []
    for half, first_row in ((early, 0), (late, half_rows)):
        shards = {top: tie(half, *gates, sums)}
        for bit in low_bits:
            for flip in list(shards):
                shards[flip ^ bit] = swap(shards[flip], bit)
        shards = [shards[flip] for flip in far_flips]
        partial = project(
            (1, 2), first_row, [shards[:-1]], every[:-1], sums, words, None, 4 * 10**9
        )
        key_value = project((1, 2), 0, [shards[-1:]], every[-1:], partial, words, ending)
        moved.append([lax.ppermute(key_value, "height", pairs) for _, _, pairs in swaps])
        halves.append(shards)
        key_values.append(key_value)
        gates.append(gate(key_value))
    queries = [project((0,), 0, halves, every, sums, words, ending, 4 * 10**9)]
    out_weights = unpack_out(out_codes, key_values[1])

    listed = jnp.transpose(windows, (1, 0, 2))
    own_rows = ((None, 0, half_rows), (None, half_rows, half_rows))
    early_rows = tuple(((by, odd), 0, half_rows) for by, odd, _ in swaps)
    late_rows = tuple(((by, odd), half_rows, half_rows) for by, odd, _ in swaps)
    running = attend(place, listed, queries, key_values, own_rows, None, None)
    running = attend(place, listed, queries, moved[0], early_rows, running, None)
    rotated = attend(
        place,
        listed,
        queries,
        moved[1],
        late_rows,
        running,
        (oin_sign, halving_order(head_count)),
    )

    bits = low_bits + [top]
    scale_rows = out_scale.reshape(-1, HAD)
    sign_rows = out_sign.reshape(-1, HAD)
    pairs, sums_sent = [], []
    first = 0
    for columns in CHUNKS:
        part, keep = out_project(rotated, out_weights, scale_rows, first, columns)
        if sums_sent:
            part = tie(part, sums_sent[-1])
        for bit in bits:
            more = swap(part, bit)
            if bit == top:
                break
            total = keep.astype(f32) + more.astype(f32)
            half = total.shape[0] // 2
            part, keep = total[:half].astype(bf16), total[half:]
            sums_sent.append(part)
        pairs.append((keep, more))
        first += columns
    return finish(pairs, sign_rows)[None]


def solution(mesh):
    return jax.shard_map(
        on_device,
        mesh=mesh,
        in_specs=(
            P(("clip", "height"), None, "head"),
            P(),
            P(None, None, "head"),
            P(None, "head"),
            P(None, "head"),
            P(("clip", "height"), None, None),
            P("head"),
            P("head", None),
            P(),
            P(),
        ),
        out_specs=P(("clip", "height"), "head", None),
        check_vma=False,
    )
```

```python
import functools

import jax
import jax.numpy as jnp
import numpy as np
from jax import lax
from jax.experimental import pallas as pl
from jax.experimental.pallas import tpu as pltpu
from jax.sharding import PartitionSpec as P

D = 5120
HD = 128
HEADS = 24
HAD = 128
TILE = 64
HROWS = 4
WTILES = 3
PLANES = 8
WORDS = HAD // PLANES
QKV_ORDER = "half"
OUT_ORDER = "byte"

epsilon = 1e-06
f32 = jnp.float32
bf16 = jnp.bfloat16
VMEM = pl.BlockSpec(memory_space=pltpu.VMEM)
SMEM = pl.BlockSpec(memory_space=pltpu.SMEM)
ANY = pl.BlockSpec(memory_space=pl.ANY)
HBM = pl.BlockSpec(memory_space=pltpu.HBM)


def shape_of(shape, dtype):
    return jax.ShapeDtypeStruct(tuple(shape), dtype)


def in_hbm(array):
    return pltpu.with_memory_space_constraint(array, pltpu.HBM)


def call(body, out_shape, in_specs, args, name, out_specs=None, megabytes=16, flops=1, **more):
    if out_specs is None:
        out_specs = jax.tree.map(lambda _: VMEM, out_shape)
    return pl.pallas_call(
        body,
        out_shape=out_shape,
        in_specs=in_specs,
        out_specs=out_specs,
        compiler_params=pltpu.CompilerParams(vmem_limit_bytes=megabytes * 2**20),
        cost_estimate=pl.CostEstimate(flops=flops, bytes_accessed=1, transcendentals=0),
        name=name,
        **more,
    )(*args)


def lanes():
    return lax.broadcasted_iota(jnp.int32, (HAD, HAD), 1)


def hadamard(order):
    row = lax.broadcasted_iota(jnp.int32, (HAD, HAD), 0)
    column = lanes()
    word = PLANES * (column & (WORDS - 1))
    if order == "half":
        column = word + column // WORDS
    if order == "byte":
        column = word + column // (2 * WORDS) + (PLANES // 2) * ((column // WORDS) & 1)
    shared = row & column
    shared = shared ^ (shared >> 4)
    shared = shared ^ (shared >> 2)
    shared = shared ^ (shared >> 1)
    return (1 - 2 * (shared & 1)).astype(f32).astype(bf16)


def double_hadamard():
    plain = hadamard("plain")
    return jnp.concatenate([plain, plain], 0)


def plane_power(base, order):
    lane = lax.broadcasted_iota(jnp.int32, (1, HAD), 1)
    if order == "half":
        power = jnp.minimum(lane // WORDS, PLANES - 2)
    else:
        power = jnp.minimum(lane // (2 * WORDS), PLANES // 2 - 2)
    value = jnp.where(power & 1 == 1, base, 1.0)
    value = value * jnp.where(power & 2 == 2, base**2, 1.0)
    return value * jnp.where(power & 4 == 4, base**4, 1.0)


def turn_factor(order):
    return plane_power(0.25, order) * np.float32(HAD ** (-0.5))


def signed(sign_bits):
    return (2 * sign_bits - 1).astype(f32)


def pieces_of(words, order):
    if order == "half":
        packed = words.astype(jnp.int16)
        masked = [packed & jnp.int16(3 << (2 * k)) for k in range(PLANES - 1)]
        masked.append((words >> 2).astype(jnp.int16) & jnp.int16(3 << (2 * PLANES - 4)))
    else:
        pair = jnp.concatenate([words & 255, words >> 8], 0)
        packed = pair.astype(jnp.int8)
        masked = [packed & jnp.int8(3 << (2 * k)) for k in range(PLANES // 2 - 1)]
        masked.append((pair >> 2).astype(jnp.int8) & jnp.int8(3 << (PLANES - 4)))
    return [piece.astype(bf16) for piece in masked]


def decode(words, order):
    blocks = []
    for first in range(0, words.shape[0], WORDS):
        blocks += pieces_of(words[first : first + WORDS], order)
    return jnp.concatenate(blocks, 0)


def product(rows, words_ref, at, cols, order, total):
    words = rows.shape[1] // PLANES
    step = 2 * WORDS if words % (2 * WORDS) == 0 else WORDS
    for first in range(0, words, step):
        weights = decode(words_ref[(*at, slice(first, first + step), cols)], order)
        part = rows[:, first * PLANES : (first + step) * PLANES]
        total = total + jnp.dot(part, weights, preferred_element_type=f32)
    return total


def row_correction(row_list, order):
    factor_row = plane_power(4.0, order) * 1.5
    total = None
    for rows in row_list:
        for first in range(0, rows.shape[1], HAD):
            term = rows[:, first : first + HAD].astype(f32)
            total = term if total is None else total + term
    return jnp.sum(total * factor_row, axis=1, keepdims=True)


def rotate_halves(values, doubled):
    high = values.astype(bf16)
    low = (values - high.astype(f32)).astype(bf16)
    return jnp.dot(jnp.concatenate([high, low], 1), doubled, preferred_element_type=f32)


def tile_width(columns):
    for width in (256, 128):
        if columns % width == 0:
            return width


def turn_kernel(place_ref, x_hbm, sign_hbm, own_ref, send_ref, x_ref, sign_ref, sems):
    copies = [
        pltpu.make_async_copy(x_hbm, x_ref, sems.at[0]),
        pltpu.make_async_copy(sign_hbm, sign_ref, sems.at[1]),
    ]
    for copy in copies:
        copy.start()
    matrix = hadamard(QKV_ORDER)
    factor = turn_factor(QKV_ORDER)
    for copy in copies:
        copy.wait()
    blocks = x_ref.shape[1] // HAD
    first = place_ref[0] * blocks
    for b in range(blocks):
        cols = slice(b * HAD, (b + 1) * HAD)
        sign_row = signed(sign_ref[pl.ds(first + b, 1), :])
        flipped = (x_ref[:, cols].astype(f32) * sign_row).astype(bf16)
        turned = jnp.dot(flipped, matrix, preferred_element_type=f32)
        turned = (turned * factor).astype(bf16)
        own_ref[:, cols] = turned
        send_ref[:, cols] = turned[: send_ref.shape[0]]


def turn(place, own_tokens, in_sign):
    sign_rows = in_sign.reshape(-1, HAD)
    rows, inner = own_tokens.shape
    return call(
        turn_kernel,
        (shape_of((rows, inner), bf16), shape_of((rows // 2, inner), bf16)),
        [SMEM, HBM, HBM],
        (place, in_hbm(own_tokens), in_hbm(sign_rows)),
        "turn",
        scratch_shapes=[
            pltpu.VMEM(own_tokens.shape, bf16),
            pltpu.VMEM(sign_rows.shape, jnp.int32),
            pltpu.SemaphoreType.DMA((2,)),
        ],
    )


def tie(array, *after):
    return call(
        lambda *refs: None,
        shape_of(array.shape, array.dtype),
        [ANY] * (1 + len(after)),
        (array, *after),
        "tie",
        out_specs=ANY,
        input_output_aliases={0: 0},
    )


def gate(array):
    def body(array_ref, out_ref):
        out_ref[...] = jnp.zeros_like(out_ref)

    return call(body, shape_of((8, HAD), f32), [ANY], (array,), "gate", flops=4 * 10**9)


def prepare_kernel(near, far, place_ref, *rest):
    shard_refs = rest[: len(near)]
    codes_hbm, sums_ref, far_ref, late_ref, near_ref, sems = rest[len(near) :]
    words, columns = near_ref.shape[2:]

    def fetch(position, kind):
        flip = (near + far)[position]
        first = pl.multiple_of((place_ref[0] ^ flip) * words, WORDS)
        there = position - len(near)
        target = near_ref.at[position, kind] if there < 0 else far_ref.at[there, kind]
        return pltpu.make_async_copy(
            codes_hbm.at[kind, pl.ds(first, words), :], target, sems.at[position, kind]
        )

    for kind in range(3):
        for position in range(len(near)):
            fetch(position, kind).start()
    for position in range(len(near), len(near + far)):
        for kind in range(3):
            fetch(position, kind).start()
    fix = row_correction([ref[...] for ref in shard_refs], QKV_ORDER)
    width = tile_width(columns)
    late_ref[...] = shard_refs[0][late_ref.shape[0] :, :]

    def every_shard(kind, carry):
        for position in range(len(near)):
            fetch(position, kind).wait()
        for first in range(0, columns, width):
            cols = slice(first, first + width)
            total = -fix
            for position, ref in enumerate(shard_refs):
                total = product(ref[...], near_ref, (position, kind), cols, QKV_ORDER, total)
            sums_ref[kind, :, cols] = total
        return carry

    lax.fori_loop(0, 3, every_shard, 0)
    for position in range(len(near), len(near + far)):
        for kind in range(3):
            fetch(position, kind).wait()


def prepare(place, near, far, shards, codes):
    rows, inner = shards[0].shape
    columns = codes.shape[2]
    words = inner // PLANES
    return call(
        functools.partial(prepare_kernel, near, far),
        (
            shape_of((3, rows, columns), f32),
            shape_of((len(far), 3, words, columns), jnp.int32),
            shape_of((rows // 2, inner), bf16),
        ),
        [SMEM] + [VMEM] * len(near) + [HBM],
        (place, *shards, in_hbm(codes)),
        "prepare",
        scratch_shapes=[
            pltpu.VMEM((len(near), 3, words, columns), jnp.int32),
            pltpu.SemaphoreType.DMA((len(near + far), 3)),
        ],
    )


def project_kernel(kinds, first_row, groups, positions, whole, ending, *rest):
    count = len(positions)
    shard_refs = rest[: groups * count]
    sums_ref, words_ref = rest[groups * count : groups * count + 2]
    if ending:
        scale_ref, sign_ref = rest[groups * count + 2 : groups * count + 4]
    out_ref = rest[-1]
    columns = sums_ref.shape[2]
    width = tile_width(columns)
    shards = []
    for place in range(count):
        parts = [shard_refs[g * count + place][...] for g in range(groups)]
        shards.append(parts[0] if groups == 1 else jnp.concatenate(parts, 0))
    fix = row_correction(shards, QKV_ORDER)
    row_count = shards[0].shape[0]
    rows = slice(first_row, first_row + row_count)
    doubled = double_hadamard()
    ones = jnp.ones((HD, HD), bf16)
    for place, kind in enumerate(kinds):
        heads = []
        for first in range(0, columns, width):
            cols = slice(first, first + width)
            part = (sums_ref[kind, rows, cols] if whole else sums_ref[place, :, cols]) - fix
            for shard, position in zip(shards, positions):
                part = product(shard, words_ref, (position, kind), cols, QKV_ORDER, part)
            if not ending:
                out_ref[place, :, cols] = part
                continue
            for lane in range(0, width, HD):
                at = slice(first + lane, first + lane + HD)
                scale_row = scale_ref[kind : kind + 1, at] * np.float32(D ** (-0.5))
                heads.append(part[:, lane : lane + HD] * scale_row)
        if not ending:
            continue
        mixed = rotate_halves(jnp.concatenate(heads, 0), doubled)
        signs = []
        for head in range(len(heads)):
            sign_row = sign_ref[kind : kind + 1, head * HD : (head + 1) * HD]
            sign_row = signed(sign_row) * np.float32(HAD ** (-0.5))
            signs.append(mixed[head * row_count : (head + 1) * row_count] * sign_row)
        if kind != 2:
            square = jnp.concatenate([(part * part).astype(bf16) for part in signs], 0)
            mean = jnp.dot(square, ones, preferred_element_type=f32) * (1.0 / HD)
            factor = lax.rsqrt(mean + epsilon)
            signs = [
                part * factor[head * row_count : (head + 1) * row_count]
                for head, part in enumerate(signs)
            ]
        for head, part in enumerate(signs):
            out_ref[place, :, head * HD : (head + 1) * HD] = part.astype(bf16)


def project(kinds, first_row, groups, positions, sums, words, ending, flops=1):
    inner = groups[0][0].shape[1]
    columns = sums.shape[2]
    row_count = sum(group[0].shape[0] for group in groups)
    whole = sums.shape[0] == 3
    args = [shard for group in groups for shard in group] + [sums, words]
    own_args = len(args) + 2
    if ending is not None:
        args += ending
    return call(
        functools.partial(
            project_kernel, kinds, first_row, len(groups), positions, whole, ending is not None
        ),
        shape_of((len(kinds), row_count, columns), f32 if ending is None else bf16),
        [VMEM] * min(len(args), own_args) + [ANY] * max(len(args) - own_args, 0),
        args,
        "project",
        flops=flops,
    )


def near_row(row, swap_pair):
    if swap_pair is None:
        return row
    by, odd = swap_pair
    return jnp.where(lax.rem(row // by, 2) == odd, row + by, row - by)


def window_mask(place_ref, windows_ref, segments, row_count):
    lane = lax.broadcasted_iota(jnp.int32, (1, sum(rows for _, _, rows in segments)), 1)
    ids, base = None, 0
    for swap_pair, first, rows in segments:
        tile = (lane + (first - base)) // TILE
        ids_here = near_row(place_ref[1], swap_pair) * WTILES + tile
        ids = ids_here if ids is None else jnp.where(lane >= base, ids_here, ids)
        base += rows
    masks = []
    for tile in range(row_count // TILE):
        hit = jnp.zeros(lane.shape, f32)
        for entry in range(windows_ref.shape[2]):
            hit = jnp.where(ids == windows_ref[tile, 0, entry], 1.0, hit)
        masks.append(jnp.broadcast_to(hit, (TILE, lane.shape[1])))
    return jnp.concatenate(masks, 0)


def attend_kernel(
    segments, halves, blocks, has_sum, last, share_order, place_ref, windows_ref, *rest
):
    rest = list(rest)
    q_refs = [rest.pop(0) for _ in range(halves)]
    kv_refs = [rest.pop(0) for _ in range(blocks)]
    sum_ref = rest.pop(0) if has_sum else None
    if last:
        oin_ref, out_ref, rotated_ref = rest
    else:
        (out_ref,) = rest
    columns = q_refs[0].shape[2]
    row_count = sum(ref.shape[1] for ref in q_refs)
    heads = [slice(head, head + HD) for head in range(0, columns, HD)]
    mask = window_mask(place_ref, windows_ref, segments, row_count)
    scores = []
    for at in heads:
        keys = jnp.concatenate([ref[0, :, at] for ref in kv_refs], 0)
        scores.append(
            lax.dot_general(
                jnp.concatenate([ref[0, :, at] for ref in q_refs], 0),
                keys,
                (((1,), (1,)), ((), ())),
                preferred_element_type=f32,
            )
        )
    weights = [
        (jnp.exp(score * np.float32(HD ** (-0.5))) * mask).astype(bf16) for score in scores
    ]
    totals = []
    for head, at in enumerate(heads):
        values = jnp.concatenate([ref[1, :, at] for ref in kv_refs], 0)
        values = jnp.concatenate([values, jnp.ones_like(values)], 1)
        total = jnp.dot(weights[head], values, preferred_element_type=f32)
        if has_sum:
            total = total + sum_ref[head]
        totals.append(total)
    if not last:
        for head, total in enumerate(totals):
            out_ref[head] = total
        return
    matrix = hadamard(OUT_ORDER)
    factor = turn_factor(OUT_ORDER)
    for head, at in enumerate(heads):
        attended = (totals[head][:, :HD] / totals[head][:, HD:]).astype(bf16)
        sign_row = signed(oin_ref[head : head + 1, :])
        flipped = (attended.astype(f32) * sign_row).astype(bf16)
        rotated_ref[:, at] = jnp.dot(flipped, matrix, preferred_element_type=f32) * factor
    share = row_count // len(share_order)
    pieces = []
    for flip in share_order:
        owner = place_ref[0] ^ flip
        pieces.append(rotated_ref[pl.ds(pl.multiple_of(owner * share, 8), share), :])
    out_ref[...] = jnp.concatenate(pieces, 0).astype(bf16)


def attend(place, windows, queries, blocks, segments, running, ending):
    columns = queries[0].shape[2]
    row_count = sum(part.shape[1] for part in queries)
    args = [place, windows, *queries, *blocks]
    if running is not None:
        args.append(running)
    scratch, share_order = [], None
    if ending is None:
        out_shape = shape_of((columns // HD, row_count, 2 * HD), f32)
    else:
        oin_sign, share_order = ending
        args.append(oin_sign.reshape(-1, HAD))
        out_shape = shape_of((row_count, columns), bf16)
        scratch = [pltpu.VMEM((row_count, columns), f32)]
    return call(
        functools.partial(
            attend_kernel,
            segments,
            len(queries),
            len(blocks),
            running is not None,
            ending is not None,
            share_order,
        ),
        out_shape,
        [SMEM] * 2 + [VMEM] * (len(args) - 2),
        args,
        "attend",
        scratch_shapes=scratch,
    )


def unpack_out_kernel(codes_ref, after_ref, weights_ref):
    for first in range(0, codes_ref.shape[0], WORDS):

        def some(step, carry):
            cols = pl.ds(pl.multiple_of(step * 512, 512), 512)
            at = first * PLANES
            for piece in pieces_of(codes_ref[first : first + WORDS, cols], OUT_ORDER):
                weights_ref[at : at + piece.shape[0], cols] = piece
                at += piece.shape[0]
            return carry

        lax.fori_loop(0, codes_ref.shape[1] // 512, some, 0)


def unpack_out(codes, after):
    words, columns = codes.shape
    return call(
        unpack_out_kernel,
        shape_of((words * PLANES, columns), bf16),
        [VMEM, ANY],
        (codes, after),
        "unpack_out",
    )


def out_kernel(first, rotated_ref, weights_ref, scale_ref, send_ref, keep_ref):
    rows = rotated_ref[...]
    fix = row_correction([rows], OUT_ORDER)
    half, columns = send_ref.shape
    width = 256
    for at in range(0, columns, width):
        cols = slice(first + at, first + at + width)
        part = jnp.dot(rows, weights_ref[:, cols], preferred_element_type=f32) - fix
        for lane in range(0, width, HAD):
            place = (first + at + lane) // HAD
            scale_row = scale_ref[place : place + 1, :] * np.float32((HEADS * HD) ** (-0.5))
            done = (part[:, lane : lane + HAD] * scale_row).astype(bf16)
            send_ref[:, at + lane : at + lane + HAD] = done[:half]
            keep_ref[:, at + lane : at + lane + HAD] = done[half:]


def out_project(rotated, weights, scale_rows, first, columns):
    row_count, inner = rotated.shape
    result = shape_of((row_count // 2, columns), bf16)
    return call(
        functools.partial(out_kernel, first),
        (result, result),
        [VMEM] * 3,
        (rotated, weights, scale_rows),
        "out_project",
    )


def finish_kernel(chunks, first, sign_ref, *rest):
    out_hbm, done_ref, sems = rest[-3:]
    doubled = double_hadamard()
    copies = []
    for chunk in range(chunks):
        keep_ref, more_ref = rest[2 * chunk : 2 * chunk + 2]
        share, columns = keep_ref.shape
        totals = keep_ref[...].astype(f32) + more_ref[...].astype(f32)
        blocks = [totals[:, at : at + HAD] for at in range(0, columns, HAD)]
        turned = rotate_halves(jnp.concatenate(blocks, 0), doubled)
        for block in range(len(blocks)):
            place = first // HAD + block
            sign_row = signed(sign_ref[place : place + 1, :]) * np.float32(HAD ** (-0.5))
            done = turned[block * share : (block + 1) * share] * sign_row
            done_ref[:, place * HAD : (place + 1) * HAD] = done.astype(bf16)
        cols = pl.ds(first, columns)
        copies.append(
            pltpu.make_async_copy(done_ref.at[:, cols], out_hbm.at[:, cols], sems.at[chunk])
        )
        copies[-1].start()
        first += columns
    for copy in copies:
        copy.wait()


def finish(pairs, sign_rows, first, base):
    share = pairs[0][0].shape[0]
    args = [sign_rows] + [array for pair in pairs for array in pair]
    in_specs = [VMEM] * len(args)
    aliases = {}
    if base is not None:
        aliases = {len(args): 0}
        args.append(base)
        in_specs.append(HBM)
    return call(
        functools.partial(finish_kernel, len(pairs), first),
        shape_of((share, D), bf16),
        in_specs,
        args,
        "finish",
        out_specs=HBM,
        scratch_shapes=[pltpu.VMEM((share, D), bf16), pltpu.SemaphoreType.DMA((len(pairs),))],
        input_output_aliases=aliases,
    )


def swap(shard, bit):
    peers = lax.axis_size("head")
    return lax.ppermute(shard, "head", [(i, i ^ bit) for i in range(peers)])


def row_swaps(row_tiles):
    swaps = []
    for by in (1, 3, 4, 5) if row_tiles > HROWS else (1,):
        for odd in (0, 1):
            low = [i for i in range(row_tiles - by) if (i // by) % 2 == odd]
            swaps.append((by, odd, [(i, i + by) for i in low] + [(i + by, i) for i in low]))
    return swaps


def halving_order(head_count):
    flips = [0]
    bit = head_count // 2
    while bit >= 1:
        flips = [f | bit for f in flips] + flips
        bit //= 2
    return tuple(flips)


CHUNKS = (2560, 2560)


def on_device(
    tokens,
    in_sign,
    qkv_codes,
    qkv_scale,
    qkv_sign,
    windows,
    oin_sign,
    out_codes,
    out_scale,
    out_sign,
):
    head_count = lax.axis_size("head")
    row_tiles = lax.axis_size("height")
    row_place = lax.axis_index("height")
    head_place = lax.axis_index("head").astype(jnp.int32)
    top = head_count // 2
    place = jnp.stack([head_place, row_place.astype(jnp.int32)])
    low_bits = [1 << b for b in range(top.bit_length() - 1)]

    own, early = turn(place, tokens[0], in_sign)
    half_rows = early.shape[0]
    early = swap(early, top)
    near = {0: own}
    for bit in low_bits:
        for flip in list(near):
            near[flip ^ bit] = swap(near[flip], bit)
    codes = jnp.transpose(qkv_codes, (1, 0, 2))
    near_flips = tuple(sorted(near))
    far_flips = tuple(flip ^ top for flip in near_flips)
    sums, words, late = prepare(
        place, near_flips, far_flips, [near[flip] for flip in near_flips], codes
    )
    late = swap(late, top)
    swaps = row_swaps(row_tiles)
    ending = [qkv_scale, qkv_sign]
    every = tuple(range(len(far_flips)))
    halves, key_values, moved, gates = [], [], [], []
    for half, first_row in ((early, 0), (late, half_rows)):
        shards = {top: tie(half, *gates, sums)}
        for bit in low_bits:
            for flip in list(shards):
                shards[flip ^ bit] = swap(shards[flip], bit)
        shards = [shards[flip] for flip in far_flips]
        partial = project(
            (1, 2), first_row, [shards[:-1]], every[:-1], sums, words, None, 4 * 10**9
        )
        key_value = project((1, 2), 0, [shards[-1:]], every[-1:], partial, words, ending)
        moved.append([lax.ppermute(key_value, "height", pairs) for _, _, pairs in swaps])
        halves.append(shards)
        key_values.append(key_value)
        gates.append(gate(key_value))
    queries = [project((0,), 0, halves, every, sums, words, ending, 4 * 10**9)]
    out_weights = unpack_out(out_codes, key_values[1])

    listed = jnp.transpose(windows, (1, 0, 2))
    own_rows = ((None, 0, half_rows), (None, half_rows, half_rows))
    early_rows = tuple(((by, odd), 0, half_rows) for by, odd, _ in swaps)
    late_rows = tuple(((by, odd), half_rows, half_rows) for by, odd, _ in swaps)
    running = attend(place, listed, queries, key_values, own_rows, None, None)
    running = attend(place, listed, queries, moved[0], early_rows, running, None)
    rotated = attend(
        place,
        listed,
        queries,
        moved[1],
        late_rows,
        running,
        (oin_sign, halving_order(head_count)),
    )

    bits = low_bits + [top]
    scale_rows = out_scale.reshape(-1, HAD)
    sign_rows = out_sign.reshape(-1, HAD)
    pairs, sums_sent = [], []
    first = 0
    for columns in CHUNKS:
        part, keep = out_project(rotated, out_weights, scale_rows, first, columns)
        if sums_sent:
            part = tie(part, sums_sent[-1])
        for bit in bits:
            more = swap(part, bit)
            if bit == top:
                break
            total = keep.astype(f32) + more.astype(f32)
            half = total.shape[0] // 2
            part, keep = total[:half].astype(bf16), total[half:]
            sums_sent.append(part)
        pairs.append((keep, more))
        first += columns
    base = finish(pairs[:-1], sign_rows, 0, None)
    return finish(pairs[-1:], sign_rows, D - CHUNKS[-1], base)[None]


def solution(mesh):
    return jax.shard_map(
        on_device,
        mesh=mesh,
        in_specs=(
            P(("clip", "height"), None, "head"),
            P(),
            P(None, None, "head"),
            P(None, "head"),
            P(None, "head"),
            P(("clip", "height"), None, None),
            P("head"),
            P("head", None),
            P(),
            P(),
        ),
        out_specs=P(("clip", "height"), "head", None),
        check_vma=False,
    )
```

```python
import functools

import jax
import jax.numpy as jnp
import numpy as np
from jax import lax
from jax.experimental import pallas as pl
from jax.experimental.pallas import tpu as pltpu
from jax.sharding import PartitionSpec as P

D = 5120
HD = 128
HEADS = 24
HAD = 128
TILE = 64
HROWS = 4
WTILES = 3
PLANES = 8
WORDS = HAD // PLANES
QKV_ORDER = "half"
OUT_ORDER = "byte"

epsilon = 1e-06
f32 = jnp.float32
bf16 = jnp.bfloat16
VMEM = pl.BlockSpec(memory_space=pltpu.VMEM)
SMEM = pl.BlockSpec(memory_space=pltpu.SMEM)
ANY = pl.BlockSpec(memory_space=pl.ANY)
HBM = pl.BlockSpec(memory_space=pltpu.HBM)


def shape_of(shape, dtype):
    return jax.ShapeDtypeStruct(tuple(shape), dtype)


def in_hbm(array):
    return pltpu.with_memory_space_constraint(array, pltpu.HBM)


def call(body, out_shape, in_specs, args, name, out_specs=None, megabytes=16, flops=1, **more):
    if out_specs is None:
        out_specs = jax.tree.map(lambda _: VMEM, out_shape)
    return pl.pallas_call(
        body,
        out_shape=out_shape,
        in_specs=in_specs,
        out_specs=out_specs,
        compiler_params=pltpu.CompilerParams(vmem_limit_bytes=megabytes * 2**20),
        cost_estimate=pl.CostEstimate(flops=flops, bytes_accessed=1, transcendentals=0),
        name=name,
        **more,
    )(*args)


def lanes():
    return lax.broadcasted_iota(jnp.int32, (HAD, HAD), 1)


def hadamard(order):
    row = lax.broadcasted_iota(jnp.int32, (HAD, HAD), 0)
    column = lanes()
    word = PLANES * (column & (WORDS - 1))
    if order == "half":
        column = word + column // WORDS
    if order == "byte":
        column = word + column // (2 * WORDS) + (PLANES // 2) * ((column // WORDS) & 1)
    shared = row & column
    shared = shared ^ (shared >> 4)
    shared = shared ^ (shared >> 2)
    shared = shared ^ (shared >> 1)
    return (1 - 2 * (shared & 1)).astype(f32).astype(bf16)


def double_hadamard():
    plain = hadamard("plain")
    return jnp.concatenate([plain, plain], 0)


def plane_power(base, order):
    lane = lax.broadcasted_iota(jnp.int32, (1, HAD), 1)
    if order == "half":
        power = jnp.minimum(lane // WORDS, PLANES - 2)
    else:
        power = jnp.minimum(lane // (2 * WORDS), PLANES // 2 - 2)
    value = jnp.where(power & 1 == 1, base, 1.0)
    value = value * jnp.where(power & 2 == 2, base**2, 1.0)
    return value * jnp.where(power & 4 == 4, base**4, 1.0)


def turn_factor(order):
    return plane_power(0.25, order) * np.float32(HAD ** (-0.5))


def signed(sign_bits):
    return (2 * sign_bits - 1).astype(f32)


def pieces_of(words, order):
    if order == "half":
        packed = words.astype(jnp.int16)
        masked = [packed & jnp.int16(3 << (2 * k)) for k in range(PLANES - 1)]
        masked.append((words >> 2).astype(jnp.int16) & jnp.int16(3 << (2 * PLANES - 4)))
    else:
        pair = jnp.concatenate([words & 255, words >> 8], 0)
        packed = pair.astype(jnp.int8)
        masked = [packed & jnp.int8(3 << (2 * k)) for k in range(PLANES // 2 - 1)]
        masked.append((pair >> 2).astype(jnp.int8) & jnp.int8(3 << (PLANES - 4)))
    return [piece.astype(bf16) for piece in masked]


def decode(words, order):
    blocks = []
    for first in range(0, words.shape[0], WORDS):
        blocks += pieces_of(words[first : first + WORDS], order)
    return jnp.concatenate(blocks, 0)


def row_correction(row_list, order):
    factor_row = plane_power(4.0, order) * 1.5
    total = None
    for rows in row_list:
        for first in range(0, rows.shape[1], HAD):
            term = rows[:, first : first + HAD].astype(f32)
            total = term if total is None else total + term
    return jnp.sum(total * factor_row, axis=1, keepdims=True)


def rotate_halves(values, doubled):
    high = values.astype(bf16)
    low = (values - high.astype(f32)).astype(bf16)
    return jnp.dot(jnp.concatenate([high, low], 1), doubled, preferred_element_type=f32)


def tile_width(columns):
    for width in (256, 128):
        if columns % width == 0:
            return width


def early_rows(rows):
    return rows * 7 // 12 // WORDS * WORDS


def turn_kernel(place_ref, x_hbm, sign_hbm, own_ref, send_ref, x_ref, sign_ref, sems):
    copies = [
        pltpu.make_async_copy(x_hbm, x_ref, sems.at[0]),
        pltpu.make_async_copy(sign_hbm, sign_ref, sems.at[1]),
    ]
    for copy in copies:
        copy.start()
    matrix = hadamard(QKV_ORDER)
    factor = turn_factor(QKV_ORDER)
    for copy in copies:
        copy.wait()
    blocks = x_ref.shape[1] // HAD
    first = place_ref[0] * blocks
    for b in range(blocks):
        cols = slice(b * HAD, (b + 1) * HAD)
        sign_row = signed(sign_ref[pl.ds(first + b, 1), :])
        flipped = (x_ref[:, cols].astype(f32) * sign_row).astype(bf16)
        turned = jnp.dot(flipped, matrix, preferred_element_type=f32)
        turned = (turned * factor).astype(bf16)
        own_ref[:, cols] = turned
        send_ref[:, cols] = turned[: send_ref.shape[0]]


def turn(place, own_tokens, in_sign):
    sign_rows = in_sign.reshape(-1, HAD)
    rows, inner = own_tokens.shape
    return call(
        turn_kernel,
        (shape_of((rows, inner), bf16), shape_of((early_rows(rows), inner), bf16)),
        [SMEM, HBM, HBM],
        (place, in_hbm(own_tokens), in_hbm(sign_rows)),
        "turn",
        scratch_shapes=[
            pltpu.VMEM(own_tokens.shape, bf16),
            pltpu.VMEM(sign_rows.shape, jnp.int32),
            pltpu.SemaphoreType.DMA((2,)),
        ],
    )


def tie(array, *after):
    return call(
        lambda *refs: None,
        shape_of(array.shape, array.dtype),
        [ANY] * (1 + len(after)),
        (array, *after),
        "tie",
        out_specs=ANY,
        input_output_aliases={0: 0},
    )


def gate(array):
    def body(array_ref, out_ref):
        out_ref[...] = jnp.zeros_like(out_ref)

    return call(body, shape_of((8, HAD), f32), [ANY], (array,), "gate", flops=4 * 10**9)


def prepare_kernel(near, far, place_ref, *rest):
    shard_refs = rest[: len(near)]
    codes_hbm, sums_ref, far_ref, late_ref, near_ref, sems = rest[len(near) :]
    words, columns = near_ref.shape[2:]

    def fetch(position, kind):
        flip = (near + far)[position]
        first = pl.multiple_of((place_ref[0] ^ flip) * words, WORDS)
        there = position - len(near)
        target = near_ref.at[position, kind] if there < 0 else far_ref.at[there, kind]
        return pltpu.make_async_copy(
            codes_hbm.at[kind, pl.ds(first, words), :], target, sems.at[position, kind]
        )

    for kind in range(3):
        for position in range(len(near)):
            fetch(position, kind).start()
    for position in range(len(near), len(near + far)):
        for kind in range(3):
            fetch(position, kind).start()
    fix = row_correction([ref[...] for ref in shard_refs], QKV_ORDER)
    width = tile_width(columns)
    late_ref[...] = shard_refs[0][shard_refs[0].shape[0] - late_ref.shape[0] :, :]

    def every_shard(kind, carry):
        for position in range(len(near)):
            fetch(position, kind).wait()
        for first in range(0, columns, width):
            cols = slice(first, first + width)
            total = -fix
            for position, ref in enumerate(shard_refs):
                weights = decode(near_ref[position, kind, :, cols], QKV_ORDER)
                total = total + jnp.dot(ref[...], weights, preferred_element_type=f32)
            sums_ref[kind, :, cols] = total
        return carry

    lax.fori_loop(0, 3, every_shard, 0)
    for position in range(len(near), len(near + far)):
        for kind in range(3):
            fetch(position, kind).wait()


def prepare(place, near, far, shards, codes):
    rows, inner = shards[0].shape
    columns = codes.shape[2]
    words = inner // PLANES
    return call(
        functools.partial(prepare_kernel, near, far),
        (
            shape_of((3, rows, columns), f32),
            shape_of((len(far), 3, words, columns), jnp.int32),
            shape_of((rows - early_rows(rows), inner), bf16),
        ),
        [SMEM] + [VMEM] * len(near) + [HBM],
        (place, *shards, in_hbm(codes)),
        "prepare",
        scratch_shapes=[
            pltpu.VMEM((len(near), 3, words, columns), jnp.int32),
            pltpu.SemaphoreType.DMA((len(near + far), 3)),
        ],
    )


def project_kernel(kinds, first_row, groups, positions, whole, ending, *rest):
    count = len(positions)
    shard_refs = rest[: groups * count]
    sums_ref, words_ref = rest[groups * count : groups * count + 2]
    if ending:
        scale_ref, sign_ref = rest[groups * count + 2 : groups * count + 4]
    out_ref = rest[-1]
    columns = sums_ref.shape[2]
    width = tile_width(columns)
    shards = []
    for place in range(count):
        parts = [shard_refs[g * count + place][...] for g in range(groups)]
        shards.append(parts[0] if groups == 1 else jnp.concatenate(parts, 0))
    fix = row_correction(shards, QKV_ORDER)
    row_count = shards[0].shape[0]
    rows = slice(first_row, first_row + row_count)
    doubled = double_hadamard()
    ones = jnp.ones((HD, HD), bf16)
    for place, kind in enumerate(kinds):
        heads = []
        for first in range(0, columns, width):
            cols = slice(first, first + width)
            part = (sums_ref[kind, rows, cols] if whole else sums_ref[place, :, cols]) - fix
            for shard, position in zip(shards, positions):
                weights = decode(words_ref[position, kind, :, cols], QKV_ORDER)
                part = part + jnp.dot(shard, weights, preferred_element_type=f32)
            if not ending:
                out_ref[place, :, cols] = part
                continue
            for lane in range(0, width, HD):
                at = slice(first + lane, first + lane + HD)
                scale_row = scale_ref[kind : kind + 1, at] * np.float32(D ** (-0.5))
                heads.append(part[:, lane : lane + HD] * scale_row)
        if not ending:
            continue
        mixed = rotate_halves(jnp.concatenate(heads, 0), doubled)
        signs = []
        for head in range(len(heads)):
            sign_row = sign_ref[kind : kind + 1, head * HD : (head + 1) * HD]
            sign_row = signed(sign_row) * np.float32(HAD ** (-0.5))
            signs.append(mixed[head * row_count : (head + 1) * row_count] * sign_row)
        if kind != 2:
            square = jnp.concatenate([(part * part).astype(bf16) for part in signs], 0)
            mean = jnp.dot(square, ones, preferred_element_type=f32) * (1.0 / HD)
            factor = lax.rsqrt(mean + epsilon)
            signs = [
                part * factor[head * row_count : (head + 1) * row_count]
                for head, part in enumerate(signs)
            ]
        for head, part in enumerate(signs):
            out_ref[place, :, head * HD : (head + 1) * HD] = part.astype(bf16)


def project(kinds, first_row, groups, positions, sums, words, ending, flops=1):
    inner = groups[0][0].shape[1]
    columns = sums.shape[2]
    row_count = sum(group[0].shape[0] for group in groups)
    whole = sums.shape[0] == 3
    args = [shard for group in groups for shard in group] + [sums, words]
    own_args = len(args) + 2
    if ending is not None:
        args += ending
    return call(
        functools.partial(
            project_kernel, kinds, first_row, len(groups), positions, whole, ending is not None
        ),
        shape_of((len(kinds), row_count, columns), f32 if ending is None else bf16),
        [VMEM] * min(len(args), own_args) + [ANY] * max(len(args) - own_args, 0),
        args,
        "project",
        flops=flops,
    )


def near_row(row, swap_pair):
    if swap_pair is None:
        return row
    by, odd = swap_pair
    return jnp.where(lax.rem(row // by, 2) == odd, row + by, row - by)


def window_mask(place_ref, windows_ref, segments, row_count):
    lane = lax.broadcasted_iota(jnp.int32, (1, sum(rows for _, _, rows in segments)), 1)
    ids, base = None, 0
    for swap_pair, first, rows in segments:
        tile = (lane + (first - base)) // TILE
        ids_here = near_row(place_ref[1], swap_pair) * WTILES + tile
        ids = ids_here if ids is None else jnp.where(lane >= base, ids_here, ids)
        base += rows
    masks = []
    for tile in range(row_count // TILE):
        hit = jnp.zeros(lane.shape, f32)
        for entry in range(windows_ref.shape[2]):
            hit = jnp.where(ids == windows_ref[tile, 0, entry], 1.0, hit)
        masks.append(jnp.broadcast_to(hit, (TILE, lane.shape[1])))
    return jnp.concatenate(masks, 0)


def attend_kernel(
    segments, halves, blocks, has_sum, last, share_order, place_ref, windows_ref, *rest
):
    rest = list(rest)
    q_refs = [rest.pop(0) for _ in range(halves)]
    kv_refs = [rest.pop(0) for _ in range(blocks)]
    sum_ref = rest.pop(0) if has_sum else None
    if last:
        oin_ref, out_ref, rotated_ref = rest
    else:
        (out_ref,) = rest
    columns = q_refs[0].shape[2]
    row_count = sum(ref.shape[1] for ref in q_refs)
    heads = [slice(head, head + HD) for head in range(0, columns, HD)]
    mask = window_mask(place_ref, windows_ref, segments, row_count)
    scores = []
    for at in heads:
        keys = jnp.concatenate([ref[0, :, at] for ref in kv_refs], 0)
        scores.append(
            lax.dot_general(
                jnp.concatenate([ref[0, :, at] for ref in q_refs], 0),
                keys,
                (((1,), (1,)), ((), ())),
                preferred_element_type=f32,
            )
        )
    weights = [
        (jnp.exp(score * np.float32(HD ** (-0.5))) * mask).astype(bf16) for score in scores
    ]
    totals = []
    for head, at in enumerate(heads):
        values = jnp.concatenate([ref[1, :, at] for ref in kv_refs], 0)
        values = jnp.concatenate([values, jnp.ones_like(values)], 1)
        total = jnp.dot(weights[head], values, preferred_element_type=f32)
        if has_sum:
            total = total + sum_ref[head]
        totals.append(total)
    if not last:
        for head, total in enumerate(totals):
            out_ref[head] = total
        return
    matrix = hadamard(OUT_ORDER)
    factor = turn_factor(OUT_ORDER)
    for head, at in enumerate(heads):
        attended = (totals[head][:, :HD] / totals[head][:, HD:]).astype(bf16)
        sign_row = signed(oin_ref[head : head + 1, :])
        flipped = (attended.astype(f32) * sign_row).astype(bf16)
        rotated_ref[:, at] = jnp.dot(flipped, matrix, preferred_element_type=f32) * factor
    share = row_count // len(share_order)
    pieces = []
    for flip in share_order:
        owner = place_ref[0] ^ flip
        pieces.append(rotated_ref[pl.ds(pl.multiple_of(owner * share, 8), share), :])
    out_ref[...] = jnp.concatenate(pieces, 0).astype(bf16)


def attend(place, windows, queries, blocks, segments, running, ending):
    columns = queries[0].shape[2]
    row_count = sum(part.shape[1] for part in queries)
    args = [place, windows, *queries, *blocks]
    if running is not None:
        args.append(running)
    scratch, share_order = [], None
    if ending is None:
        out_shape = shape_of((columns // HD, row_count, 2 * HD), f32)
    else:
        oin_sign, share_order = ending
        args.append(oin_sign.reshape(-1, HAD))
        out_shape = shape_of((row_count, columns), bf16)
        scratch = [pltpu.VMEM((row_count, columns), f32)]
    return call(
        functools.partial(
            attend_kernel,
            segments,
            len(queries),
            len(blocks),
            running is not None,
            ending is not None,
            share_order,
        ),
        out_shape,
        [SMEM] * 2 + [VMEM] * (len(args) - 2),
        args,
        "attend",
        scratch_shapes=scratch,
    )


def unpack_out_kernel(codes_ref, after_ref, weights_ref):
    for first in range(0, codes_ref.shape[0], WORDS):

        def some(step, carry):
            cols = pl.ds(pl.multiple_of(step * 512, 512), 512)
            at = first * PLANES
            for piece in pieces_of(codes_ref[first : first + WORDS, cols], OUT_ORDER):
                weights_ref[at : at + piece.shape[0], cols] = piece
                at += piece.shape[0]
            return carry

        lax.fori_loop(0, codes_ref.shape[1] // 512, some, 0)


def unpack_out(codes, after):
    words, columns = codes.shape
    return call(
        unpack_out_kernel,
        shape_of((words * PLANES, columns), bf16),
        [VMEM, ANY],
        (codes, after),
        "unpack_out",
    )


def out_kernel(first, rotated_ref, weights_ref, scale_ref, send_ref, keep_ref):
    rows = rotated_ref[...]
    fix = row_correction([rows], OUT_ORDER)
    half, columns = send_ref.shape
    width = 256
    for at in range(0, columns, width):
        cols = slice(first + at, first + at + width)
        part = jnp.dot(rows, weights_ref[:, cols], preferred_element_type=f32) - fix
        for lane in range(0, width, HAD):
            place = (first + at + lane) // HAD
            scale_row = scale_ref[place : place + 1, :] * np.float32((HEADS * HD) ** (-0.5))
            done = (part[:, lane : lane + HAD] * scale_row).astype(bf16)
            send_ref[:, at + lane : at + lane + HAD] = done[:half]
            keep_ref[:, at + lane : at + lane + HAD] = done[half:]


def out_project(rotated, weights, scale_rows, first, columns):
    row_count, inner = rotated.shape
    result = shape_of((row_count // 2, columns), bf16)
    return call(
        functools.partial(out_kernel, first),
        (result, result),
        [VMEM] * 3,
        (rotated, weights, scale_rows),
        "out_project",
    )


def finish_kernel(chunks, first, sign_ref, *rest):
    out_hbm, done_ref, sems = rest[-3:]
    doubled = double_hadamard()
    copies = []
    for chunk in range(chunks):
        keep_ref, more_ref = rest[2 * chunk : 2 * chunk + 2]
        share, columns = keep_ref.shape
        totals = keep_ref[...].astype(f32) + more_ref[...].astype(f32)
        blocks = [totals[:, at : at + HAD] for at in range(0, columns, HAD)]
        turned = rotate_halves(jnp.concatenate(blocks, 0), doubled)
        for block in range(len(blocks)):
            place = first // HAD + block
            sign_row = signed(sign_ref[place : place + 1, :]) * np.float32(HAD ** (-0.5))
            done = turned[block * share : (block + 1) * share] * sign_row
            done_ref[:, place * HAD : (place + 1) * HAD] = done.astype(bf16)
        cols = pl.ds(first, columns)
        copies.append(
            pltpu.make_async_copy(done_ref.at[:, cols], out_hbm.at[:, cols], sems.at[chunk])
        )
        copies[-1].start()
        first += columns
    for copy in copies:
        copy.wait()


def finish(pairs, sign_rows, first, base):
    share = pairs[0][0].shape[0]
    args = [sign_rows] + [array for pair in pairs for array in pair]
    in_specs = [VMEM] * len(args)
    aliases = {}
    if base is not None:
        aliases = {len(args): 0}
        args.append(base)
        in_specs.append(HBM)
    return call(
        functools.partial(finish_kernel, len(pairs), first),
        shape_of((share, D), bf16),
        in_specs,
        args,
        "finish",
        out_specs=HBM,
        scratch_shapes=[pltpu.VMEM((share, D), bf16), pltpu.SemaphoreType.DMA((len(pairs),))],
        input_output_aliases=aliases,
    )


def swap(shard, bit):
    peers = lax.axis_size("head")
    return lax.ppermute(shard, "head", [(i, i ^ bit) for i in range(peers)])


def row_swaps(row_tiles):
    swaps = []
    for by in (1, 3, 4, 5) if row_tiles > HROWS else (1,):
        for odd in (1, 0):
            low = [i for i in range(row_tiles - by) if (i // by) % 2 == odd]
            swaps.append((by, odd, [(i, i + by) for i in low] + [(i + by, i) for i in low]))
    return swaps


def halving_order(head_count):
    flips = [0]
    bit = head_count // 2
    while bit >= 1:
        flips = [f | bit for f in flips] + flips
        bit //= 2
    return tuple(flips)


CHUNKS = (2560, 2560)


def on_device(
    tokens,
    in_sign,
    qkv_codes,
    qkv_scale,
    qkv_sign,
    windows,
    oin_sign,
    out_codes,
    out_scale,
    out_sign,
):
    head_count = lax.axis_size("head")
    row_tiles = lax.axis_size("height")
    row_place = lax.axis_index("height")
    head_place = lax.axis_index("head").astype(jnp.int32)
    top = head_count // 2
    place = jnp.stack([head_place, row_place.astype(jnp.int32)])
    low_bits = [1 << b for b in range(top.bit_length() - 1)]

    own, early = turn(place, tokens[0], in_sign)
    half_rows = early.shape[0]
    early = swap(early, top)
    near = {0: own}
    for bit in low_bits:
        for flip in list(near):
            near[flip ^ bit] = swap(near[flip], bit)
    codes = jnp.transpose(qkv_codes, (1, 0, 2))
    near_flips = tuple(sorted(near))
    far_flips = tuple(flip ^ top for flip in near_flips)
    sums, words, late = prepare(
        place, near_flips, far_flips, [near[flip] for flip in near_flips], codes
    )
    late = swap(late, top)
    swaps = row_swaps(row_tiles)
    ending = [qkv_scale, qkv_sign]
    every = tuple(range(len(far_flips)))
    halves, key_values, moved, gates = [], [], [], []
    for half, first_row in ((early, 0), (late, half_rows)):
        shards = {top: tie(half, *gates, sums)}
        for bit in low_bits:
            for flip in list(shards):
                shards[flip ^ bit] = swap(shards[flip], bit)
        shards = [shards[flip] for flip in far_flips]
        partial = project(
            (1, 2), first_row, [shards[:-1]], every[:-1], sums, words, None, 4 * 10**9
        )
        key_value = project((1, 2), 0, [shards[-1:]], every[-1:], partial, words, ending)
        moved.append([lax.ppermute(key_value, "height", pairs) for _, _, pairs in swaps])
        halves.append(shards)
        key_values.append(key_value)
        gates.append(gate(key_value))
    queries = [project((0,), 0, halves, every, sums, words, ending, 4 * 10**9)]
    out_weights = unpack_out(out_codes, key_values[1])

    listed = jnp.transpose(windows, (1, 0, 2))
    late_rows = own.shape[0] - half_rows
    own_keys = ((None, 0, half_rows), (None, half_rows, late_rows))
    early_keys = tuple(((by, odd), 0, half_rows) for by, odd, _ in swaps)
    late_keys = tuple(((by, odd), half_rows, late_rows) for by, odd, _ in swaps)
    running = attend(place, listed, queries, key_values, own_keys, None, None)
    running = attend(place, listed, queries, moved[0], early_keys, running, None)
    rotated = attend(
        place,
        listed,
        queries,
        moved[1],
        late_keys,
        running,
        (oin_sign, halving_order(head_count)),
    )

    bits = low_bits + [top]
    scale_rows = out_scale.reshape(-1, HAD)
    sign_rows = out_sign.reshape(-1, HAD)
    pairs, sums_sent = [], []
    first = 0
    for columns in CHUNKS:
        part, keep = out_project(rotated, out_weights, scale_rows, first, columns)
        if sums_sent:
            part = tie(part, sums_sent[-1])
        for bit in bits:
            more = swap(part, bit)
            if bit == top:
                break
            total = keep.astype(f32) + more.astype(f32)
            half = total.shape[0] // 2
            part, keep = total[:half].astype(bf16), total[half:]
            sums_sent.append(part)
        pairs.append((keep, more))
        first += columns
    base = finish(pairs[:-1], sign_rows, 0, None)
    return finish(pairs[-1:], sign_rows, D - CHUNKS[-1], base)[None]


def solution(mesh):
    return jax.shard_map(
        on_device,
        mesh=mesh,
        in_specs=(
            P(("clip", "height"), None, "head"),
            P(),
            P(None, None, "head"),
            P(None, "head"),
            P(None, "head"),
            P(("clip", "height"), None, None),
            P("head"),
            P("head", None),
            P(),
            P(),
        ),
        out_specs=P(("clip", "height"), "head", None),
        check_vma=False,
    )
```

```python
import functools

import jax
import jax.numpy as jnp
import numpy as np
from jax import lax
from jax.experimental import pallas as pl
from jax.experimental.pallas import tpu as pltpu
from jax.sharding import PartitionSpec as P

D = 5120
HD = 128
HEADS = 24
HAD = 128
TILE = 64
HROWS = 4
WTILES = 3
PLANES = 8
WORDS = HAD // PLANES
QKV_ORDER = "half"
OUT_ORDER = "byte"

epsilon = 1e-06
f32 = jnp.float32
bf16 = jnp.bfloat16
VMEM = pl.BlockSpec(memory_space=pltpu.VMEM)
SMEM = pl.BlockSpec(memory_space=pltpu.SMEM)
ANY = pl.BlockSpec(memory_space=pl.ANY)
HBM = pl.BlockSpec(memory_space=pltpu.HBM)


def shape_of(shape, dtype):
    return jax.ShapeDtypeStruct(tuple(shape), dtype)


def in_hbm(array):
    return pltpu.with_memory_space_constraint(array, pltpu.HBM)


def call(body, out_shape, in_specs, args, name, out_specs=None, megabytes=16, flops=1, **more):
    if out_specs is None:
        out_specs = jax.tree.map(lambda _: VMEM, out_shape)
    return pl.pallas_call(
        body,
        out_shape=out_shape,
        in_specs=in_specs,
        out_specs=out_specs,
        compiler_params=pltpu.CompilerParams(vmem_limit_bytes=megabytes * 2**20),
        cost_estimate=pl.CostEstimate(flops=flops, bytes_accessed=1, transcendentals=0),
        name=name,
        **more,
    )(*args)


def lanes():
    return lax.broadcasted_iota(jnp.int32, (HAD, HAD), 1)


def hadamard(order):
    row = lax.broadcasted_iota(jnp.int32, (HAD, HAD), 0)
    column = lanes()
    word = PLANES * (column & (WORDS - 1))
    if order == "half":
        column = word + column // WORDS
    if order == "byte":
        column = word + column // (2 * WORDS) + (PLANES // 2) * ((column // WORDS) & 1)
    shared = row & column
    shared = shared ^ (shared >> 4)
    shared = shared ^ (shared >> 2)
    shared = shared ^ (shared >> 1)
    return (1 - 2 * (shared & 1)).astype(f32).astype(bf16)


def double_hadamard():
    plain = hadamard("plain")
    return jnp.concatenate([plain, plain], 0)


def plane_power(base, order):
    lane = lax.broadcasted_iota(jnp.int32, (1, HAD), 1)
    if order == "half":
        power = jnp.minimum(lane // WORDS, PLANES - 2)
    else:
        power = jnp.minimum(lane // (2 * WORDS), PLANES // 2 - 2)
    value = jnp.where(power & 1 == 1, base, 1.0)
    value = value * jnp.where(power & 2 == 2, base**2, 1.0)
    return value * jnp.where(power & 4 == 4, base**4, 1.0)


def turn_factor(order):
    return plane_power(0.25, order) * np.float32(HAD ** (-0.5))


def signed(sign_bits):
    return (2 * sign_bits - 1).astype(f32)


def pieces_of(words, order):
    if order == "half":
        packed = words.astype(jnp.int16)
        masked = [packed & jnp.int16(3 << (2 * k)) for k in range(PLANES - 1)]
        masked.append((words >> 2).astype(jnp.int16) & jnp.int16(3 << (2 * PLANES - 4)))
    else:
        pair = jnp.concatenate([words & 255, words >> 8], 0)
        packed = pair.astype(jnp.int8)
        masked = [packed & jnp.int8(3 << (2 * k)) for k in range(PLANES // 2 - 1)]
        masked.append((pair >> 2).astype(jnp.int8) & jnp.int8(3 << (PLANES - 4)))
    return [piece.astype(bf16) for piece in masked]


def decode(words, order):
    blocks = []
    for first in range(0, words.shape[0], WORDS):
        blocks += pieces_of(words[first : first + WORDS], order)
    return jnp.concatenate(blocks, 0)


def row_correction(row_list, order):
    factor_row = plane_power(4.0, order) * 1.5
    total = None
    for rows in row_list:
        for first in range(0, rows.shape[1], HAD):
            term = rows[:, first : first + HAD].astype(f32)
            total = term if total is None else total + term
    return jnp.sum(total * factor_row, axis=1, keepdims=True)


def rotate_halves(values, doubled):
    high = values.astype(bf16)
    low = (values - high.astype(f32)).astype(bf16)
    return jnp.dot(jnp.concatenate([high, low], 1), doubled, preferred_element_type=f32)


def tile_width(columns):
    return columns


def early_rows(rows):
    return rows * 7 // 12 // WORDS * WORDS


def turn_kernel(place_ref, x_hbm, sign_hbm, own_ref, send_ref, x_ref, sign_ref, sems):
    copies = [
        pltpu.make_async_copy(x_hbm, x_ref, sems.at[0]),
        pltpu.make_async_copy(sign_hbm, sign_ref, sems.at[1]),
    ]
    for copy in copies:
        copy.start()
    matrix = hadamard(QKV_ORDER)
    factor = turn_factor(QKV_ORDER)
    for copy in copies:
        copy.wait()
    blocks = x_ref.shape[1] // HAD
    first = place_ref[0] * blocks
    for b in range(blocks):
        cols = slice(b * HAD, (b + 1) * HAD)
        sign_row = signed(sign_ref[pl.ds(first + b, 1), :])
        flipped = (x_ref[:, cols].astype(f32) * sign_row).astype(bf16)
        turned = jnp.dot(flipped, matrix, preferred_element_type=f32)
        turned = (turned * factor).astype(bf16)
        own_ref[:, cols] = turned
        send_ref[:, cols] = turned[: send_ref.shape[0]]


def turn(place, own_tokens, in_sign):
    sign_rows = in_sign.reshape(-1, HAD)
    rows, inner = own_tokens.shape
    return call(
        turn_kernel,
        (shape_of((rows, inner), bf16), shape_of((early_rows(rows), inner), bf16)),
        [SMEM, HBM, HBM],
        (place, in_hbm(own_tokens), in_hbm(sign_rows)),
        "turn",
        scratch_shapes=[
            pltpu.VMEM(own_tokens.shape, bf16),
            pltpu.VMEM(sign_rows.shape, jnp.int32),
            pltpu.SemaphoreType.DMA((2,)),
        ],
    )


def tie(array, *after):
    return call(
        lambda *refs: None,
        shape_of(array.shape, array.dtype),
        [ANY] * (1 + len(after)),
        (array, *after),
        "tie",
        out_specs=ANY,
        input_output_aliases={0: 0},
    )


def gate(array):
    def body(array_ref, out_ref):
        out_ref[...] = jnp.zeros_like(out_ref)

    return call(body, shape_of((8, HAD), f32), [ANY], (array,), "gate", flops=4 * 10**9)


def prepare_kernel(near, far, place_ref, *rest):
    shard_refs = rest[: len(near)]
    codes_hbm, sums_ref, far_ref, late_ref, near_ref, sems = rest[len(near) :]
    words, columns = near_ref.shape[2:]

    def fetch(position, kind):
        flip = (near + far)[position]
        first = pl.multiple_of((place_ref[0] ^ flip) * words, WORDS)
        there = position - len(near)
        target = near_ref.at[position, kind] if there < 0 else far_ref.at[there, kind]
        return pltpu.make_async_copy(
            codes_hbm.at[kind, pl.ds(first, words), :], target, sems.at[position, kind]
        )

    for kind in range(3):
        for position in range(len(near)):
            fetch(position, kind).start()
    for position in range(len(near), len(near + far)):
        for kind in range(3):
            fetch(position, kind).start()
    fix = row_correction([ref[...] for ref in shard_refs], QKV_ORDER)
    width = tile_width(columns)
    late_ref[...] = shard_refs[0][shard_refs[0].shape[0] - late_ref.shape[0] :, :]

    def every_shard(kind, carry):
        for position in range(len(near)):
            fetch(position, kind).wait()
        for first in range(0, columns, width):
            cols = slice(first, first + width)
            total = -fix
            for position, ref in enumerate(shard_refs):
                weights = decode(near_ref[position, kind, :, cols], QKV_ORDER)
                total = total + jnp.dot(ref[...], weights, preferred_element_type=f32)
            sums_ref[kind, :, cols] = total
        return carry

    lax.fori_loop(0, 3, every_shard, 0)
    for position in range(len(near), len(near + far)):
        for kind in range(3):
            fetch(position, kind).wait()


def prepare(place, near, far, shards, codes):
    rows, inner = shards[0].shape
    columns = codes.shape[2]
    words = inner // PLANES
    return call(
        functools.partial(prepare_kernel, near, far),
        (
            shape_of((3, rows, columns), f32),
            shape_of((len(far), 3, words, columns), jnp.int32),
            shape_of((rows - early_rows(rows), inner), bf16),
        ),
        [SMEM] + [VMEM] * len(near) + [HBM],
        (place, *shards, in_hbm(codes)),
        "prepare",
        scratch_shapes=[
            pltpu.VMEM((len(near), 3, words, columns), jnp.int32),
            pltpu.SemaphoreType.DMA((len(near + far), 3)),
        ],
    )


def project_kernel(kinds, first_row, groups, positions, whole, ending, *rest):
    count = len(positions)
    shard_refs = rest[: groups * count]
    sums_ref, words_ref = rest[groups * count : groups * count + 2]
    if ending:
        scale_ref, sign_ref = rest[groups * count + 2 : groups * count + 4]
    out_ref = rest[-1]
    columns = sums_ref.shape[2]
    width = tile_width(columns)
    shards = []
    for place in range(count):
        parts = [shard_refs[g * count + place][...] for g in range(groups)]
        shards.append(parts[0] if groups == 1 else jnp.concatenate(parts, 0))
    fix = row_correction(shards, QKV_ORDER)
    row_count = shards[0].shape[0]
    rows = slice(first_row, first_row + row_count)
    doubled = double_hadamard()
    ones = jnp.ones((HD, HD), bf16)
    for place, kind in enumerate(kinds):
        heads = []
        for first in range(0, columns, width):
            cols = slice(first, first + width)
            part = (sums_ref[kind, rows, cols] if whole else sums_ref[place, :, cols]) - fix
            for shard, position in zip(shards, positions):
                weights = decode(words_ref[position, kind, :, cols], QKV_ORDER)
                part = part + jnp.dot(shard, weights, preferred_element_type=f32)
            if not ending:
                out_ref[place, :, cols] = part
                continue
            for lane in range(0, width, HD):
                at = slice(first + lane, first + lane + HD)
                scale_row = scale_ref[kind : kind + 1, at] * np.float32(D ** (-0.5))
                heads.append(part[:, lane : lane + HD] * scale_row)
        if not ending:
            continue
        mixed = rotate_halves(jnp.concatenate(heads, 0), doubled)
        signs = []
        for head in range(len(heads)):
            sign_row = sign_ref[kind : kind + 1, head * HD : (head + 1) * HD]
            sign_row = signed(sign_row) * np.float32(HAD ** (-0.5))
            signs.append(mixed[head * row_count : (head + 1) * row_count] * sign_row)
        if kind != 2:
            square = jnp.concatenate([(part * part).astype(bf16) for part in signs], 0)
            mean = jnp.dot(square, ones, preferred_element_type=f32) * (1.0 / HD)
            factor = lax.rsqrt(mean + epsilon)
            signs = [
                part * factor[head * row_count : (head + 1) * row_count]
                for head, part in enumerate(signs)
            ]
        for head, part in enumerate(signs):
            out_ref[place, :, head * HD : (head + 1) * HD] = part.astype(bf16)


def project(kinds, first_row, groups, positions, sums, words, ending, flops=1):
    inner = groups[0][0].shape[1]
    columns = sums.shape[2]
    row_count = sum(group[0].shape[0] for group in groups)
    whole = sums.shape[0] == 3
    args = [shard for group in groups for shard in group] + [sums, words]
    own_args = len(args) + 2
    if ending is not None:
        args += ending
    return call(
        functools.partial(
            project_kernel, kinds, first_row, len(groups), positions, whole, ending is not None
        ),
        shape_of((len(kinds), row_count, columns), f32 if ending is None else bf16),
        [VMEM] * min(len(args), own_args) + [ANY] * max(len(args) - own_args, 0),
        args,
        "project",
        flops=flops,
    )


def near_row(row, swap_pair):
    if swap_pair is None:
        return row
    by, odd = swap_pair
    return jnp.where(lax.rem(row // by, 2) == odd, row + by, row - by)


def window_mask(place_ref, windows_ref, segments, row_count):
    lane = lax.broadcasted_iota(jnp.int32, (1, sum(rows for _, _, rows in segments)), 1)
    ids, base = None, 0
    for swap_pair, first, rows in segments:
        tile = (lane + (first - base)) // TILE
        ids_here = near_row(place_ref[1], swap_pair) * WTILES + tile
        ids = ids_here if ids is None else jnp.where(lane >= base, ids_here, ids)
        base += rows
    masks = []
    for tile in range(row_count // TILE):
        hit = jnp.zeros(lane.shape, f32)
        for entry in range(windows_ref.shape[2]):
            hit = jnp.where(ids == windows_ref[tile, 0, entry], 1.0, hit)
        masks.append(jnp.broadcast_to(hit, (TILE, lane.shape[1])))
    return jnp.concatenate(masks, 0)


def attend_kernel(
    segments, halves, blocks, has_sum, last, share_order, place_ref, windows_ref, *rest
):
    rest = list(rest)
    q_refs = [rest.pop(0) for _ in range(halves)]
    kv_refs = [rest.pop(0) for _ in range(blocks)]
    sum_ref = rest.pop(0) if has_sum else None
    if last:
        oin_ref, out_ref, rotated_ref = rest
    else:
        (out_ref,) = rest
    columns = q_refs[0].shape[2]
    row_count = sum(ref.shape[1] for ref in q_refs)
    heads = [slice(head, head + HD) for head in range(0, columns, HD)]
    mask = window_mask(place_ref, windows_ref, segments, row_count)
    scores = []
    for at in heads:
        keys = jnp.concatenate([ref[0, :, at] for ref in kv_refs], 0)
        scores.append(
            lax.dot_general(
                jnp.concatenate([ref[0, :, at] for ref in q_refs], 0),
                keys,
                (((1,), (1,)), ((), ())),
                preferred_element_type=f32,
            )
        )
    weights = [
        (jnp.exp(score * np.float32(HD ** (-0.5))) * mask).astype(bf16) for score in scores
    ]
    totals = []
    for head, at in enumerate(heads):
        values = jnp.concatenate([ref[1, :, at] for ref in kv_refs], 0)
        values = jnp.concatenate([values, jnp.ones_like(values)], 1)
        total = jnp.dot(weights[head], values, preferred_element_type=f32)
        if has_sum:
            total = total + sum_ref[head]
        totals.append(total)
    if not last:
        for head, total in enumerate(totals):
            out_ref[head] = total
        return
    matrix = hadamard(OUT_ORDER)
    factor = turn_factor(OUT_ORDER)
    for head, at in enumerate(heads):
        attended = (totals[head][:, :HD] / totals[head][:, HD:]).astype(bf16)
        sign_row = signed(oin_ref[head : head + 1, :])
        flipped = (attended.astype(f32) * sign_row).astype(bf16)
        rotated_ref[:, at] = jnp.dot(flipped, matrix, preferred_element_type=f32) * factor
    share = row_count // len(share_order)
    pieces = []
    for flip in share_order:
        owner = place_ref[0] ^ flip
        pieces.append(rotated_ref[pl.ds(pl.multiple_of(owner * share, 8), share), :])
    out_ref[...] = jnp.concatenate(pieces, 0).astype(bf16)


def attend(place, windows, queries, blocks, segments, running, ending):
    columns = queries[0].shape[2]
    row_count = sum(part.shape[1] for part in queries)
    args = [place, windows, *queries, *blocks]
    if running is not None:
        args.append(running)
    scratch, share_order = [], None
    if ending is None:
        out_shape = shape_of((columns // HD, row_count, 2 * HD), f32)
    else:
        oin_sign, share_order = ending
        args.append(oin_sign.reshape(-1, HAD))
        out_shape = shape_of((row_count, columns), bf16)
        scratch = [pltpu.VMEM((row_count, columns), f32)]
    return call(
        functools.partial(
            attend_kernel,
            segments,
            len(queries),
            len(blocks),
            running is not None,
            ending is not None,
            share_order,
        ),
        out_shape,
        [SMEM] * 2 + [VMEM] * (len(args) - 2),
        args,
        "attend",
        scratch_shapes=scratch,
    )


def unpack_out_kernel(codes_ref, after_ref, weights_ref):
    for first in range(0, codes_ref.shape[0], WORDS):

        def some(step, carry):
            cols = pl.ds(pl.multiple_of(step * 512, 512), 512)
            at = first * PLANES
            for piece in pieces_of(codes_ref[first : first + WORDS, cols], OUT_ORDER):
                weights_ref[at : at + piece.shape[0], cols] = piece
                at += piece.shape[0]
            return carry

        lax.fori_loop(0, codes_ref.shape[1] // 512, some, 0)


def unpack_out(codes, after):
    words, columns = codes.shape
    return call(
        unpack_out_kernel,
        shape_of((words * PLANES, columns), bf16),
        [VMEM, ANY],
        (codes, after),
        "unpack_out",
    )


def out_kernel(first, rotated_ref, weights_ref, scale_ref, send_ref, keep_ref):
    rows = rotated_ref[...]
    fix = row_correction([rows], OUT_ORDER)
    half, columns = send_ref.shape
    width = 512
    for at in range(0, columns, width):
        cols = slice(first + at, first + at + width)
        part = jnp.dot(rows, weights_ref[:, cols], preferred_element_type=f32) - fix
        for lane in range(0, width, HAD):
            place = (first + at + lane) // HAD
            scale_row = scale_ref[place : place + 1, :] * np.float32((HEADS * HD) ** (-0.5))
            done = (part[:, lane : lane + HAD] * scale_row).astype(bf16)
            send_ref[:, at + lane : at + lane + HAD] = done[:half]
            keep_ref[:, at + lane : at + lane + HAD] = done[half:]


def out_project(rotated, weights, scale_rows, first, columns):
    row_count, inner = rotated.shape
    result = shape_of((row_count // 2, columns), bf16)
    return call(
        functools.partial(out_kernel, first),
        (result, result),
        [VMEM] * 3,
        (rotated, weights, scale_rows),
        "out_project",
    )


def finish_kernel(chunks, first, sign_ref, *rest):
    out_hbm, done_ref, sems = rest[-3:]
    doubled = double_hadamard()
    copies = []
    for chunk in range(chunks):
        keep_ref, more_ref = rest[2 * chunk : 2 * chunk + 2]
        share, columns = keep_ref.shape
        totals = keep_ref[...].astype(f32) + more_ref[...].astype(f32)
        blocks = [totals[:, at : at + HAD] for at in range(0, columns, HAD)]
        turned = rotate_halves(jnp.concatenate(blocks, 0), doubled)
        for block in range(len(blocks)):
            place = first // HAD + block
            sign_row = signed(sign_ref[place : place + 1, :]) * np.float32(HAD ** (-0.5))
            done = turned[block * share : (block + 1) * share] * sign_row
            done_ref[:, place * HAD : (place + 1) * HAD] = done.astype(bf16)
        cols = pl.ds(first, columns)
        copies.append(
            pltpu.make_async_copy(done_ref.at[:, cols], out_hbm.at[:, cols], sems.at[chunk])
        )
        copies[-1].start()
        first += columns
    for copy in copies:
        copy.wait()


def finish(pairs, sign_rows, first, base):
    share = pairs[0][0].shape[0]
    args = [sign_rows] + [array for pair in pairs for array in pair]
    in_specs = [VMEM] * len(args)
    aliases = {}
    if base is not None:
        aliases = {len(args): 0}
        args.append(base)
        in_specs.append(HBM)
    return call(
        functools.partial(finish_kernel, len(pairs), first),
        shape_of((share, D), bf16),
        in_specs,
        args,
        "finish",
        out_specs=HBM,
        scratch_shapes=[pltpu.VMEM((share, D), bf16), pltpu.SemaphoreType.DMA((len(pairs),))],
        input_output_aliases=aliases,
    )


def swap(shard, bit):
    peers = lax.axis_size("head")
    return lax.ppermute(shard, "head", [(i, i ^ bit) for i in range(peers)])


def row_swaps(row_tiles):
    swaps = []
    for by in (1, 3, 4, 5) if row_tiles > HROWS else (1,):
        for odd in (1, 0):
            low = [i for i in range(row_tiles - by) if (i // by) % 2 == odd]
            swaps.append((by, odd, [(i, i + by) for i in low] + [(i + by, i) for i in low]))
    return swaps


def halving_order(head_count):
    flips = [0]
    bit = head_count // 2
    while bit >= 1:
        flips = [f | bit for f in flips] + flips
        bit //= 2
    return tuple(flips)


CHUNKS = (2560, 2560)


def on_device(
    tokens,
    in_sign,
    qkv_codes,
    qkv_scale,
    qkv_sign,
    windows,
    oin_sign,
    out_codes,
    out_scale,
    out_sign,
):
    head_count = lax.axis_size("head")
    row_tiles = lax.axis_size("height")
    row_place = lax.axis_index("height")
    head_place = lax.axis_index("head").astype(jnp.int32)
    top = head_count // 2
    place = jnp.stack([head_place, row_place.astype(jnp.int32)])
    low_bits = [1 << b for b in range(top.bit_length() - 1)]

    own, early = turn(place, tokens[0], in_sign)
    half_rows = early.shape[0]
    early = swap(early, top)
    near = {0: own}
    for bit in low_bits:
        for flip in list(near):
            near[flip ^ bit] = swap(near[flip], bit)
    codes = jnp.transpose(qkv_codes, (1, 0, 2))
    near_flips = tuple(sorted(near))
    far_flips = tuple(flip ^ top for flip in near_flips)
    sums, words, late = prepare(
        place, near_flips, far_flips, [near[flip] for flip in near_flips], codes
    )
    late = swap(late, top)
    swaps = row_swaps(row_tiles)
    ending = [qkv_scale, qkv_sign]
    every = tuple(range(len(far_flips)))
    halves, key_values, moved, gates = [], [], [], []
    for half, first_row in ((early, 0), (late, half_rows)):
        shards = {top: tie(half, *gates, sums)}
        for bit in low_bits:
            for flip in list(shards):
                shards[flip ^ bit] = swap(shards[flip], bit)
        shards = [shards[flip] for flip in far_flips]
        partial = project(
            (1, 2), first_row, [shards[:-1]], every[:-1], sums, words, None, 4 * 10**9
        )
        key_value = project((1, 2), 0, [shards[-1:]], every[-1:], partial, words, ending)
        moved.append([lax.ppermute(key_value, "height", pairs) for _, _, pairs in swaps])
        halves.append(shards)
        key_values.append(key_value)
        gates.append(gate(key_value))
    queries = [project((0,), 0, halves, every, sums, words, ending, 4 * 10**9)]
    out_weights = unpack_out(out_codes, key_values[1])

    listed = jnp.transpose(windows, (1, 0, 2))
    late_rows = own.shape[0] - half_rows
    own_keys = ((None, 0, half_rows), (None, half_rows, late_rows))
    early_keys = tuple(((by, odd), 0, half_rows) for by, odd, _ in swaps)
    late_keys = tuple(((by, odd), half_rows, late_rows) for by, odd, _ in swaps)
    running = attend(place, listed, queries, key_values, own_keys, None, None)
    running = attend(place, listed, queries, moved[0], early_keys, running, None)
    running = attend(place, listed, queries, moved[1][1:], late_keys[1:], running, None)
    rotated = attend(
        place,
        listed,
        queries,
        moved[1][:1],
        late_keys[:1],
        running,
        (oin_sign, halving_order(head_count)),
    )

    bits = low_bits + [top]
    scale_rows = out_scale.reshape(-1, HAD)
    sign_rows = out_sign.reshape(-1, HAD)
    pairs, sums_sent = [], []
    first = 0
    for columns in CHUNKS:
        part, keep = out_project(rotated, out_weights, scale_rows, first, columns)
        if sums_sent:
            part = tie(part, sums_sent[-1])
        for bit in bits:
            more = swap(part, bit)
            if bit == top:
                break
            total = keep.astype(f32) + more.astype(f32)
            half = total.shape[0] // 2
            part, keep = total[:half].astype(bf16), total[half:]
            sums_sent.append(part)
        pairs.append((keep, more))
        first += columns
    base = finish(pairs[:-1], sign_rows, 0, None)
    return finish(pairs[-1:], sign_rows, D - CHUNKS[-1], base)[None]


def solution(mesh):
    return jax.shard_map(
        on_device,
        mesh=mesh,
        in_specs=(
            P(("clip", "height"), None, "head"),
            P(),
            P(None, None, "head"),
            P(None, "head"),
            P(None, "head"),
            P(("clip", "height"), None, None),
            P("head"),
            P("head", None),
            P(),
            P(),
        ),
        out_specs=P(("clip", "height"), "head", None),
        check_vma=False,
    )
```

```python
import functools

import jax
import jax.numpy as jnp
import numpy as np
from jax import lax
from jax.experimental import pallas as pl
from jax.experimental.pallas import tpu as pltpu
from jax.sharding import PartitionSpec as P

D = 5120
HD = 128
HEADS = 24
HAD = 128
TILE = 64
HROWS = 4
WTILES = 3
PLANES = 8
WORDS = HAD // PLANES
QKV_ORDER = "half"
OUT_ORDER = "byte"

epsilon = 1e-06
f32 = jnp.float32
bf16 = jnp.bfloat16
VMEM = pl.BlockSpec(memory_space=pltpu.VMEM)
SMEM = pl.BlockSpec(memory_space=pltpu.SMEM)
ANY = pl.BlockSpec(memory_space=pl.ANY)
HBM = pl.BlockSpec(memory_space=pltpu.HBM)


def shape_of(shape, dtype):
    return jax.ShapeDtypeStruct(tuple(shape), dtype)


def in_hbm(array):
    return pltpu.with_memory_space_constraint(array, pltpu.HBM)


def call(body, out_shape, in_specs, args, name, out_specs=None, megabytes=16, flops=1, **more):
    if out_specs is None:
        out_specs = jax.tree.map(lambda _: VMEM, out_shape)
    return pl.pallas_call(
        body,
        out_shape=out_shape,
        in_specs=in_specs,
        out_specs=out_specs,
        compiler_params=pltpu.CompilerParams(vmem_limit_bytes=megabytes * 2**20),
        cost_estimate=pl.CostEstimate(flops=flops, bytes_accessed=1, transcendentals=0),
        name=name,
        **more,
    )(*args)


def lanes():
    return lax.broadcasted_iota(jnp.int32, (HAD, HAD), 1)


def hadamard(order):
    row = lax.broadcasted_iota(jnp.int32, (HAD, HAD), 0)
    column = lanes()
    word = PLANES * (column & (WORDS - 1))
    if order == "half":
        column = word + column // WORDS
    if order == "byte":
        column = word + column // (2 * WORDS) + (PLANES // 2) * ((column // WORDS) & 1)
    shared = row & column
    shared = shared ^ (shared >> 4)
    shared = shared ^ (shared >> 2)
    shared = shared ^ (shared >> 1)
    return (1 - 2 * (shared & 1)).astype(f32).astype(bf16)


def double_hadamard():
    plain = hadamard("plain")
    return jnp.concatenate([plain, plain], 0)


def plane_power(base, order):
    lane = lax.broadcasted_iota(jnp.int32, (1, HAD), 1)
    if order == "half":
        power = jnp.minimum(lane // WORDS, PLANES - 2)
    else:
        power = jnp.minimum(lane // (2 * WORDS), PLANES // 2 - 2)
    value = jnp.where(power & 1 == 1, base, 1.0)
    value = value * jnp.where(power & 2 == 2, base**2, 1.0)
    return value * jnp.where(power & 4 == 4, base**4, 1.0)


def turn_factor(order):
    return plane_power(0.25, order) * np.float32(HAD ** (-0.5))


def signed(sign_bits):
    return (2 * sign_bits - 1).astype(f32)


def pieces_of(words, order):
    if order == "half":
        packed = words.astype(jnp.int16)
        masked = [packed & jnp.int16(3 << (2 * k)) for k in range(PLANES - 1)]
        masked.append((words >> 2).astype(jnp.int16) & jnp.int16(3 << (2 * PLANES - 4)))
    else:
        pair = jnp.concatenate([words & 255, words >> 8], 0)
        packed = pair.astype(jnp.int8)
        masked = [packed & jnp.int8(3 << (2 * k)) for k in range(PLANES // 2 - 1)]
        masked.append((pair >> 2).astype(jnp.int8) & jnp.int8(3 << (PLANES - 4)))
    return [piece.astype(bf16) for piece in masked]


def decode(words, order):
    blocks = []
    for first in range(0, words.shape[0], WORDS):
        blocks += pieces_of(words[first : first + WORDS], order)
    return jnp.concatenate(blocks, 0)


def row_correction(row_list, order):
    factor_row = plane_power(4.0, order) * 1.5
    total = None
    for rows in row_list:
        for first in range(0, rows.shape[1], HAD):
            term = rows[:, first : first + HAD].astype(f32)
            total = term if total is None else total + term
    return jnp.sum(total * factor_row, axis=1, keepdims=True)


def rotate_halves(values, doubled):
    high = values.astype(bf16)
    low = (values - high.astype(f32)).astype(bf16)
    return jnp.dot(jnp.concatenate([high, low], 1), doubled, preferred_element_type=f32)


def early_rows(rows):
    return rows * 7 // 12 // WORDS * WORDS


def turn_kernel(x_hbm, sign_hbm, own_ref, send_ref, x_ref, sign_ref, sems):
    copies = [
        pltpu.make_async_copy(x_hbm, x_ref, sems.at[0]),
        pltpu.make_async_copy(sign_hbm, sign_ref, sems.at[1]),
    ]
    for copy in copies:
        copy.start()
    matrix = hadamard(QKV_ORDER)
    factor = turn_factor(QKV_ORDER)
    for copy in copies:
        copy.wait()
    blocks = x_ref.shape[1] // HAD
    first = lax.axis_index("head") * blocks
    for b in range(blocks):
        cols = slice(b * HAD, (b + 1) * HAD)
        sign_row = signed(sign_ref[pl.ds(first + b, 1), :])
        flipped = (x_ref[:, cols].astype(f32) * sign_row).astype(bf16)
        turned = jnp.dot(flipped, matrix, preferred_element_type=f32)
        turned = (turned * factor).astype(bf16)
        own_ref[:, cols] = turned
        send_ref[:, cols] = turned[: send_ref.shape[0]]


def turn(own_tokens, in_sign):
    sign_rows = in_sign.reshape(-1, HAD)
    rows, inner = own_tokens.shape
    return call(
        turn_kernel,
        (shape_of((rows, inner), bf16), shape_of((early_rows(rows), inner), bf16)),
        [HBM, HBM],
        (in_hbm(own_tokens), in_hbm(sign_rows)),
        "turn",
        scratch_shapes=[
            pltpu.VMEM(own_tokens.shape, bf16),
            pltpu.VMEM(sign_rows.shape, jnp.int32),
            pltpu.SemaphoreType.DMA((2,)),
        ],
    )


def tie(array, *after):
    return call(
        lambda *refs: None,
        shape_of(array.shape, array.dtype),
        [ANY] * (1 + len(after)),
        (array, *after),
        "tie",
        out_specs=ANY,
        input_output_aliases={0: 0},
    )


def gate(array):
    def body(array_ref, out_ref):
        out_ref[...] = jnp.zeros_like(out_ref)

    return call(body, shape_of((8, HAD), f32), [ANY], (array,), "gate", flops=4 * 10**9)


def prepare_kernel(near, far, *rest):
    shard_refs = rest[: len(near)]
    codes_hbm, sums_ref, far_ref, late_ref, near_ref, sems = rest[len(near) :]
    words, columns = near_ref.shape[2:]

    def fetch(position, kind):
        flip = (near + far)[position]
        first = pl.multiple_of((lax.axis_index("head") ^ flip) * words, WORDS)
        there = position - len(near)
        target = near_ref.at[position, kind] if there < 0 else far_ref.at[there, kind]
        return pltpu.make_async_copy(
            codes_hbm.at[kind, pl.ds(first, words), :], target, sems.at[position, kind]
        )

    for kind in range(3):
        for position in range(len(near)):
            fetch(position, kind).start()
    for position in range(len(near), len(near + far)):
        for kind in range(3):
            fetch(position, kind).start()
    fix = row_correction([ref[...] for ref in shard_refs], QKV_ORDER)
    late_ref[...] = shard_refs[0][shard_refs[0].shape[0] - late_ref.shape[0] :, :]

    def every_shard(kind, carry):
        for position in range(len(near)):
            fetch(position, kind).wait()
        total = -fix
        for position, ref in enumerate(shard_refs):
            weights = decode(near_ref[position, kind], QKV_ORDER)
            total = total + jnp.dot(ref[...], weights, preferred_element_type=f32)
        sums_ref[kind] = total
        return carry

    lax.fori_loop(0, 3, every_shard, 0)
    for position in range(len(near), len(near + far)):
        for kind in range(3):
            fetch(position, kind).wait()


def prepare(near, far, shards, codes):
    rows, inner = shards[0].shape
    columns = codes.shape[2]
    words = inner // PLANES
    return call(
        functools.partial(prepare_kernel, near, far),
        (
            shape_of((3, rows, columns), f32),
            shape_of((len(far), 3, words, columns), jnp.int32),
            shape_of((rows - early_rows(rows), inner), bf16),
        ),
        [VMEM] * len(near) + [HBM],
        (*shards, in_hbm(codes)),
        "prepare",
        scratch_shapes=[
            pltpu.VMEM((len(near), 3, words, columns), jnp.int32),
            pltpu.SemaphoreType.DMA((len(near + far), 3)),
        ],
    )


def project_kernel(kinds, first_row, groups, positions, whole, ending, *rest):
    count = len(positions)
    shard_refs = rest[: groups * count]
    sums_ref, words_ref = rest[groups * count : groups * count + 2]
    if ending:
        scale_ref, sign_ref = rest[groups * count + 2 : groups * count + 4]
    out_ref = rest[-1]
    columns = sums_ref.shape[2]
    shards = []
    for place in range(count):
        parts = [shard_refs[g * count + place][...] for g in range(groups)]
        shards.append(parts[0] if groups == 1 else jnp.concatenate(parts, 0))
    fix = row_correction(shards, QKV_ORDER)
    row_count = shards[0].shape[0]
    rows = slice(first_row, first_row + row_count)
    doubled = double_hadamard()
    ones = jnp.ones((HD, HD), bf16)
    for place, kind in enumerate(kinds):
        part = (sums_ref[kind, rows, :] if whole else sums_ref[place]) - fix
        for shard, position in zip(shards, positions):
            weights = decode(words_ref[position, kind], QKV_ORDER)
            part = part + jnp.dot(shard, weights, preferred_element_type=f32)
        if not ending:
            out_ref[place] = part
            continue
        heads = []
        for first in range(0, columns, HD):
            at = slice(first, first + HD)
            scale_row = scale_ref[kind : kind + 1, at] * np.float32(D ** (-0.5))
            heads.append(part[:, at] * scale_row)
        mixed = rotate_halves(jnp.concatenate(heads, 0), doubled)
        signs = []
        for head in range(len(heads)):
            sign_row = sign_ref[kind : kind + 1, head * HD : (head + 1) * HD]
            sign_row = signed(sign_row) * np.float32(HAD ** (-0.5))
            signs.append(mixed[head * row_count : (head + 1) * row_count] * sign_row)
        if kind != 2:
            square = jnp.concatenate([(part * part).astype(bf16) for part in signs], 0)
            mean = jnp.dot(square, ones, preferred_element_type=f32) * (1.0 / HD)
            factor = lax.rsqrt(mean + epsilon)
            signs = [
                part * factor[head * row_count : (head + 1) * row_count]
                for head, part in enumerate(signs)
            ]
        for head, part in enumerate(signs):
            out_ref[place, :, head * HD : (head + 1) * HD] = part.astype(bf16)


def project(kinds, first_row, groups, positions, sums, words, ending, flops=1):
    inner = groups[0][0].shape[1]
    columns = sums.shape[2]
    row_count = sum(group[0].shape[0] for group in groups)
    whole = sums.shape[0] == 3
    args = [shard for group in groups for shard in group] + [sums, words]
    own_args = len(args) + 2
    if ending is not None:
        args += ending
    return call(
        functools.partial(
            project_kernel, kinds, first_row, len(groups), positions, whole, ending is not None
        ),
        shape_of((len(kinds), row_count, columns), f32 if ending is None else bf16),
        [VMEM] * min(len(args), own_args) + [ANY] * max(len(args) - own_args, 0),
        args,
        "project",
        flops=flops,
    )


def near_row(row, swap_pair):
    if swap_pair is None:
        return row
    by, odd = swap_pair
    return jnp.where(lax.rem(row // by, 2) == odd, row + by, row - by)


def masks_kernel(steps, windows_ref, after_ref, *mask_refs):
    row = lax.axis_index("height")
    for segments, mask_ref in zip(steps, mask_refs):
        lane = lax.broadcasted_iota(jnp.int32, (1, mask_ref.shape[1]), 1)
        ids, base = None, 0
        for swap_pair, first, rows in segments:
            tile = (lane + (first - base)) // TILE
            ids_here = near_row(row, swap_pair) * WTILES + tile
            ids = ids_here if ids is None else jnp.where(lane >= base, ids_here, ids)
            base += rows
        for tile in range(mask_ref.shape[0]):
            hit = jnp.zeros(lane.shape, f32)
            for entry in range(windows_ref.shape[2]):
                hit = jnp.where(ids == windows_ref[tile, 0, entry], 1.0, hit)
            mask_ref[tile : tile + 1, :] = hit


def make_masks(windows, after, steps):
    listed = jnp.transpose(windows, (1, 0, 2))
    shapes = [
        shape_of((listed.shape[0], sum(rows for _, _, rows in segments)), f32) for segments in steps
    ]
    return call(
        functools.partial(masks_kernel, steps), shapes, [SMEM, ANY], (listed, after), "window_masks"
    )


def attend_kernel(halves, blocks, has_sum, last, share_order, *rest):
    rest = list(rest)
    q_refs = [rest.pop(0) for _ in range(halves)]
    kv_refs = [rest.pop(0) for _ in range(blocks)]
    mask_ref = rest.pop(0)
    sum_ref = rest.pop(0) if has_sum else None
    if last:
        oin_ref, out_ref, rotated_ref = rest
    else:
        (out_ref,) = rest
    columns = q_refs[0].shape[2]
    row_count = sum(ref.shape[1] for ref in q_refs)
    heads = [slice(head, head + HD) for head in range(0, columns, HD)]
    mask = jnp.concatenate(
        [
            jnp.broadcast_to(mask_ref[t : t + 1, :], (TILE, mask_ref.shape[1]))
            for t in range(row_count // TILE)
        ],
        0,
    )
    scores = []
    for at in heads:
        keys = jnp.concatenate([ref[0, :, at] for ref in kv_refs], 0)
        scores.append(
            lax.dot_general(
                jnp.concatenate([ref[0, :, at] for ref in q_refs], 0),
                keys,
                (((1,), (1,)), ((), ())),
                preferred_element_type=f32,
            )
        )
    weights = [
        (jnp.exp(score * np.float32(HD ** (-0.5))) * mask).astype(bf16) for score in scores
    ]
    totals = []
    for head, at in enumerate(heads):
        values = jnp.concatenate([ref[1, :, at] for ref in kv_refs], 0)
        values = jnp.concatenate([values, jnp.ones_like(values)], 1)
        total = jnp.dot(weights[head], values, preferred_element_type=f32)
        if has_sum:
            total = total + sum_ref[head]
        totals.append(total)
    if not last:
        for head, total in enumerate(totals):
            out_ref[head] = total
        return
    matrix = hadamard(OUT_ORDER)
    factor = turn_factor(OUT_ORDER)
    for head, at in enumerate(heads):
        attended = (totals[head][:, :HD] / totals[head][:, HD:]).astype(bf16)
        sign_row = signed(oin_ref[head : head + 1, :])
        flipped = (attended.astype(f32) * sign_row).astype(bf16)
        rotated_ref[:, at] = jnp.dot(flipped, matrix, preferred_element_type=f32) * factor
    share = row_count // len(share_order)
    pieces = []
    for flip in share_order:
        owner = lax.axis_index("head") ^ flip
        pieces.append(rotated_ref[pl.ds(pl.multiple_of(owner * share, 8), share), :])
    out_ref[...] = jnp.concatenate(pieces, 0).astype(bf16)


def attend(queries, blocks, mask, running, ending):
    columns = queries[0].shape[2]
    row_count = sum(part.shape[1] for part in queries)
    args = [*queries, *blocks, mask]
    if running is not None:
        args.append(running)
    scratch, share_order = [], None
    if ending is None:
        out_shape = shape_of((columns // HD, row_count, 2 * HD), f32)
    else:
        oin_sign, share_order = ending
        args.append(oin_sign.reshape(-1, HAD))
        out_shape = shape_of((row_count, columns), bf16)
        scratch = [pltpu.VMEM((row_count, columns), f32)]
    return call(
        functools.partial(
            attend_kernel,
            len(queries),
            len(blocks),
            running is not None,
            ending is not None,
            share_order,
        ),
        out_shape,
        [VMEM] * len(args),
        args,
        "attend",
        scratch_shapes=scratch,
    )


def unpack_out_kernel(codes_ref, after_ref, weights_ref):
    for first in range(0, codes_ref.shape[0], WORDS):

        def some(step, carry):
            cols = pl.ds(pl.multiple_of(step * 512, 512), 512)
            at = first * PLANES
            for piece in pieces_of(codes_ref[first : first + WORDS, cols], OUT_ORDER):
                weights_ref[at : at + piece.shape[0], cols] = piece
                at += piece.shape[0]
            return carry

        lax.fori_loop(0, codes_ref.shape[1] // 512, some, 0)


def unpack_out(codes, after):
    words, columns = codes.shape
    return call(
        unpack_out_kernel,
        shape_of((words * PLANES, columns), bf16),
        [VMEM, ANY],
        (codes, after),
        "unpack_out",
    )


def out_kernel(first, rotated_ref, weights_ref, scale_ref, send_ref, keep_ref):
    rows = rotated_ref[...]
    fix = row_correction([rows], OUT_ORDER)
    half, columns = send_ref.shape
    width = 512
    for at in range(0, columns, width):
        cols = slice(first + at, first + at + width)
        part = jnp.dot(rows, weights_ref[:, cols], preferred_element_type=f32) - fix
        for lane in range(0, width, HAD):
            place = (first + at + lane) // HAD
            scale_row = scale_ref[place : place + 1, :] * np.float32((HEADS * HD) ** (-0.5))
            done = (part[:, lane : lane + HAD] * scale_row).astype(bf16)
            send_ref[:, at + lane : at + lane + HAD] = done[:half]
            keep_ref[:, at + lane : at + lane + HAD] = done[half:]


def out_project(rotated, weights, scale_rows, first, columns):
    row_count, inner = rotated.shape
    result = shape_of((row_count // 2, columns), bf16)
    return call(
        functools.partial(out_kernel, first),
        (result, result),
        [VMEM] * 3,
        (rotated, weights, scale_rows),
        "out_project",
    )


def finish_kernel(chunks, first, sign_ref, *rest):
    out_hbm, done_ref, sems = rest[-3:]
    doubled = double_hadamard()
    copies = []
    for chunk in range(chunks):
        keep_ref, more_ref = rest[2 * chunk : 2 * chunk + 2]
        share, columns = keep_ref.shape
        totals = keep_ref[...].astype(f32) + more_ref[...].astype(f32)
        blocks = [totals[:, at : at + HAD] for at in range(0, columns, HAD)]
        turned = rotate_halves(jnp.concatenate(blocks, 0), doubled)
        for block in range(len(blocks)):
            place = first // HAD + block
            sign_row = signed(sign_ref[place : place + 1, :]) * np.float32(HAD ** (-0.5))
            done = turned[block * share : (block + 1) * share] * sign_row
            done_ref[:, place * HAD : (place + 1) * HAD] = done.astype(bf16)
        cols = pl.ds(first, columns)
        copies.append(
            pltpu.make_async_copy(done_ref.at[:, cols], out_hbm.at[:, cols], sems.at[chunk])
        )
        copies[-1].start()
        first += columns
    for copy in copies:
        copy.wait()


def finish(pairs, sign_rows, first, base):
    share = pairs[0][0].shape[0]
    args = [sign_rows] + [array for pair in pairs for array in pair]
    in_specs = [VMEM] * len(args)
    aliases = {}
    if base is not None:
        aliases = {len(args): 0}
        args.append(base)
        in_specs.append(HBM)
    return call(
        functools.partial(finish_kernel, len(pairs), first),
        shape_of((share, D), bf16),
        in_specs,
        args,
        "finish",
        out_specs=HBM,
        scratch_shapes=[pltpu.VMEM((share, D), bf16), pltpu.SemaphoreType.DMA((len(pairs),))],
        input_output_aliases=aliases,
    )


def swap(shard, bit):
    peers = lax.axis_size("head")
    return lax.ppermute(shard, "head", [(i, i ^ bit) for i in range(peers)])


def row_swaps(row_tiles):
    swaps = []
    for by in (1, 3, 4, 5) if row_tiles > HROWS else (1,):
        for odd in (1, 0):
            low = [i for i in range(row_tiles - by) if (i // by) % 2 == odd]
            swaps.append((by, odd, [(i, i + by) for i in low] + [(i + by, i) for i in low]))
    return swaps


def halving_order(head_count):
    flips = [0]
    bit = head_count // 2
    while bit >= 1:
        flips = [f | bit for f in flips] + flips
        bit //= 2
    return tuple(flips)


CHUNKS = (2560, 2560)


def on_device(
    tokens,
    in_sign,
    qkv_codes,
    qkv_scale,
    qkv_sign,
    windows,
    oin_sign,
    out_codes,
    out_scale,
    out_sign,
):
    head_count = lax.axis_size("head")
    row_tiles = lax.axis_size("height")
    top = head_count // 2
    low_bits = [1 << b for b in range(top.bit_length() - 1)]

    own, early = turn(tokens[0], in_sign)
    half_rows = early.shape[0]
    early = swap(early, top)
    near = {0: own}
    for bit in low_bits:
        for flip in list(near):
            near[flip ^ bit] = swap(near[flip], bit)
    codes = jnp.transpose(qkv_codes, (1, 0, 2))
    near_flips = tuple(sorted(near))
    far_flips = tuple(flip ^ top for flip in near_flips)
    sums, words, late = prepare(
        near_flips, far_flips, [near[flip] for flip in near_flips], codes
    )
    late = swap(late, top)
    swaps = row_swaps(row_tiles)
    ending = [qkv_scale, qkv_sign]
    every = tuple(range(len(far_flips)))
    halves, key_values, moved, gates = [], [], [], []
    for half, first_row in ((early, 0), (late, half_rows)):
        shards = {top: tie(half, *gates, sums)}
        for bit in low_bits:
            for flip in list(shards):
                shards[flip ^ bit] = swap(shards[flip], bit)
        shards = [shards[flip] for flip in far_flips]
        partial = project(
            (1, 2), first_row, [shards[:-1]], every[:-1], sums, words, None, 4 * 10**9
        )
        key_value = project((1, 2), 0, [shards[-1:]], every[-1:], partial, words, ending)
        moved.append([lax.ppermute(key_value, "height", pairs) for _, _, pairs in swaps])
        halves.append(shards)
        key_values.append(key_value)
        gates.append(gate(key_value))
    queries = [project((0,), 0, halves, every, sums, words, ending, 4 * 10**9)]
    out_weights = unpack_out(out_codes, key_values[1])

    late_rows = own.shape[0] - half_rows
    own_keys = ((None, 0, half_rows), (None, half_rows, late_rows))
    early_keys = tuple(((by, odd), 0, half_rows) for by, odd, _ in swaps)
    late_keys = tuple(((by, odd), half_rows, late_rows) for by, odd, _ in swaps)
    steps = (own_keys, early_keys, late_keys[1:], late_keys[:1])
    masks = make_masks(windows, key_values[1], steps)
    running = attend(queries, key_values, masks[0], None, None)
    running = attend(queries, moved[0], masks[1], running, None)
    running = attend(queries, moved[1][1:], masks[2], running, None)
    rotated = attend(
        queries, moved[1][:1], masks[3], running, (oin_sign, halving_order(head_count))
    )

    bits = low_bits + [top]
    scale_rows = out_scale.reshape(-1, HAD)
    sign_rows = out_sign.reshape(-1, HAD)
    pairs, sums_sent = [], []
    first = 0
    for columns in CHUNKS:
        part, keep = out_project(rotated, out_weights, scale_rows, first, columns)
        if sums_sent:
            part = tie(part, sums_sent[-1])
        for bit in bits:
            more = swap(part, bit)
            if bit == top:
                break
            total = keep.astype(f32) + more.astype(f32)
            half = total.shape[0] // 2
            part, keep = total[:half].astype(bf16), total[half:]
            sums_sent.append(part)
        pairs.append((keep, more))
        first += columns
    base = finish(pairs[:-1], sign_rows, 0, None)
    return finish(pairs[-1:], sign_rows, D - CHUNKS[-1], base)[None]


def solution(mesh):
    return jax.shard_map(
        on_device,
        mesh=mesh,
        in_specs=(
            P(("clip", "height"), None, "head"),
            P(),
            P(None, None, "head"),
            P(None, "head"),
            P(None, "head"),
            P(("clip", "height"), None, None),
            P("head"),
            P("head", None),
            P(),
            P(),
        ),
        out_specs=P(("clip", "height"), "head", None),
        check_vma=False,
    )
```

```python
import functools

import jax
import jax.numpy as jnp
import numpy as np
from jax import lax
from jax.experimental import pallas as pl
from jax.experimental.pallas import tpu as pltpu
from jax.sharding import PartitionSpec as P

D = 5120
HD = 128
HEADS = 24
HAD = 128
TILE = 64
HROWS = 4
WTILES = 3
PLANES = 8
WORDS = HAD // PLANES
QKV_ORDER = "half"
OUT_ORDER = "byte"
FINISH_BLOCK = 5 * HAD

epsilon = 1e-06
f32 = jnp.float32
bf16 = jnp.bfloat16
VMEM = pl.BlockSpec(memory_space=pltpu.VMEM)
SMEM = pl.BlockSpec(memory_space=pltpu.SMEM)
ANY = pl.BlockSpec(memory_space=pl.ANY)
HBM = pl.BlockSpec(memory_space=pltpu.HBM)


def shape_of(shape, dtype):
    return jax.ShapeDtypeStruct(tuple(shape), dtype)


def in_hbm(array):
    return pltpu.with_memory_space_constraint(array, pltpu.HBM)


def call(body, out_shape, in_specs, args, name, out_specs=None, megabytes=16, flops=1, **more):
    if out_specs is None:
        out_specs = jax.tree.map(lambda _: VMEM, out_shape)
    return pl.pallas_call(
        body,
        out_shape=out_shape,
        in_specs=in_specs,
        out_specs=out_specs,
        compiler_params=pltpu.CompilerParams(vmem_limit_bytes=megabytes * 2**20),
        cost_estimate=pl.CostEstimate(flops=flops, bytes_accessed=1, transcendentals=0),
        name=name,
        **more,
    )(*args)


def lanes():
    return lax.broadcasted_iota(jnp.int32, (HAD, HAD), 1)


def hadamard(order):
    row = lax.broadcasted_iota(jnp.int32, (HAD, HAD), 0)
    column = lanes()
    word = PLANES * (column & (WORDS - 1))
    if order == "half":
        column = word + column // WORDS
    if order == "byte":
        column = word + column // (2 * WORDS) + (PLANES // 2) * ((column // WORDS) & 1)
    shared = row & column
    shared = shared ^ (shared >> 4)
    shared = shared ^ (shared >> 2)
    shared = shared ^ (shared >> 1)
    return (1 - 2 * (shared & 1)).astype(f32).astype(bf16)


def double_hadamard():
    plain = hadamard("plain")
    return jnp.concatenate([plain, plain], 0)


def plane_power(base, order):
    lane = lax.broadcasted_iota(jnp.int32, (1, HAD), 1)
    if order == "half":
        power = jnp.minimum(lane // WORDS, PLANES - 2)
    else:
        power = jnp.minimum(lane // (2 * WORDS), PLANES // 2 - 2)
    value = jnp.where(power & 1 == 1, base, 1.0)
    value = value * jnp.where(power & 2 == 2, base**2, 1.0)
    return value * jnp.where(power & 4 == 4, base**4, 1.0)


def turn_factor(order):
    return plane_power(0.25, order) * np.float32(HAD ** (-0.5))


def signed(sign_bits):
    return (2 * sign_bits - 1).astype(f32)


def pieces_of(words, order):
    if order == "half":
        packed = words.astype(jnp.int16)
        masked = [packed & jnp.int16(3 << (2 * k)) for k in range(PLANES - 1)]
        masked.append((words >> 2).astype(jnp.int16) & jnp.int16(3 << (2 * PLANES - 4)))
    else:
        pair = jnp.concatenate([words & 255, words >> 8], 0)
        packed = pair.astype(jnp.int8)
        masked = [packed & jnp.int8(3 << (2 * k)) for k in range(PLANES // 2 - 1)]
        masked.append((pair >> 2).astype(jnp.int8) & jnp.int8(3 << (PLANES - 4)))
    return [piece.astype(bf16) for piece in masked]


def decode(words, order):
    blocks = []
    for first in range(0, words.shape[0], WORDS):
        blocks += pieces_of(words[first : first + WORDS], order)
    return jnp.concatenate(blocks, 0)


def row_correction(row_list, order):
    factor_row = plane_power(4.0, order) * 1.5
    total = None
    for rows in row_list:
        for first in range(0, rows.shape[1], HAD):
            term = rows[:, first : first + HAD].astype(f32)
            total = term if total is None else total + term
    return jnp.sum(total * factor_row, axis=1, keepdims=True)


def rotate_halves(values, doubled):
    high = values.astype(bf16)
    low = (values - high.astype(f32)).astype(bf16)
    return jnp.dot(jnp.concatenate([high, low], 1), doubled, preferred_element_type=f32)


def early_rows(rows):
    return rows * 5 // 12 // WORDS * WORDS


def turn_kernel(x_hbm, sign_hbm, own_ref, send_ref, x_ref, sign_ref, sems):
    copies = [
        pltpu.make_async_copy(x_hbm, x_ref, sems.at[0]),
        pltpu.make_async_copy(sign_hbm, sign_ref, sems.at[1]),
    ]
    for copy in copies:
        copy.start()
    matrix = hadamard(QKV_ORDER)
    factor = turn_factor(QKV_ORDER)
    for copy in copies:
        copy.wait()
    blocks = x_ref.shape[1] // HAD
    first = lax.axis_index("head") * blocks
    for b in range(blocks):
        cols = slice(b * HAD, (b + 1) * HAD)
        sign_row = signed(sign_ref[pl.ds(first + b, 1), :])
        flipped = (x_ref[:, cols].astype(f32) * sign_row).astype(bf16)
        turned = jnp.dot(flipped, matrix, preferred_element_type=f32)
        turned = (turned * factor).astype(bf16)
        own_ref[:, cols] = turned
        send_ref[:, cols] = turned[: send_ref.shape[0]]


def turn(own_tokens, in_sign):
    sign_rows = in_sign.reshape(-1, HAD)
    rows, inner = own_tokens.shape
    return call(
        turn_kernel,
        (shape_of((rows, inner), bf16), shape_of((early_rows(rows), inner), bf16)),
        [HBM, HBM],
        (in_hbm(own_tokens), in_hbm(sign_rows)),
        "turn",
        scratch_shapes=[
            pltpu.VMEM(own_tokens.shape, bf16),
            pltpu.VMEM(sign_rows.shape, jnp.int32),
            pltpu.SemaphoreType.DMA((2,)),
        ],
    )


def tie(array, *after):
    return call(
        lambda *refs: None,
        shape_of(array.shape, array.dtype),
        [ANY] * (1 + len(after)),
        (array, *after),
        "tie",
        out_specs=ANY,
        input_output_aliases={0: 0},
    )


def gate(array):
    def body(array_ref, out_ref):
        out_ref[...] = jnp.zeros_like(out_ref)

    return call(body, shape_of((8, HAD), f32), [ANY], (array,), "gate", flops=4 * 10**9)


def prepare_kernel(near, far, *rest):
    shard_refs = rest[: len(near)]
    codes_hbm, sums_ref, far_ref, late_ref, near_ref, sems = rest[len(near) :]
    words, columns = near_ref.shape[2:]

    def fetch(position, kind):
        flip = (near + far)[position]
        first = pl.multiple_of((lax.axis_index("head") ^ flip) * words, WORDS)
        there = position - len(near)
        target = near_ref.at[position, kind] if there < 0 else far_ref.at[there, kind]
        return pltpu.make_async_copy(
            codes_hbm.at[kind, pl.ds(first, words), :], target, sems.at[position, kind]
        )

    for kind in range(3):
        for position in range(len(near)):
            fetch(position, kind).start()
    for position in range(len(near), len(near + far)):
        for kind in range(3):
            fetch(position, kind).start()
    fix = row_correction([ref[...] for ref in shard_refs], QKV_ORDER)
    late_ref[...] = shard_refs[0][shard_refs[0].shape[0] - late_ref.shape[0] :, :]

    def every_shard(kind, carry):
        for position in range(len(near)):
            fetch(position, kind).wait()
        total = -fix
        for position, ref in enumerate(shard_refs):
            weights = decode(near_ref[position, kind], QKV_ORDER)
            total = total + jnp.dot(ref[...], weights, preferred_element_type=f32)
        sums_ref[kind] = total
        return carry

    lax.fori_loop(0, 3, every_shard, 0)
    for position in range(len(near), len(near + far)):
        for kind in range(3):
            fetch(position, kind).wait()


def prepare(near, far, shards, codes):
    rows, inner = shards[0].shape
    columns = codes.shape[2]
    words = inner // PLANES
    return call(
        functools.partial(prepare_kernel, near, far),
        (
            shape_of((3, rows, columns), f32),
            shape_of((len(far), 3, words, columns), jnp.int32),
            shape_of((rows - early_rows(rows), inner), bf16),
        ),
        [VMEM] * len(near) + [HBM],
        (*shards, in_hbm(codes)),
        "prepare",
        scratch_shapes=[
            pltpu.VMEM((len(near), 3, words, columns), jnp.int32),
            pltpu.SemaphoreType.DMA((len(near + far), 3)),
        ],
    )


def project_kernel(kinds, first_row, groups, positions, whole, ending, *rest):
    count = len(positions)
    shard_refs = rest[: groups * count]
    sums_ref, words_ref = rest[groups * count : groups * count + 2]
    if ending:
        scale_ref, sign_ref = rest[groups * count + 2 : groups * count + 4]
    out_ref = rest[-1]
    columns = sums_ref.shape[2]
    shards = []
    for place in range(count):
        parts = [shard_refs[g * count + place][...] for g in range(groups)]
        shards.append(parts[0] if groups == 1 else jnp.concatenate(parts, 0))
    fix = row_correction(shards, QKV_ORDER)
    row_count = shards[0].shape[0]
    rows = slice(first_row, first_row + row_count)
    doubled = double_hadamard()
    ones = jnp.ones((HD, HD), bf16)
    for place, kind in enumerate(kinds):
        part = (sums_ref[kind, rows, :] if whole else sums_ref[place]) - fix
        for shard, position in zip(shards, positions):
            weights = decode(words_ref[position, kind], QKV_ORDER)
            part = part + jnp.dot(shard, weights, preferred_element_type=f32)
        if not ending:
            out_ref[place] = part
            continue
        heads = []
        for first in range(0, columns, HD):
            at = slice(first, first + HD)
            scale_row = scale_ref[kind : kind + 1, at] * np.float32(D ** (-0.5))
            heads.append(part[:, at] * scale_row)
        mixed = rotate_halves(jnp.concatenate(heads, 0), doubled)
        signs = []
        for head in range(len(heads)):
            sign_row = sign_ref[kind : kind + 1, head * HD : (head + 1) * HD]
            sign_row = signed(sign_row) * np.float32(HAD ** (-0.5))
            signs.append(mixed[head * row_count : (head + 1) * row_count] * sign_row)
        if kind != 2:
            square = jnp.concatenate([(part * part).astype(bf16) for part in signs], 0)
            mean = jnp.dot(square, ones, preferred_element_type=f32) * (1.0 / HD)
            factor = lax.rsqrt(mean + epsilon)
            signs = [
                part * factor[head * row_count : (head + 1) * row_count]
                for head, part in enumerate(signs)
            ]
        for head, part in enumerate(signs):
            out_ref[place, :, head * HD : (head + 1) * HD] = part.astype(bf16)


def project(kinds, first_row, groups, positions, sums, words, ending, flops=1):
    inner = groups[0][0].shape[1]
    columns = sums.shape[2]
    row_count = sum(group[0].shape[0] for group in groups)
    whole = sums.shape[0] == 3
    args = [shard for group in groups for shard in group] + [sums, words]
    own_args = len(args) + 2
    if ending is not None:
        args += ending
    return call(
        functools.partial(
            project_kernel, kinds, first_row, len(groups), positions, whole, ending is not None
        ),
        shape_of((len(kinds), row_count, columns), f32 if ending is None else bf16),
        [VMEM] * min(len(args), own_args) + [ANY] * max(len(args) - own_args, 0),
        args,
        "project",
        flops=flops,
    )


def near_row(row, swap_pair):
    if swap_pair is None:
        return row
    by, odd = swap_pair
    return jnp.where(lax.rem(row // by, 2) == odd, row + by, row - by)


def masks_kernel(steps, windows_ref, after_ref, *mask_refs):
    row = lax.axis_index("height")
    for segments, mask_ref in zip(steps, mask_refs):
        lane = lax.broadcasted_iota(jnp.int32, (1, mask_ref.shape[1]), 1)
        ids, base = None, 0
        for swap_pair, first, rows in segments:
            tile = (lane + (first - base)) // TILE
            ids_here = near_row(row, swap_pair) * WTILES + tile
            ids = ids_here if ids is None else jnp.where(lane >= base, ids_here, ids)
            base += rows
        for tile in range(mask_ref.shape[0]):
            hit = jnp.zeros(lane.shape, f32)
            for entry in range(windows_ref.shape[2]):
                hit = jnp.where(ids == windows_ref[tile, 0, entry], 1.0, hit)
            mask_ref[tile : tile + 1, :] = hit


def make_masks(windows, after, steps):
    listed = jnp.transpose(windows, (1, 0, 2))
    shapes = [
        shape_of((listed.shape[0], sum(rows for _, _, rows in segments)), f32) for segments in steps
    ]
    return call(
        functools.partial(masks_kernel, steps), shapes, [SMEM, ANY], (listed, after), "window_masks"
    )


def attend_kernel(halves, blocks, has_sum, last, share_order, *rest):
    rest = list(rest)
    q_refs = [rest.pop(0) for _ in range(halves)]
    kv_refs = [rest.pop(0) for _ in range(blocks)]
    mask_ref = rest.pop(0)
    sum_ref = rest.pop(0) if has_sum else None
    if last:
        oin_ref, out_ref, rotated_ref = rest
    else:
        (out_ref,) = rest
    columns = q_refs[0].shape[2]
    row_count = sum(ref.shape[1] for ref in q_refs)
    heads = [slice(head, head + HD) for head in range(0, columns, HD)]
    mask = jnp.concatenate(
        [
            jnp.broadcast_to(mask_ref[t : t + 1, :], (TILE, mask_ref.shape[1]))
            for t in range(row_count // TILE)
        ],
        0,
    )
    scores = []
    for at in heads:
        keys = jnp.concatenate([ref[0, :, at] for ref in kv_refs], 0)
        scores.append(
            lax.dot_general(
                jnp.concatenate([ref[0, :, at] for ref in q_refs], 0),
                keys,
                (((1,), (1,)), ((), ())),
                preferred_element_type=f32,
            )
        )
    weights = [
        (jnp.exp(score * np.float32(HD ** (-0.5))) * mask).astype(bf16) for score in scores
    ]
    totals = []
    for head, at in enumerate(heads):
        values = jnp.concatenate([ref[1, :, at] for ref in kv_refs], 0)
        values = jnp.concatenate([values, jnp.ones_like(values)], 1)
        total = jnp.dot(weights[head], values, preferred_element_type=f32)
        if has_sum:
            total = total + sum_ref[head]
        totals.append(total)
    if not last:
        for head, total in enumerate(totals):
            out_ref[head] = total
        return
    matrix = hadamard(OUT_ORDER)
    factor = turn_factor(OUT_ORDER)
    for head, at in enumerate(heads):
        attended = (totals[head][:, :HD] / totals[head][:, HD:]).astype(bf16)
        sign_row = signed(oin_ref[head : head + 1, :])
        flipped = (attended.astype(f32) * sign_row).astype(bf16)
        rotated_ref[:, at] = jnp.dot(flipped, matrix, preferred_element_type=f32) * factor
    share = row_count // len(share_order)
    pieces = []
    for flip in share_order:
        owner = lax.axis_index("head") ^ flip
        pieces.append(rotated_ref[pl.ds(pl.multiple_of(owner * share, 8), share), :])
    out_ref[...] = jnp.concatenate(pieces, 0).astype(bf16)


def attend(queries, blocks, mask, running, ending):
    columns = queries[0].shape[2]
    row_count = sum(part.shape[1] for part in queries)
    args = [*queries, *blocks, mask]
    if running is not None:
        args.append(running)
    scratch, share_order = [], None
    if ending is None:
        out_shape = shape_of((columns // HD, row_count, 2 * HD), f32)
    else:
        oin_sign, share_order = ending
        args.append(oin_sign.reshape(-1, HAD))
        out_shape = shape_of((row_count, columns), bf16)
        scratch = [pltpu.VMEM((row_count, columns), f32)]
    return call(
        functools.partial(
            attend_kernel,
            len(queries),
            len(blocks),
            running is not None,
            ending is not None,
            share_order,
        ),
        out_shape,
        [VMEM] * len(args),
        args,
        "attend",
        scratch_shapes=scratch,
    )


def unpack_out_kernel(codes_ref, after_ref, weights_ref):
    for first in range(0, codes_ref.shape[0], WORDS):

        def some(step, carry):
            cols = pl.ds(pl.multiple_of(step * 512, 512), 512)
            at = first * PLANES
            for piece in pieces_of(codes_ref[first : first + WORDS, cols], OUT_ORDER):
                weights_ref[at : at + piece.shape[0], cols] = piece
                at += piece.shape[0]
            return carry

        lax.fori_loop(0, codes_ref.shape[1] // 512, some, 0)


def unpack_out(codes, after):
    words, columns = codes.shape
    return call(
        unpack_out_kernel,
        shape_of((words * PLANES, columns), bf16),
        [VMEM, ANY],
        (codes, after),
        "unpack_out",
    )


def out_kernel(first, rotated_ref, weights_ref, scale_ref, send_ref, keep_ref):
    rows = rotated_ref[...]
    fix = row_correction([rows], OUT_ORDER)
    half, columns = send_ref.shape
    width = 512
    for at in range(0, columns, width):
        cols = slice(first + at, first + at + width)
        part = jnp.dot(rows, weights_ref[:, cols], preferred_element_type=f32) - fix
        for lane in range(0, width, HAD):
            place = (first + at + lane) // HAD
            scale_row = scale_ref[place : place + 1, :] * np.float32((HEADS * HD) ** (-0.5))
            done = (part[:, lane : lane + HAD] * scale_row).astype(bf16)
            send_ref[:, at + lane : at + lane + HAD] = done[:half]
            keep_ref[:, at + lane : at + lane + HAD] = done[half:]


def out_project(rotated, weights, scale_rows, first, columns):
    row_count, inner = rotated.shape
    result = shape_of((row_count // 2, columns), bf16)
    return call(
        functools.partial(out_kernel, first),
        (result, result),
        [VMEM] * 3,
        (rotated, weights, scale_rows),
        "out_project",
    )


def finish_kernel(chunks, first, sign_ref, *rest):
    out_hbm, done_ref, sems = rest[-3:]
    doubled = double_hadamard()
    copies = []
    for chunk in range(chunks):
        keep_ref, more_ref = rest[2 * chunk : 2 * chunk + 2]
        share, columns = keep_ref.shape
        for part in range(0, columns, FINISH_BLOCK):
            cols = slice(part, part + FINISH_BLOCK)
            totals = keep_ref[:, cols].astype(f32) + more_ref[:, cols].astype(f32)
            blocks = [totals[:, at : at + HAD] for at in range(0, FINISH_BLOCK, HAD)]
            turned = rotate_halves(jnp.concatenate(blocks, 0), doubled)
            for block in range(len(blocks)):
                place = first // HAD + block
                sign_row = signed(sign_ref[place : place + 1, :]) * np.float32(HAD ** (-0.5))
                done = turned[block * share : (block + 1) * share] * sign_row
                done_ref[:, place * HAD : (place + 1) * HAD] = done.astype(bf16)
            where = pl.ds(first, FINISH_BLOCK)
            copies.append(
                pltpu.make_async_copy(
                    done_ref.at[:, where], out_hbm.at[:, where], sems.at[len(copies)]
                )
            )
            copies[-1].start()
            first += FINISH_BLOCK
    for copy in copies:
        copy.wait()


def finish(pairs, sign_rows, first, base):
    share = pairs[0][0].shape[0]
    args = [sign_rows] + [array for pair in pairs for array in pair]
    in_specs = [VMEM] * len(args)
    aliases = {}
    if base is not None:
        aliases = {len(args): 0}
        args.append(base)
        in_specs.append(HBM)
    return call(
        functools.partial(finish_kernel, len(pairs), first),
        shape_of((share, D), bf16),
        in_specs,
        args,
        "finish",
        out_specs=HBM,
        scratch_shapes=[
            pltpu.VMEM((share, D), bf16),
            pltpu.SemaphoreType.DMA((D // FINISH_BLOCK,)),
        ],
        input_output_aliases=aliases,
    )


def swap(shard, bit):
    peers = lax.axis_size("head")
    return lax.ppermute(shard, "head", [(i, i ^ bit) for i in range(peers)])


def row_swaps(row_tiles):
    swaps = []
    for by in (1, 3, 4, 5) if row_tiles > HROWS else (1,):
        for odd in (1, 0):
            low = [i for i in range(row_tiles - by) if (i // by) % 2 == odd]
            swaps.append((by, odd, [(i, i + by) for i in low] + [(i + by, i) for i in low]))
    return swaps


def halving_order(head_count):
    flips = [0]
    bit = head_count // 2
    while bit >= 1:
        flips = [f | bit for f in flips] + flips
        bit //= 2
    return tuple(flips)


CHUNKS = (2560, 2560)


def on_device(
    tokens,
    in_sign,
    qkv_codes,
    qkv_scale,
    qkv_sign,
    windows,
    oin_sign,
    out_codes,
    out_scale,
    out_sign,
):
    head_count = lax.axis_size("head")
    row_tiles = lax.axis_size("height")
    top = head_count // 2
    low_bits = [1 << b for b in range(top.bit_length() - 1)]

    own, early = turn(tokens[0], in_sign)
    half_rows = early.shape[0]
    early = swap(early, top)
    near = {0: own}
    for bit in low_bits:
        for flip in list(near):
            near[flip ^ bit] = swap(near[flip], bit)
    codes = jnp.transpose(qkv_codes, (1, 0, 2))
    near_flips = tuple(sorted(near))
    far_flips = tuple(flip ^ top for flip in near_flips)
    sums, words, late = prepare(
        near_flips, far_flips, [near[flip] for flip in near_flips], codes
    )
    late = swap(late, top)
    swaps = row_swaps(row_tiles)
    ending = [qkv_scale, qkv_sign]
    every = tuple(range(len(far_flips)))
    halves, key_values, moved, gates = [], [], [], []
    for half, first_row in ((early, 0), (late, half_rows)):
        shards = {top: tie(half, *gates, sums)}
        for bit in low_bits:
            for flip in list(shards):
                shards[flip ^ bit] = swap(shards[flip], bit)
        shards = [shards[flip] for flip in far_flips]
        partial = project(
            (1, 2), first_row, [shards[:-1]], every[:-1], sums, words, None, 4 * 10**9
        )
        key_value = project((1, 2), 0, [shards[-1:]], every[-1:], partial, words, ending)
        moved.append([lax.ppermute(key_value, "height", pairs) for _, _, pairs in swaps])
        halves.append(shards)
        key_values.append(key_value)
        gates.append(gate(key_value))
    queries = [project((0,), 0, halves, every, sums, words, ending, 4 * 10**9)]
    out_weights = unpack_out(out_codes, key_values[1])

    late_rows = own.shape[0] - half_rows
    own_keys = ((None, 0, half_rows), (None, half_rows, late_rows))
    early_keys = tuple(((by, odd), 0, half_rows) for by, odd, _ in swaps)
    late_keys = tuple(((by, odd), half_rows, late_rows) for by, odd, _ in swaps)
    steps = (own_keys, early_keys, late_keys[1:], late_keys[:1])
    masks = make_masks(windows, key_values[1], steps)
    running = attend(queries, key_values, masks[0], None, None)
    running = attend(queries, moved[0], masks[1], running, None)
    running = attend(queries, moved[1][1:], masks[2], running, None)
    rotated = attend(
        queries, moved[1][:1], masks[3], running, (oin_sign, halving_order(head_count))
    )

    bits = low_bits + [top]
    scale_rows = out_scale.reshape(-1, HAD)
    sign_rows = out_sign.reshape(-1, HAD)
    pairs, sums_sent = [], []
    first = 0
    for columns in CHUNKS:
        part, keep = out_project(rotated, out_weights, scale_rows, first, columns)
        if sums_sent:
            part = tie(part, sums_sent[-1])
        for bit in bits:
            more = swap(part, bit)
            if bit == top:
                break
            total = keep.astype(f32) + more.astype(f32)
            half = total.shape[0] // 2
            part, keep = total[:half].astype(bf16), total[half:]
            sums_sent.append(part)
        pairs.append((keep, more))
        first += columns
    base = finish(pairs[:-1], sign_rows, 0, None)
    return finish(pairs[-1:], sign_rows, D - CHUNKS[-1], base)[None]


def solution(mesh):
    return jax.shard_map(
        on_device,
        mesh=mesh,
        in_specs=(
            P(("clip", "height"), None, "head"),
            P(),
            P(None, None, "head"),
            P(None, "head"),
            P(None, "head"),
            P(("clip", "height"), None, None),
            P("head"),
            P("head", None),
            P(),
            P(),
        ),
        out_specs=P(("clip", "height"), "head", None),
        check_vma=False,
    )
```

```python
import functools

import jax
import jax.numpy as jnp
import numpy as np
from jax import lax
from jax.experimental import pallas as pl
from jax.experimental.pallas import tpu as pltpu
from jax.sharding import PartitionSpec as P

D = 5120
HD = 128
HEADS = 24
HAD = 128
TILE = 64
HROWS = 4
WTILES = 3
PLANES = 8
WORDS = HAD // PLANES
QKV_ORDER = "half"
OUT_ORDER = "byte"

epsilon = 1e-06
f32 = jnp.float32
bf16 = jnp.bfloat16
VMEM = pl.BlockSpec(memory_space=pltpu.VMEM)
SMEM = pl.BlockSpec(memory_space=pltpu.SMEM)
ANY = pl.BlockSpec(memory_space=pl.ANY)
HBM = pl.BlockSpec(memory_space=pltpu.HBM)


def shape_of(shape, dtype):
    return jax.ShapeDtypeStruct(tuple(shape), dtype)


def in_hbm(array):
    return pltpu.with_memory_space_constraint(array, pltpu.HBM)


def call(body, out_shape, in_specs, args, name, out_specs=None, megabytes=16, flops=1, **more):
    if out_specs is None:
        out_specs = jax.tree.map(lambda _: VMEM, out_shape)
    return pl.pallas_call(
        body,
        out_shape=out_shape,
        in_specs=in_specs,
        out_specs=out_specs,
        compiler_params=pltpu.CompilerParams(vmem_limit_bytes=megabytes * 2**20),
        cost_estimate=pl.CostEstimate(flops=flops, bytes_accessed=1, transcendentals=0),
        name=name,
        **more,
    )(*args)


def lanes():
    return lax.broadcasted_iota(jnp.int32, (HAD, HAD), 1)


def hadamard(order):
    row = lax.broadcasted_iota(jnp.int32, (HAD, HAD), 0)
    column = lanes()
    word = PLANES * (column & (WORDS - 1))
    if order == "half":
        column = word + column // WORDS
    if order == "byte":
        column = word + column // (2 * WORDS) + (PLANES // 2) * ((column // WORDS) & 1)
    shared = row & column
    shared = shared ^ (shared >> 4)
    shared = shared ^ (shared >> 2)
    shared = shared ^ (shared >> 1)
    return (1 - 2 * (shared & 1)).astype(f32).astype(bf16)


def double_hadamard():
    plain = hadamard("plain")
    return jnp.concatenate([plain, plain], 0)


def plane_power(base, order):
    lane = lax.broadcasted_iota(jnp.int32, (1, HAD), 1)
    if order == "half":
        power = jnp.minimum(lane // WORDS, PLANES - 2)
    else:
        power = jnp.minimum(lane // (2 * WORDS), PLANES // 2 - 2)
    value = jnp.where(power & 1 == 1, base, 1.0)
    value = value * jnp.where(power & 2 == 2, base**2, 1.0)
    return value * jnp.where(power & 4 == 4, base**4, 1.0)


def turn_factor(order):
    return plane_power(0.25, order) * np.float32(HAD ** (-0.5))


def signed(sign_bits):
    return (2 * sign_bits - 1).astype(f32)


def pieces_of(words, order):
    if order == "half":
        packed = words.astype(jnp.int16)
        masked = [packed & jnp.int16(3 << (2 * k)) for k in range(PLANES - 1)]
        masked.append((words >> 2).astype(jnp.int16) & jnp.int16(3 << (2 * PLANES - 4)))
    else:
        pair = jnp.concatenate([words & 255, words >> 8], 0)
        packed = pair.astype(jnp.int8)
        masked = [packed & jnp.int8(3 << (2 * k)) for k in range(PLANES // 2 - 1)]
        masked.append((pair >> 2).astype(jnp.int8) & jnp.int8(3 << (PLANES - 4)))
    return [piece.astype(bf16) for piece in masked]


def decode(words, order):
    blocks = []
    for first in range(0, words.shape[0], WORDS):
        blocks += pieces_of(words[first : first + WORDS], order)
    return jnp.concatenate(blocks, 0)


def row_correction(row_list, order):
    factor_row = plane_power(4.0, order) * 1.5
    total = None
    for rows in row_list:
        for first in range(0, rows.shape[1], HAD):
            term = rows[:, first : first + HAD].astype(f32)
            total = term if total is None else total + term
    return jnp.sum(total * factor_row, axis=1, keepdims=True)


def rotate_halves(values, doubled):
    high = values.astype(bf16)
    low = (values - high.astype(f32)).astype(bf16)
    return jnp.dot(jnp.concatenate([high, low], 1), doubled, preferred_element_type=f32)


def early_rows(rows):
    return rows // 2 // WORDS * WORDS


def turn_kernel(x_hbm, sign_hbm, own_ref, send_ref, x_ref, sign_ref, sems):
    copies = [
        pltpu.make_async_copy(x_hbm, x_ref, sems.at[0]),
        pltpu.make_async_copy(sign_hbm, sign_ref, sems.at[1]),
    ]
    for copy in copies:
        copy.start()
    matrix = hadamard(QKV_ORDER)
    factor = turn_factor(QKV_ORDER)
    for copy in copies:
        copy.wait()
    blocks = x_ref.shape[1] // HAD
    first = lax.axis_index("head") * blocks
    for b in range(blocks):
        cols = slice(b * HAD, (b + 1) * HAD)
        sign_row = signed(sign_ref[pl.ds(first + b, 1), :])
        flipped = (x_ref[:, cols].astype(f32) * sign_row).astype(bf16)
        turned = jnp.dot(flipped, matrix, preferred_element_type=f32)
        turned = (turned * factor).astype(bf16)
        own_ref[:, cols] = turned
        send_ref[:, cols] = turned[: send_ref.shape[0]]


def turn(own_tokens, in_sign):
    sign_rows = in_sign.reshape(-1, HAD)
    rows, inner = own_tokens.shape
    return call(
        turn_kernel,
        (shape_of((rows, inner), bf16), shape_of((early_rows(rows), inner), bf16)),
        [HBM, HBM],
        (in_hbm(own_tokens), in_hbm(sign_rows)),
        "turn",
        scratch_shapes=[
            pltpu.VMEM(own_tokens.shape, bf16),
            pltpu.VMEM(sign_rows.shape, jnp.int32),
            pltpu.SemaphoreType.DMA((2,)),
        ],
    )


def tie(array, *after):
    return call(
        lambda *refs: None,
        shape_of(array.shape, array.dtype),
        [ANY] * (1 + len(after)),
        (array, *after),
        "tie",
        out_specs=ANY,
        input_output_aliases={0: 0},
    )


def gate(array):
    def body(array_ref, out_ref):
        out_ref[...] = jnp.zeros_like(out_ref)

    return call(body, shape_of((8, HAD), f32), [ANY], (array,), "gate", flops=4 * 10**9)


def prepare_kernel(near, far, *rest):
    shard_refs = rest[: len(near)]
    codes_hbm, sums_ref, far_ref, late_ref, near_ref, sems = rest[len(near) :]
    words, columns = near_ref.shape[2:]

    def fetch(position, kind):
        flip = (near + far)[position]
        first = pl.multiple_of((lax.axis_index("head") ^ flip) * words, WORDS)
        there = position - len(near)
        target = near_ref.at[position, kind] if there < 0 else far_ref.at[there, kind]
        return pltpu.make_async_copy(
            codes_hbm.at[kind, pl.ds(first, words), :], target, sems.at[position, kind]
        )

    for kind in range(3):
        for position in range(len(near)):
            fetch(position, kind).start()
    for position in range(len(near), len(near + far)):
        for kind in range(3):
            fetch(position, kind).start()
    fix = row_correction([ref[...] for ref in shard_refs], QKV_ORDER)
    late_ref[...] = shard_refs[0][shard_refs[0].shape[0] - late_ref.shape[0] :, :]

    def every_shard(kind, carry):
        for position in range(len(near)):
            fetch(position, kind).wait()
        total = -fix
        for position, ref in enumerate(shard_refs):
            weights = decode(near_ref[position, kind], QKV_ORDER)
            total = total + jnp.dot(ref[...], weights, preferred_element_type=f32)
        sums_ref[kind] = total
        return carry

    lax.fori_loop(0, 3, every_shard, 0)
    for position in range(len(near), len(near + far)):
        for kind in range(3):
            fetch(position, kind).wait()


def prepare(near, far, shards, codes):
    rows, inner = shards[0].shape
    columns = codes.shape[2]
    words = inner // PLANES
    return call(
        functools.partial(prepare_kernel, near, far),
        (
            shape_of((3, rows, columns), f32),
            shape_of((len(far), 3, words, columns), jnp.int32),
            shape_of((rows - early_rows(rows), inner), bf16),
        ),
        [VMEM] * len(near) + [HBM],
        (*shards, in_hbm(codes)),
        "prepare",
        scratch_shapes=[
            pltpu.VMEM((len(near), 3, words, columns), jnp.int32),
            pltpu.SemaphoreType.DMA((len(near + far), 3)),
        ],
    )


def project_kernel(kinds, first_row, groups, positions, whole, ending, *rest):
    count = len(positions)
    shard_refs = rest[: groups * count]
    sums_ref, words_ref = rest[groups * count : groups * count + 2]
    if ending:
        scale_ref, sign_ref = rest[groups * count + 2 : groups * count + 4]
    out_ref = rest[-1]
    columns = sums_ref.shape[2]
    shards = []
    for place in range(count):
        parts = [shard_refs[g * count + place][...] for g in range(groups)]
        shards.append(parts[0] if groups == 1 else jnp.concatenate(parts, 0))
    fix = row_correction(shards, QKV_ORDER)
    row_count = shards[0].shape[0]
    rows = slice(first_row, first_row + row_count)
    doubled = double_hadamard()
    ones = jnp.ones((HD, HD), bf16)
    for place, kind in enumerate(kinds):
        part = (sums_ref[kind, rows, :] if whole else sums_ref[place]) - fix
        for shard, position in zip(shards, positions):
            weights = decode(words_ref[position, kind], QKV_ORDER)
            part = part + jnp.dot(shard, weights, preferred_element_type=f32)
        if not ending:
            out_ref[place] = part
            continue
        heads = []
        for first in range(0, columns, HD):
            at = slice(first, first + HD)
            scale_row = scale_ref[kind : kind + 1, at] * np.float32(D ** (-0.5))
            heads.append(part[:, at] * scale_row)
        mixed = rotate_halves(jnp.concatenate(heads, 0), doubled)
        signs = []
        for head in range(len(heads)):
            sign_row = sign_ref[kind : kind + 1, head * HD : (head + 1) * HD]
            sign_row = signed(sign_row) * np.float32(HAD ** (-0.5))
            signs.append(mixed[head * row_count : (head + 1) * row_count] * sign_row)
        if kind != 2:
            square = jnp.concatenate([(part * part).astype(bf16) for part in signs], 0)
            mean = jnp.dot(square, ones, preferred_element_type=f32) * (1.0 / HD)
            factor = lax.rsqrt(mean + epsilon)
            signs = [
                part * factor[head * row_count : (head + 1) * row_count]
                for head, part in enumerate(signs)
            ]
        for head, part in enumerate(signs):
            out_ref[place, :, head * HD : (head + 1) * HD] = part.astype(bf16)


def project(kinds, first_row, groups, positions, sums, words, ending, flops=1):
    inner = groups[0][0].shape[1]
    columns = sums.shape[2]
    row_count = sum(group[0].shape[0] for group in groups)
    whole = sums.shape[0] == 3
    args = [shard for group in groups for shard in group] + [sums, words]
    own_args = len(args) + 2
    if ending is not None:
        args += ending
    return call(
        functools.partial(
            project_kernel, kinds, first_row, len(groups), positions, whole, ending is not None
        ),
        shape_of((len(kinds), row_count, columns), f32 if ending is None else bf16),
        [VMEM] * min(len(args), own_args) + [ANY] * max(len(args) - own_args, 0),
        args,
        "project",
        flops=flops,
    )


def near_row(row, swap_pair):
    if swap_pair is None:
        return row
    by, odd = swap_pair
    return jnp.where(lax.rem(row // by, 2) == odd, row + by, row - by)


def masks_kernel(steps, windows_ref, after_ref, *mask_refs):
    row = lax.axis_index("height")
    for segments, mask_ref in zip(steps, mask_refs):
        lane = lax.broadcasted_iota(jnp.int32, (1, mask_ref.shape[1]), 1)
        ids, base = None, 0
        for swap_pair, first, rows in segments:
            tile = (lane + (first - base)) // TILE
            ids_here = near_row(row, swap_pair) * WTILES + tile
            ids = ids_here if ids is None else jnp.where(lane >= base, ids_here, ids)
            base += rows
        for tile in range(mask_ref.shape[0]):
            hit = jnp.zeros(lane.shape, f32)
            for entry in range(windows_ref.shape[2]):
                hit = jnp.where(ids == windows_ref[tile, 0, entry], 1.0, hit)
            mask_ref[tile : tile + 1, :] = hit


def make_masks(windows, after, steps):
    listed = jnp.transpose(windows, (1, 0, 2))
    shapes = [
        shape_of((listed.shape[0], sum(rows for _, _, rows in segments)), f32) for segments in steps
    ]
    return call(
        functools.partial(masks_kernel, steps), shapes, [SMEM, ANY], (listed, after), "window_masks"
    )


def attend_kernel(halves, blocks, has_sum, last, share_order, *rest):
    rest = list(rest)
    q_refs = [rest.pop(0) for _ in range(halves)]
    kv_refs = [rest.pop(0) for _ in range(blocks)]
    mask_ref = rest.pop(0)
    sum_ref = rest.pop(0) if has_sum else None
    if last:
        oin_ref, out_ref, rotated_ref = rest
    else:
        (out_ref,) = rest
    columns = q_refs[0].shape[2]
    row_count = sum(ref.shape[1] for ref in q_refs)
    heads = [slice(head, head + HD) for head in range(0, columns, HD)]
    mask = jnp.concatenate(
        [
            jnp.broadcast_to(mask_ref[t : t + 1, :], (TILE, mask_ref.shape[1]))
            for t in range(row_count // TILE)
        ],
        0,
    )
    scores = []
    for at in heads:
        keys = jnp.concatenate([ref[0, :, at] for ref in kv_refs], 0)
        scores.append(
            lax.dot_general(
                jnp.concatenate([ref[0, :, at] for ref in q_refs], 0),
                keys,
                (((1,), (1,)), ((), ())),
                preferred_element_type=f32,
            )
        )
    weights = [
        (jnp.exp(score * np.float32(HD ** (-0.5))) * mask).astype(bf16) for score in scores
    ]
    totals = []
    for head, at in enumerate(heads):
        values = jnp.concatenate([ref[1, :, at] for ref in kv_refs], 0)
        values = jnp.concatenate([values, jnp.ones_like(values)], 1)
        total = jnp.dot(weights[head], values, preferred_element_type=f32)
        if has_sum:
            total = total + sum_ref[head]
        totals.append(total)
    if not last:
        for head, total in enumerate(totals):
            out_ref[head] = total
        return
    matrix = hadamard(OUT_ORDER)
    factor = turn_factor(OUT_ORDER)
    for head, at in enumerate(heads):
        attended = (totals[head][:, :HD] / totals[head][:, HD:]).astype(bf16)
        sign_row = signed(oin_ref[head : head + 1, :])
        flipped = (attended.astype(f32) * sign_row).astype(bf16)
        rotated_ref[:, at] = jnp.dot(flipped, matrix, preferred_element_type=f32) * factor
    share = row_count // len(share_order)
    pieces = []
    for flip in share_order:
        owner = lax.axis_index("head") ^ flip
        pieces.append(rotated_ref[pl.ds(pl.multiple_of(owner * share, 8), share), :])
    out_ref[...] = jnp.concatenate(pieces, 0).astype(bf16)


def attend(queries, blocks, mask, running, ending):
    columns = queries[0].shape[2]
    row_count = sum(part.shape[1] for part in queries)
    args = [*queries, *blocks, mask]
    if running is not None:
        args.append(running)
    scratch, share_order = [], None
    if ending is None:
        out_shape = shape_of((columns // HD, row_count, 2 * HD), f32)
    else:
        oin_sign, share_order = ending
        args.append(oin_sign.reshape(-1, HAD))
        out_shape = shape_of((row_count, columns), bf16)
        scratch = [pltpu.VMEM((row_count, columns), f32)]
    return call(
        functools.partial(
            attend_kernel,
            len(queries),
            len(blocks),
            running is not None,
            ending is not None,
            share_order,
        ),
        out_shape,
        [VMEM] * len(args),
        args,
        "attend",
        scratch_shapes=scratch,
    )


def unpack_out_kernel(codes_ref, after_ref, weights_ref):
    for first in range(0, codes_ref.shape[0], WORDS):

        def some(step, carry):
            cols = pl.ds(pl.multiple_of(step * 512, 512), 512)
            at = first * PLANES
            for piece in pieces_of(codes_ref[first : first + WORDS, cols], OUT_ORDER):
                weights_ref[at : at + piece.shape[0], cols] = piece
                at += piece.shape[0]
            return carry

        lax.fori_loop(0, codes_ref.shape[1] // 512, some, 0)


def unpack_out(codes, after):
    words, columns = codes.shape
    return call(
        unpack_out_kernel,
        shape_of((words * PLANES, columns), bf16),
        [VMEM, ANY],
        (codes, after),
        "unpack_out",
    )


def out_kernel(first, rotated_ref, weights_ref, scale_ref, send_ref, keep_ref):
    rows = rotated_ref[...]
    fix = row_correction([rows], OUT_ORDER)
    half, columns = send_ref.shape
    width = 512
    for at in range(0, columns, width):
        cols = slice(first + at, first + at + width)
        part = jnp.dot(rows, weights_ref[:, cols], preferred_element_type=f32) - fix
        for lane in range(0, width, HAD):
            place = (first + at + lane) // HAD
            scale_row = scale_ref[place : place + 1, :] * np.float32((HEADS * HD) ** (-0.5))
            done = (part[:, lane : lane + HAD] * scale_row).astype(bf16)
            send_ref[:, at + lane : at + lane + HAD] = done[:half]
            keep_ref[:, at + lane : at + lane + HAD] = done[half:]


def out_project(rotated, weights, scale_rows, first, columns):
    row_count, inner = rotated.shape
    result = shape_of((row_count // 2, columns), bf16)
    return call(
        functools.partial(out_kernel, first),
        (result, result),
        [VMEM] * 3,
        (rotated, weights, scale_rows),
        "out_project",
    )


def finish_kernel(chunks, first, sign_ref, *rest):
    out_hbm, done_ref, sems = rest[-3:]
    doubled = double_hadamard()
    copies = []
    for chunk in range(chunks):
        keep_ref, more_ref = rest[2 * chunk : 2 * chunk + 2]
        share, columns = keep_ref.shape
        totals = keep_ref[...].astype(f32) + more_ref[...].astype(f32)
        blocks = [totals[:, at : at + HAD] for at in range(0, columns, HAD)]
        turned = rotate_halves(jnp.concatenate(blocks, 0), doubled)
        for block in range(len(blocks)):
            place = first // HAD + block
            sign_row = signed(sign_ref[place : place + 1, :]) * np.float32(HAD ** (-0.5))
            done = turned[block * share : (block + 1) * share] * sign_row
            done_ref[:, place * HAD : (place + 1) * HAD] = done.astype(bf16)
        cols = pl.ds(first, columns)
        copies.append(
            pltpu.make_async_copy(done_ref.at[:, cols], out_hbm.at[:, cols], sems.at[chunk])
        )
        copies[-1].start()
        first += columns
    for copy in copies:
        copy.wait()


def finish(pairs, sign_rows, first, base):
    share = pairs[0][0].shape[0]
    args = [sign_rows] + [array for pair in pairs for array in pair]
    in_specs = [VMEM] * len(args)
    aliases = {}
    if base is not None:
        aliases = {len(args): 0}
        args.append(base)
        in_specs.append(HBM)
    return call(
        functools.partial(finish_kernel, len(pairs), first),
        shape_of((share, D), bf16),
        in_specs,
        args,
        "finish",
        out_specs=HBM,
        scratch_shapes=[pltpu.VMEM((share, D), bf16), pltpu.SemaphoreType.DMA((len(pairs),))],
        input_output_aliases=aliases,
    )


def swap(shard, bit):
    peers = lax.axis_size("head")
    return lax.ppermute(shard, "head", [(i, i ^ bit) for i in range(peers)])


def row_swaps(row_tiles):
    swaps = []
    for by in (1, 3, 4, 5) if row_tiles > HROWS else (1,):
        for odd in (1, 0):
            low = [i for i in range(row_tiles - by) if (i // by) % 2 == odd]
            swaps.append((by, odd, [(i, i + by) for i in low] + [(i + by, i) for i in low]))
    return swaps


def halving_order(head_count):
    flips = [0]
    bit = head_count // 2
    while bit >= 1:
        flips = [f | bit for f in flips] + flips
        bit //= 2
    return tuple(flips)


CHUNKS = (2560, 2560)


def on_device(
    tokens,
    in_sign,
    qkv_codes,
    qkv_scale,
    qkv_sign,
    windows,
    oin_sign,
    out_codes,
    out_scale,
    out_sign,
):
    head_count = lax.axis_size("head")
    row_tiles = lax.axis_size("height")
    top = head_count // 2
    low_bits = [1 << b for b in range(top.bit_length() - 1)]

    own, early = turn(tokens[0], in_sign)
    half_rows = early.shape[0]
    early = swap(early, top)
    near = {0: own}
    for bit in low_bits:
        for flip in list(near):
            near[flip ^ bit] = swap(near[flip], bit)
    codes = jnp.transpose(qkv_codes, (1, 0, 2))
    near_flips = tuple(sorted(near))
    far_flips = tuple(flip ^ top for flip in near_flips)
    sums, words, late = prepare(
        near_flips, far_flips, [near[flip] for flip in near_flips], codes
    )
    late = swap(late, top)
    swaps = row_swaps(row_tiles)
    ending = [qkv_scale, qkv_sign]
    every = tuple(range(len(far_flips)))
    halves, key_values, moved, gates = [], [], [], []
    for half, first_row in ((early, 0), (late, half_rows)):
        shards = {top: tie(half, *gates, sums)}
        for bit in low_bits:
            for flip in list(shards):
                shards[flip ^ bit] = swap(shards[flip], bit)
        shards = [shards[flip] for flip in far_flips]
        partial = project(
            (1, 2), first_row, [shards[:-1]], every[:-1], sums, words, None, 4 * 10**9
        )
        key_value = project((1, 2), 0, [shards[-1:]], every[-1:], partial, words, ending)
        moved.append([lax.ppermute(key_value, "height", pairs) for _, _, pairs in swaps])
        halves.append(shards)
        key_values.append(key_value)
        gates.append(gate(key_value))
    queries = [project((0,), 0, halves, every, sums, words, ending, 4 * 10**9)]
    out_weights = unpack_out(out_codes, key_values[1])

    late_rows = own.shape[0] - half_rows
    own_keys = ((None, 0, half_rows), (None, half_rows, late_rows))
    early_keys = tuple(((by, odd), 0, half_rows) for by, odd, _ in swaps)
    late_keys = tuple(((by, odd), half_rows, late_rows) for by, odd, _ in swaps)
    steps = (own_keys, early_keys, late_keys[1:], late_keys[:1])
    masks = make_masks(windows, key_values[1], steps)
    running = attend(queries, key_values, masks[0], None, None)
    running = attend(queries, moved[0], masks[1], running, None)
    running = attend(queries, moved[1][1:], masks[2], running, None)
    rotated = attend(
        queries, moved[1][:1], masks[3], running, (oin_sign, halving_order(head_count))
    )

    bits = low_bits + [top]
    scale_rows = out_scale.reshape(-1, HAD)
    sign_rows = out_sign.reshape(-1, HAD)
    pairs, sums_sent = [], []
    first = 0
    for columns in CHUNKS:
        part, keep = out_project(rotated, out_weights, scale_rows, first, columns)
        if sums_sent:
            part = tie(part, sums_sent[-1])
        for bit in bits:
            more = swap(part, bit)
            if bit == top:
                break
            total = keep.astype(f32) + more.astype(f32)
            half = total.shape[0] // 2
            part, keep = total[:half].astype(bf16), total[half:]
            sums_sent.append(part)
        pairs.append((keep, more))
        first += columns
    base = finish(pairs[:-1], sign_rows, 0, None)
    return finish(pairs[-1:], sign_rows, D - CHUNKS[-1], base)[None]


def solution(mesh):
    return jax.shard_map(
        on_device,
        mesh=mesh,
        in_specs=(
            P(("clip", "height"), None, "head"),
            P(),
            P(None, None, "head"),
            P(None, "head"),
            P(None, "head"),
            P(("clip", "height"), None, None),
            P("head"),
            P("head", None),
            P(),
            P(),
        ),
        out_specs=P(("clip", "height"), "head", None),
        check_vma=False,
    )
```

```python
import functools

import jax
import jax.numpy as jnp
import numpy as np
from jax import lax
from jax.experimental import pallas as pl
from jax.experimental.pallas import tpu as pltpu
from jax.sharding import PartitionSpec as P

D = 5120
HD = 128
HEADS = 24
HAD = 128
TILE = 64
HROWS = 4
WTILES = 3
PLANES = 8
WORDS = HAD // PLANES
QKV_ORDER = "half"
OUT_ORDER = "byte"
TURN_PIECES = 5

epsilon = 1e-06
f32 = jnp.float32
bf16 = jnp.bfloat16
VMEM = pl.BlockSpec(memory_space=pltpu.VMEM)
SMEM = pl.BlockSpec(memory_space=pltpu.SMEM)
ANY = pl.BlockSpec(memory_space=pl.ANY)
HBM = pl.BlockSpec(memory_space=pltpu.HBM)


def shape_of(shape, dtype):
    return jax.ShapeDtypeStruct(tuple(shape), dtype)


def in_hbm(array):
    return pltpu.with_memory_space_constraint(array, pltpu.HBM)


def call(body, out_shape, in_specs, args, name, out_specs=None, megabytes=16, flops=1, **more):
    if out_specs is None:
        out_specs = jax.tree.map(lambda _: VMEM, out_shape)
    return pl.pallas_call(
        body,
        out_shape=out_shape,
        in_specs=in_specs,
        out_specs=out_specs,
        compiler_params=pltpu.CompilerParams(vmem_limit_bytes=megabytes * 2**20),
        cost_estimate=pl.CostEstimate(flops=flops, bytes_accessed=1, transcendentals=0),
        name=name,
        **more,
    )(*args)


def lanes():
    return lax.broadcasted_iota(jnp.int32, (HAD, HAD), 1)


def hadamard(order):
    row = lax.broadcasted_iota(jnp.int32, (HAD, HAD), 0)
    column = lanes()
    word = PLANES * (column & (WORDS - 1))
    if order == "half":
        column = word + column // WORDS
    if order == "byte":
        column = word + column // (2 * WORDS) + (PLANES // 2) * ((column // WORDS) & 1)
    shared = row & column
    shared = shared ^ (shared >> 4)
    shared = shared ^ (shared >> 2)
    shared = shared ^ (shared >> 1)
    return (1 - 2 * (shared & 1)).astype(f32).astype(bf16)


def double_hadamard():
    plain = hadamard("plain")
    return jnp.concatenate([plain, plain], 0)


def plane_power(base, order):
    lane = lax.broadcasted_iota(jnp.int32, (1, HAD), 1)
    if order == "half":
        power = jnp.minimum(lane // WORDS, PLANES - 2)
    else:
        power = jnp.minimum(lane // (2 * WORDS), PLANES // 2 - 2)
    value = jnp.where(power & 1 == 1, base, 1.0)
    value = value * jnp.where(power & 2 == 2, base**2, 1.0)
    return value * jnp.where(power & 4 == 4, base**4, 1.0)


def turn_factor(order):
    return plane_power(0.25, order) * np.float32(HAD ** (-0.5))


def signed(sign_bits):
    return (2 * sign_bits - 1).astype(f32)


def pieces_of(words, order):
    if order == "half":
        packed = words.astype(jnp.int16)
        masked = [packed & jnp.int16(3 << (2 * k)) for k in range(PLANES - 1)]
        masked.append((words >> 2).astype(jnp.int16) & jnp.int16(3 << (2 * PLANES - 4)))
    else:
        pair = jnp.concatenate([words & 255, words >> 8], 0)
        packed = pair.astype(jnp.int8)
        masked = [packed & jnp.int8(3 << (2 * k)) for k in range(PLANES // 2 - 1)]
        masked.append((pair >> 2).astype(jnp.int8) & jnp.int8(3 << (PLANES - 4)))
    return [piece.astype(bf16) for piece in masked]


def decode(words, order):
    blocks = []
    for first in range(0, words.shape[0], WORDS):
        blocks += pieces_of(words[first : first + WORDS], order)
    return jnp.concatenate(blocks, 0)


def row_correction(row_list, order):
    factor_row = plane_power(4.0, order) * 1.5
    total = None
    for rows in row_list:
        for first in range(0, rows.shape[1], HAD):
            term = rows[:, first : first + HAD].astype(f32)
            total = term if total is None else total + term
    return jnp.sum(total * factor_row, axis=1, keepdims=True)


def rotate_halves(values, doubled):
    high = values.astype(bf16)
    low = (values - high.astype(f32)).astype(bf16)
    return jnp.dot(jnp.concatenate([high, low], 1), doubled, preferred_element_type=f32)


def early_rows(rows):
    return rows * 7 // 12 // WORDS * WORDS


def turn_kernel(x_hbm, sign_hbm, own_ref, send_ref, x_ref, sign_ref, sems):
    blocks = x_ref.shape[1] // HAD
    per_piece = blocks // TURN_PIECES
    signs = pltpu.make_async_copy(sign_hbm, sign_ref, sems.at[TURN_PIECES])
    copies = []
    for piece in range(TURN_PIECES):
        where = pl.ds(piece * per_piece * HAD, per_piece * HAD)
        copies.append(
            pltpu.make_async_copy(x_hbm.at[:, where], x_ref.at[:, where], sems.at[piece])
        )
    for copy in [signs] + copies:
        copy.start()
    matrix = hadamard(QKV_ORDER)
    factor = turn_factor(QKV_ORDER)
    signs.wait()
    first = lax.axis_index("head") * blocks
    for b in range(blocks):
        if b % per_piece == 0:
            copies[b // per_piece].wait()
        cols = slice(b * HAD, (b + 1) * HAD)
        sign_row = signed(sign_ref[pl.ds(first + b, 1), :])
        flipped = (x_ref[:, cols].astype(f32) * sign_row).astype(bf16)
        turned = jnp.dot(flipped, matrix, preferred_element_type=f32)
        turned = (turned * factor).astype(bf16)
        own_ref[:, cols] = turned
        send_ref[:, cols] = turned[: send_ref.shape[0]]


def turn(own_tokens, in_sign):
    sign_rows = in_sign.reshape(-1, HAD)
    rows, inner = own_tokens.shape
    return call(
        turn_kernel,
        (shape_of((rows, inner), bf16), shape_of((early_rows(rows), inner), bf16)),
        [HBM, HBM],
        (in_hbm(own_tokens), in_hbm(sign_rows)),
        "turn",
        scratch_shapes=[
            pltpu.VMEM(own_tokens.shape, bf16),
            pltpu.VMEM(sign_rows.shape, jnp.int32),
            pltpu.SemaphoreType.DMA((TURN_PIECES + 1,)),
        ],
    )


def tie(array, *after):
    return call(
        lambda *refs: None,
        shape_of(array.shape, array.dtype),
        [ANY] * (1 + len(after)),
        (array, *after),
        "tie",
        out_specs=ANY,
        input_output_aliases={0: 0},
    )


def gate(array):
    def body(array_ref, out_ref):
        out_ref[...] = jnp.zeros_like(out_ref)

    return call(body, shape_of((8, HAD), f32), [ANY], (array,), "gate", flops=4 * 10**9)


def prepare_kernel(near, far, *rest):
    shard_refs = rest[: len(near)]
    codes_hbm, sums_ref, far_ref, late_ref, near_ref, sems = rest[len(near) :]
    words, columns = near_ref.shape[2:]

    def fetch(position, kind):
        flip = (near + far)[position]
        first = pl.multiple_of((lax.axis_index("head") ^ flip) * words, WORDS)
        there = position - len(near)
        target = near_ref.at[position, kind] if there < 0 else far_ref.at[there, kind]
        return pltpu.make_async_copy(
            codes_hbm.at[kind, pl.ds(first, words), :], target, sems.at[position, kind]
        )

    for kind in range(3):
        for position in range(len(near)):
            fetch(position, kind).start()
    for position in range(len(near), len(near + far)):
        for kind in range(3):
            fetch(position, kind).start()
    fix = row_correction([ref[...] for ref in shard_refs], QKV_ORDER)
    late_ref[...] = shard_refs[0][shard_refs[0].shape[0] - late_ref.shape[0] :, :]

    def every_shard(kind, carry):
        for position in range(len(near)):
            fetch(position, kind).wait()
        total = -fix
        for position, ref in enumerate(shard_refs):
            weights = decode(near_ref[position, kind], QKV_ORDER)
            total = total + jnp.dot(ref[...], weights, preferred_element_type=f32)
        sums_ref[kind] = total
        return carry

    lax.fori_loop(0, 3, every_shard, 0)
    for position in range(len(near), len(near + far)):
        for kind in range(3):
            fetch(position, kind).wait()


def prepare(near, far, shards, codes):
    rows, inner = shards[0].shape
    columns = codes.shape[2]
    words = inner // PLANES
    return call(
        functools.partial(prepare_kernel, near, far),
        (
            shape_of((3, rows, columns), f32),
            shape_of((len(far), 3, words, columns), jnp.int32),
            shape_of((rows - early_rows(rows), inner), bf16),
        ),
        [VMEM] * len(near) + [HBM],
        (*shards, in_hbm(codes)),
        "prepare",
        scratch_shapes=[
            pltpu.VMEM((len(near), 3, words, columns), jnp.int32),
            pltpu.SemaphoreType.DMA((len(near + far), 3)),
        ],
    )


def project_kernel(kinds, first_row, groups, positions, whole, ending, *rest):
    count = len(positions)
    shard_refs = rest[: groups * count]
    sums_ref, words_ref = rest[groups * count : groups * count + 2]
    if ending:
        scale_ref, sign_ref = rest[groups * count + 2 : groups * count + 4]
    out_ref = rest[-1]
    columns = sums_ref.shape[2]
    shards = []
    for place in range(count):
        parts = [shard_refs[g * count + place][...] for g in range(groups)]
        shards.append(parts[0] if groups == 1 else jnp.concatenate(parts, 0))
    fix = row_correction(shards, QKV_ORDER)
    row_count = shards[0].shape[0]
    rows = slice(first_row, first_row + row_count)
    doubled = double_hadamard()
    ones = jnp.ones((HD, HD), bf16)
    for place, kind in enumerate(kinds):
        part = (sums_ref[kind, rows, :] if whole else sums_ref[place]) - fix
        for shard, position in zip(shards, positions):
            weights = decode(words_ref[position, kind], QKV_ORDER)
            part = part + jnp.dot(shard, weights, preferred_element_type=f32)
        if not ending:
            out_ref[place] = part
            continue
        heads = []
        for first in range(0, columns, HD):
            at = slice(first, first + HD)
            scale_row = scale_ref[kind : kind + 1, at] * np.float32(D ** (-0.5))
            heads.append(part[:, at] * scale_row)
        mixed = rotate_halves(jnp.concatenate(heads, 0), doubled)
        signs = []
        for head in range(len(heads)):
            sign_row = sign_ref[kind : kind + 1, head * HD : (head + 1) * HD]
            sign_row = signed(sign_row) * np.float32(HAD ** (-0.5))
            signs.append(mixed[head * row_count : (head + 1) * row_count] * sign_row)
        if kind != 2:
            square = jnp.concatenate([(part * part).astype(bf16) for part in signs], 0)
            mean = jnp.dot(square, ones, preferred_element_type=f32) * (1.0 / HD)
            factor = lax.rsqrt(mean + epsilon)
            signs = [
                part * factor[head * row_count : (head + 1) * row_count]
                for head, part in enumerate(signs)
            ]
        for head, part in enumerate(signs):
            out_ref[place, :, head * HD : (head + 1) * HD] = part.astype(bf16)


def project(kinds, first_row, groups, positions, sums, words, ending, flops=1):
    inner = groups[0][0].shape[1]
    columns = sums.shape[2]
    row_count = sum(group[0].shape[0] for group in groups)
    whole = sums.shape[0] == 3
    args = [shard for group in groups for shard in group] + [sums, words]
    own_args = len(args) + 2
    if ending is not None:
        args += ending
    return call(
        functools.partial(
            project_kernel, kinds, first_row, len(groups), positions, whole, ending is not None
        ),
        shape_of((len(kinds), row_count, columns), f32 if ending is None else bf16),
        [VMEM] * min(len(args), own_args) + [ANY] * max(len(args) - own_args, 0),
        args,
        "project",
        flops=flops,
    )


def near_row(row, swap_pair):
    if swap_pair is None:
        return row
    by, odd = swap_pair
    return jnp.where(lax.rem(row // by, 2) == odd, row + by, row - by)


def masks_kernel(steps, windows_ref, after_ref, *mask_refs):
    row = lax.axis_index("height")
    for segments, mask_ref in zip(steps, mask_refs):
        lane = lax.broadcasted_iota(jnp.int32, (1, mask_ref.shape[1]), 1)
        ids, base = None, 0
        for swap_pair, first, rows in segments:
            tile = (lane + (first - base)) // TILE
            ids_here = near_row(row, swap_pair) * WTILES + tile
            ids = ids_here if ids is None else jnp.where(lane >= base, ids_here, ids)
            base += rows
        for tile in range(mask_ref.shape[0]):
            hit = jnp.zeros(lane.shape, f32)
            for entry in range(windows_ref.shape[2]):
                hit = jnp.where(ids == windows_ref[tile, 0, entry], 1.0, hit)
            mask_ref[tile : tile + 1, :] = hit


def make_masks(windows, after, steps):
    listed = jnp.transpose(windows, (1, 0, 2))
    shapes = [
        shape_of((listed.shape[0], sum(rows for _, _, rows in segments)), f32) for segments in steps
    ]
    return call(
        functools.partial(masks_kernel, steps), shapes, [SMEM, ANY], (listed, after), "window_masks"
    )


def attend_kernel(halves, blocks, has_sum, last, share_order, *rest):
    rest = list(rest)
    q_refs = [rest.pop(0) for _ in range(halves)]
    kv_refs = [rest.pop(0) for _ in range(blocks)]
    mask_ref = rest.pop(0)
    sum_ref = rest.pop(0) if has_sum else None
    if last:
        oin_ref, out_ref, rotated_ref = rest
    else:
        (out_ref,) = rest
    columns = q_refs[0].shape[2]
    row_count = sum(ref.shape[1] for ref in q_refs)
    heads = [slice(head, head + HD) for head in range(0, columns, HD)]
    mask = jnp.concatenate(
        [
            jnp.broadcast_to(mask_ref[t : t + 1, :], (TILE, mask_ref.shape[1]))
            for t in range(row_count // TILE)
        ],
        0,
    )
    scores = []
    for at in heads:
        keys = jnp.concatenate([ref[0, :, at] for ref in kv_refs], 0)
        scores.append(
            lax.dot_general(
                jnp.concatenate([ref[0, :, at] for ref in q_refs], 0),
                keys,
                (((1,), (1,)), ((), ())),
                preferred_element_type=f32,
            )
        )
    weights = [
        (jnp.exp(score * np.float32(HD ** (-0.5))) * mask).astype(bf16) for score in scores
    ]
    totals = []
    for head, at in enumerate(heads):
        values = jnp.concatenate([ref[1, :, at] for ref in kv_refs], 0)
        values = jnp.concatenate([values, jnp.ones_like(values)], 1)
        total = jnp.dot(weights[head], values, preferred_element_type=f32)
        if has_sum:
            total = total + sum_ref[head]
        totals.append(total)
    if not last:
        for head, total in enumerate(totals):
            out_ref[head] = total
        return
    matrix = hadamard(OUT_ORDER)
    factor = turn_factor(OUT_ORDER)
    for head, at in enumerate(heads):
        attended = (totals[head][:, :HD] / totals[head][:, HD:]).astype(bf16)
        sign_row = signed(oin_ref[head : head + 1, :])
        flipped = (attended.astype(f32) * sign_row).astype(bf16)
        rotated_ref[:, at] = jnp.dot(flipped, matrix, preferred_element_type=f32) * factor
    share = row_count // len(share_order)
    pieces = []
    for flip in share_order:
        owner = lax.axis_index("head") ^ flip
        pieces.append(rotated_ref[pl.ds(pl.multiple_of(owner * share, 8), share), :])
    out_ref[...] = jnp.concatenate(pieces, 0).astype(bf16)


def attend(queries, blocks, mask, running, ending):
    columns = queries[0].shape[2]
    row_count = sum(part.shape[1] for part in queries)
    args = [*queries, *blocks, mask]
    if running is not None:
        args.append(running)
    scratch, share_order = [], None
    if ending is None:
        out_shape = shape_of((columns // HD, row_count, 2 * HD), f32)
    else:
        oin_sign, share_order = ending
        args.append(oin_sign.reshape(-1, HAD))
        out_shape = shape_of((row_count, columns), bf16)
        scratch = [pltpu.VMEM((row_count, columns), f32)]
    return call(
        functools.partial(
            attend_kernel,
            len(queries),
            len(blocks),
            running is not None,
            ending is not None,
            share_order,
        ),
        out_shape,
        [VMEM] * len(args),
        args,
        "attend",
        scratch_shapes=scratch,
    )


def unpack_out_kernel(codes_ref, after_ref, weights_ref):
    for first in range(0, codes_ref.shape[0], WORDS):

        def some(step, carry):
            cols = pl.ds(pl.multiple_of(step * 512, 512), 512)
            at = first * PLANES
            for piece in pieces_of(codes_ref[first : first + WORDS, cols], OUT_ORDER):
                weights_ref[at : at + piece.shape[0], cols] = piece
                at += piece.shape[0]
            return carry

        lax.fori_loop(0, codes_ref.shape[1] // 512, some, 0)


def unpack_out(codes, after):
    words, columns = codes.shape
    return call(
        unpack_out_kernel,
        shape_of((words * PLANES, columns), bf16),
        [VMEM, ANY],
        (codes, after),
        "unpack_out",
    )


def out_kernel(first, rotated_ref, weights_ref, scale_ref, send_ref, keep_ref):
    rows = rotated_ref[...]
    fix = row_correction([rows], OUT_ORDER)
    half, columns = send_ref.shape
    width = 512
    for at in range(0, columns, width):
        cols = slice(first + at, first + at + width)
        part = jnp.dot(rows, weights_ref[:, cols], preferred_element_type=f32) - fix
        for lane in range(0, width, HAD):
            place = (first + at + lane) // HAD
            scale_row = scale_ref[place : place + 1, :] * np.float32((HEADS * HD) ** (-0.5))
            done = (part[:, lane : lane + HAD] * scale_row).astype(bf16)
            send_ref[:, at + lane : at + lane + HAD] = done[:half]
            keep_ref[:, at + lane : at + lane + HAD] = done[half:]


def out_project(rotated, weights, scale_rows, first, columns):
    row_count, inner = rotated.shape
    result = shape_of((row_count // 2, columns), bf16)
    return call(
        functools.partial(out_kernel, first),
        (result, result),
        [VMEM] * 3,
        (rotated, weights, scale_rows),
        "out_project",
    )


def finish_kernel(chunks, first, sign_ref, *rest):
    out_hbm, done_ref, sems = rest[-3:]
    doubled = double_hadamard()
    copies = []
    for chunk in range(chunks):
        keep_ref, more_ref = rest[2 * chunk : 2 * chunk + 2]
        share, columns = keep_ref.shape
        totals = keep_ref[...].astype(f32) + more_ref[...].astype(f32)
        blocks = [totals[:, at : at + HAD] for at in range(0, columns, HAD)]
        turned = rotate_halves(jnp.concatenate(blocks, 0), doubled)
        for block in range(len(blocks)):
            place = first // HAD + block
            sign_row = signed(sign_ref[place : place + 1, :]) * np.float32(HAD ** (-0.5))
            done = turned[block * share : (block + 1) * share] * sign_row
            done_ref[:, place * HAD : (place + 1) * HAD] = done.astype(bf16)
        cols = pl.ds(first, columns)
        copies.append(
            pltpu.make_async_copy(done_ref.at[:, cols], out_hbm.at[:, cols], sems.at[chunk])
        )
        copies[-1].start()
        first += columns
    for copy in copies:
        copy.wait()


def finish(pairs, sign_rows, first, base):
    share = pairs[0][0].shape[0]
    args = [sign_rows] + [array for pair in pairs for array in pair]
    in_specs = [VMEM] * len(args)
    aliases = {}
    if base is not None:
        aliases = {len(args): 0}
        args.append(base)
        in_specs.append(HBM)
    return call(
        functools.partial(finish_kernel, len(pairs), first),
        shape_of((share, D), bf16),
        in_specs,
        args,
        "finish",
        out_specs=HBM,
        scratch_shapes=[pltpu.VMEM((share, D), bf16), pltpu.SemaphoreType.DMA((len(pairs),))],
        input_output_aliases=aliases,
    )


def swap(shard, bit):
    peers = lax.axis_size("head")
    return lax.ppermute(shard, "head", [(i, i ^ bit) for i in range(peers)])


def row_swaps(row_tiles):
    swaps = []
    for by in (1, 3, 4, 5) if row_tiles > HROWS else (1,):
        for odd in (1, 0):
            low = [i for i in range(row_tiles - by) if (i // by) % 2 == odd]
            swaps.append((by, odd, [(i, i + by) for i in low] + [(i + by, i) for i in low]))
    return swaps


def halving_order(head_count):
    flips = [0]
    bit = head_count // 2
    while bit >= 1:
        flips = [f | bit for f in flips] + flips
        bit //= 2
    return tuple(flips)


CHUNKS = (2560, 2560)


def on_device(
    tokens,
    in_sign,
    qkv_codes,
    qkv_scale,
    qkv_sign,
    windows,
    oin_sign,
    out_codes,
    out_scale,
    out_sign,
):
    head_count = lax.axis_size("head")
    row_tiles = lax.axis_size("height")
    top = head_count // 2
    low_bits = [1 << b for b in range(top.bit_length() - 1)]

    own, early = turn(tokens[0], in_sign)
    half_rows = early.shape[0]
    early = swap(early, top)
    near = {0: own}
    for bit in low_bits:
        for flip in list(near):
            near[flip ^ bit] = swap(near[flip], bit)
    codes = jnp.transpose(qkv_codes, (1, 0, 2))
    near_flips = tuple(sorted(near))
    far_flips = tuple(flip ^ top for flip in near_flips)
    sums, words, late = prepare(
        near_flips, far_flips, [near[flip] for flip in near_flips], codes
    )
    late = swap(late, top)
    swaps = row_swaps(row_tiles)
    ending = [qkv_scale, qkv_sign]
    every = tuple(range(len(far_flips)))
    halves, key_values, moved, gates = [], [], [], []
    for half, first_row in ((early, 0), (late, half_rows)):
        shards = {top: tie(half, *gates, sums)}
        for bit in low_bits:
            for flip in list(shards):
                shards[flip ^ bit] = swap(shards[flip], bit)
        shards = [shards[flip] for flip in far_flips]
        partial = project(
            (1, 2), first_row, [shards[:-1]], every[:-1], sums, words, None, 4 * 10**9
        )
        key_value = project((1, 2), 0, [shards[-1:]], every[-1:], partial, words, ending)
        moved.append([lax.ppermute(key_value, "height", pairs) for _, _, pairs in swaps])
        halves.append(shards)
        key_values.append(key_value)
        gates.append(gate(key_value))
    queries = [project((0,), 0, halves, every, sums, words, ending, 4 * 10**9)]
    out_weights = unpack_out(out_codes, key_values[1])

    late_rows = own.shape[0] - half_rows
    own_keys = ((None, 0, half_rows), (None, half_rows, late_rows))
    early_keys = tuple(((by, odd), 0, half_rows) for by, odd, _ in swaps)
    late_keys = tuple(((by, odd), half_rows, late_rows) for by, odd, _ in swaps)
    steps = (own_keys, early_keys, late_keys[1:], late_keys[:1])
    masks = make_masks(windows, key_values[1], steps)
    running = attend(queries, key_values, masks[0], None, None)
    running = attend(queries, moved[0], masks[1], running, None)
    running = attend(queries, moved[1][1:], masks[2], running, None)
    rotated = attend(
        queries, moved[1][:1], masks[3], running, (oin_sign, halving_order(head_count))
    )

    bits = low_bits + [top]
    scale_rows = out_scale.reshape(-1, HAD)
    sign_rows = out_sign.reshape(-1, HAD)
    pairs, sums_sent = [], []
    first = 0
    for columns in CHUNKS:
        part, keep = out_project(rotated, out_weights, scale_rows, first, columns)
        if sums_sent:
            part = tie(part, sums_sent[-1])
        for bit in bits:
            more = swap(part, bit)
            if bit == top:
                break
            total = keep.astype(f32) + more.astype(f32)
            half = total.shape[0] // 2
            part, keep = total[:half].astype(bf16), total[half:]
            sums_sent.append(part)
        pairs.append((keep, more))
        first += columns
    base = finish(pairs[:-1], sign_rows, 0, None)
    return finish(pairs[-1:], sign_rows, D - CHUNKS[-1], base)[None]


def solution(mesh):
    return jax.shard_map(
        on_device,
        mesh=mesh,
        in_specs=(
            P(("clip", "height"), None, "head"),
            P(),
            P(None, None, "head"),
            P(None, "head"),
            P(None, "head"),
            P(("clip", "height"), None, None),
            P("head"),
            P("head", None),
            P(),
            P(),
        ),
        out_specs=P(("clip", "height"), "head", None),
        check_vma=False,
    )
```
